32 devices in a mesh: seq: 2 (over y), ctx: 4 (over x, core), fsdp: 4 (over z).
Axes of the slice: x: 2, y: 2, z: 4, core: 2. Of those that a mesh axis runs over, the one named last changes fastest.
Arguments:
- inputs: bfloat16 [16, 1024, 768], P(('seq', 'fsdp'), 'ctx'), may hold values from -6 to 6
- positions: int32 [16, 1024], P(('seq', 'fsdp')), may hold values from 0 to 1534, as said below
- w_query: bfloat16 [768, 768], P('fsdp'), may hold values from -0.109375 to 0.109375
- w_key: bfloat16 [768, 768], P('fsdp'), may hold values from -0.109375 to 0.109375
- w_value: bfloat16 [768, 768], P('fsdp'), may hold values from -0.21875 to 0.21875
- w_output: bfloat16 [768, 768], P(None, 'fsdp'), may hold values from -1.75 to 1.75
- gain_attn: bfloat16 [768], P('fsdp'), may hold values from 0.099609375 to 1.8984375
- rel_table: bfloat16 [32, 12], P('fsdp'), may hold values from -4 to 4
- w_in: bfloat16 [768, 3072], P('fsdp'), may hold values from -0.21875 to 0.21875
- w_out: bfloat16 [3072, 768], P(None, 'fsdp'), may hold values from -0.109375 to 0.109375
- gain_ffn: bfloat16 [768], P('fsdp'), may hold values from 0.099609375 to 1.8984375
- cotangent: bfloat16 [16, 1024, 768], P(('seq', 'fsdp'), 'ctx'), may hold values from -6 to 6
Outputs:
- output: bfloat16 [16, 1024, 768], P(('seq', 'fsdp'), 'ctx')
- input_grad: float32 [16, 1024, 768], P(('seq', 'fsdp'), 'ctx')
- grad_w_query: float32 [768, 768], P('fsdp')
- grad_w_key: float32 [768, 768], P('fsdp')
- grad_w_value: float32 [768, 768], P('fsdp')
- grad_w_output: float32 [768, 768], P(None, 'fsdp')
- grad_gain_attn: float32 [768], P('fsdp')
- grad_rel_table: float32 [32, 12], P('fsdp')
- grad_w_in: float32 [768, 3072], P('fsdp')
- grad_w_out: float32 [3072, 768], P(None, 'fsdp')
- grad_gain_ffn: float32 [768], P('fsdp')
The draws below stay inside these ranges and needn't reach their ends.
Inputs may be any that keep to these rules, and one draw needn't show every extreme that they name: In each sequence the first position is 0, positions rise by 1 or 2 from one token to the next, and the last position of every sequence is exactly 1534.
All inputs are finite; a program needn't handle non-finite values.
Results may differ from the reference program's by a relative error of at most 0.023.
Values may be sent and summed in bfloat16 or wider, within the bound.
A program may use at most 192 MiB of HBM per device.

```python
import jax
import jax.numpy as jnp
from jax import lax

D = 768
HEADS = 12
HEAD_DIM = 64
FF = 3072
BUCKETS = 32
BLK = 256
INNER = 768
L = 1024
SEQS = 16
N_CTX = 4


def draw_positions(key, part):
    count = L - 1
    seq_keys = jax.random.split(jax.random.fold_in(key, 7), SEQS)

    def one_sequence(seq_key):
        order = jax.random.permutation(seq_key, count)
        steps_drawn = 1 + (order < count // 2).astype(jnp.int32)
        return jnp.concatenate([jnp.zeros((1,), jnp.int32), jnp.cumsum(steps_drawn).astype(jnp.int32)])
    return jax.vmap(one_sequence)(seq_keys).astype(jnp.int32)


def block_levels(own_key, shape, pieces, least, top_value):
    level = 1.0
    for position, shards_of in pieces:
        steps = jax.random.uniform(jax.random.fold_in(jax.random.fold_in(own_key, 6), position), (shards_of,), jnp.float32, least / len(pieces), top_value / len(pieces))
        level = level * jnp.repeat(jnp.exp(steps), shape[position] // shards_of).reshape((-1,) + (1,) * (len(shape) - 1 - position))
    return level


def normal_values(own_key, extent, deviation, limit, cuts=(), kind=jnp.bfloat16):
    values = deviation * jax.random.normal(own_key, extent, jnp.float32)
    if cuts:
        values = values * block_levels(own_key, extent, cuts, -0.22, 0.18)
    return jnp.clip(values, -limit, limit).astype(kind)


def setup_inputs(seed: int = 0) -> dict:
    key_of = jax.random.split(jax.random.key(seed), 13)
    return {
        "inputs": normal_values(key_of[0], (SEQS, L, D), 1.0, 6.0, ((0, 8), (1, 4))),
        "positions": draw_positions(jax.random.fold_in(key_of[12], 71), 0),
        "w_query": normal_values(key_of[2], (D, INNER), (4 * D) ** -0.5, 0.109375, ((0, 4),)),
        "w_key": normal_values(key_of[3], (D, INNER), (4 * D) ** -0.5, 0.109375, ((0, 4),)),
        "w_value": normal_values(key_of[4], (D, INNER), D ** -0.5, 0.21875, ((0, 4),)),
        "w_output": normal_values(key_of[5], (INNER, D), (max(INNER // 64, 2)) ** -0.5, 1.75, ((1, 4),)),
        "gain_attn": jnp.clip(1.0 + 0.18 * jax.random.normal(key_of[6], (D,), jnp.float32), 0.099609375, 1.8984375).astype(jnp.bfloat16),
        "rel_table": normal_values(key_of[7], (BUCKETS, HEADS), 1.0, 4.0, ((0, 4),)),
        "w_in": normal_values(key_of[8], (D, FF), D ** -0.5, 0.21875, ((0, 4),)),
        "w_out": normal_values(key_of[9], (FF, D), FF ** -0.5, 0.109375, ((1, 4),)),
        "gain_ffn": jnp.clip(1.0 + 0.18 * jax.random.normal(key_of[10], (D,), jnp.float32), 0.099609375, 1.8984375).astype(jnp.bfloat16),
        "cotangent": normal_values(key_of[11], (SEQS, L, D), 1.0, 6.0, ((0, 8), (1, 4))),
    }


EPS = 1e-06
BORDERS = (12, 16, 23, 32, 46, 64, 91)
HIGHEST_ACCURACY = lax.Precision.HIGHEST

@jax.custom_vjp
def low(v):
    return lax.optimization_barrier(v.astype(jnp.bfloat16)).astype(jnp.float32)

@jax.custom_vjp
def low_back(v):
    return v

def low_keep(v):
    return (low(v), None)

def low_pass(kept, grad):
    return (grad,)

def back_keep(v):
    return (v, None)

def back_low(kept, grad):
    return (low(grad),)
low.defvjp(low_keep, low_pass)
low_back.defvjp(back_keep, back_low)

def bucket_of(offset):
    magnitude = jnp.abs(offset)
    logbins = 8 + sum(((magnitude >= border).astype(jnp.int32) for border in BORDERS))
    closed = jnp.where(magnitude < 8, magnitude, logbins)
    return (closed + jnp.where(offset > 0, 16, 0)).astype(jnp.int32)

def rms_norm(values, gain):
    return values * lax.rsqrt(lax.optimization_barrier(jnp.mean(values * values, axis=-1, keepdims=True)) + EPS) * gain

def matmul(left_operand, right_operand):
    return jnp.einsum('ktc,cu->ktu', left_operand, right_operand, precision=HIGHEST_ACCURACY)

def attend_sequence(query, key_all, value_all, places, table):
    key_heads = key_all.reshape(L, HEADS, HEAD_DIM)
    value_heads = value_all.reshape(L, HEADS, HEAD_DIM)

    def one_block(block_args):
        query_rows, query_positions = block_args
        query_heads = query_rows.reshape(BLK, HEADS, HEAD_DIM)
        scores = jnp.einsum('qhd,khd->hqk', query_heads, key_heads, precision=HIGHEST_ACCURACY)
        buckets = bucket_of(places[None, :] - query_positions[:, None])
        scores = scores + jnp.transpose(table[buckets], (2, 0, 1))
        scores = low_back(scores)
        weights = low(jax.nn.softmax(scores, axis=-1))
        mixed = jnp.einsum('hqk,khd->qhd', weights, value_heads, precision=HIGHEST_ACCURACY)
        return mixed.reshape(BLK, INNER)
    blocks = lax.map(jax.checkpoint(one_block), (query.reshape(N_CTX, BLK, INNER), places.reshape(N_CTX, BLK)))
    return blocks.reshape(L, INNER)

def reference(inputs, positions, w_query, w_key, w_value, w_output, gain_attn, rel_table, w_in, w_out, gain_ffn, cotangent):

    def layer(inputs_f, query_w, key_w, value_w, output_w, gain_one, table, in_w, out_w, gain_two):
        normed = low(rms_norm(inputs_f, gain_one))
        query = low_back(low(matmul(normed, query_w)))
        key_all = low_back(low(matmul(normed, key_w)))
        value_all = low_back(low(matmul(normed, value_w)))

        def per_sequence(seq_args):
            return attend_sequence(seq_args[0], seq_args[1], seq_args[2], seq_args[3], table)
        mixed = lax.map(per_sequence, (query, key_all, value_all, positions))
        mixed = low_back(low(mixed))
        middle = inputs_f + low_back(matmul(mixed, output_w))
        normed_two = low(rms_norm(middle, gain_two))
        hidden = low_back(matmul(normed_two, in_w))
        active = low(jax.nn.gelu(hidden))
        return middle + low_back(matmul(active, out_w))
    floats = [item.astype(jnp.float32) for item in (inputs, w_query, w_key, w_value, w_output, gain_attn, rel_table, w_in, w_out, gain_ffn)]
    result, pullback = jax.vjp(layer, *floats)
    grads = pullback(cotangent.astype(jnp.float32))
    return (result.astype(jnp.bfloat16), grads[0], grads[1], grads[2], grads[3], grads[4], grads[5], grads[6], grads[7], grads[8], grads[9])
```

```python
import functools
import math

import jax
import jax.numpy as jnp
from jax import lax
from jax.experimental import pallas as pl
from jax.experimental.pallas import tpu as pltpu
from jax.sharding import PartitionSpec as P

MESH = pl.DeviceIdType.MESH
F32 = jnp.float32
BF = jnp.bfloat16
EPS = 1e-06
BORDERS = (12, 16, 23, 32, 46, 64, 91)
LOG2E = math.log2(math.e)
T = 128


def dot_nn(a, b):
    return jnp.dot(a, b, preferred_element_type=F32)


def dot_nt(a, b):
    return lax.dot_general(a, b, (((1,), (1,)), ((), ())), preferred_element_type=F32)


def dot_tn(a, b):
    return lax.dot_general(a, b, (((0,), (0,)), ((), ())), preferred_element_type=F32)


def bucket_of(offset):
    magnitude = jnp.abs(offset)
    logbins = jnp.full_like(magnitude, 8)
    for border in BORDERS:
        logbins = logbins + jnp.where(magnitude >= border, 1, 0)
    return jnp.where(magnitude < 8, magnitude, logbins) + jnp.where(offset > 0, 16, 0)


class Place:
    def __init__(self, z_count):
        self.y = lax.axis_index("seq")
        self.ctx = lax.axis_index("ctx")
        self.z = lax.axis_index("fsdp")
        self.x = self.ctx // 2
        self.core = self.ctx % 2
        self.col = self.y * 2 + self.x
        self.z_count = z_count
        self.sib = (self.y, self.x * 2 + 1 - self.core, self.z)
        self.xn = (self.y, (1 - self.x) * 2 + self.core, self.z)
        self.yn = (1 - self.y, self.ctx, self.z)

    def zn(self, d):
        return (self.y, self.ctx, lax.rem(self.z + d, self.z_count))


def remote(src, dst, send, recv, device):
    return pltpu.make_async_remote_copy(
        src_ref=src, dst_ref=dst, send_sem=send, recv_sem=recv, device_id=device, device_id_type=MESH
    )


class Gather:
    def __init__(self, w, ssem, rsem, slot, lo, mid, hi, here, shard, piece):
        self.w, self.ssem, self.rsem, self.slot = w, ssem, rsem, slot
        self.lo, self.mid, self.hi = lo, mid, hi
        self.here, self.shard, self.piece = here, shard, piece

    def view(self, z, col, lo, hi):
        first = pl.multiple_of(z * self.shard + col * self.piece, 16)
        return self.w.at[pl.ds(first, self.piece), pl.ds(lo, hi - lo)]

    def copy(self, kind, d, arriving):
        p = self.here
        zs = lax.rem(p.z + p.z_count - d, p.z_count)
        col_x, col_y, col_d = p.y * 2 + 1 - p.x, (1 - p.y) * 2 + p.x, (1 - p.y) * 2 + 1 - p.x
        index = kind * 3 + d - 1
        send, recv = self.ssem.at[self.slot, index], self.rsem.at[self.slot, index]
        if kind == 0:
            ref = self.view(zs if arriving else p.z, p.col, self.lo, self.hi)
            return remote(ref, ref, send, recv, p.zn(d))
        if kind == 1:
            ref = self.view(zs, col_x if arriving else p.col, self.lo, self.hi)
            return remote(ref, ref, send, recv, p.xn)
        if kind == 2:
            ref = self.view(zs, col_y if arriving else p.col, self.lo, self.hi)
            return remote(ref, ref, send, recv, p.yn)
        if kind == 3:
            ref = self.view(zs, col_d if arriving else col_x, self.lo, self.mid)
            return remote(ref, ref, send, recv, p.yn)
        ref = self.view(zs, col_d if arriving else col_y, self.mid, self.hi)
        return remote(ref, ref, send, recv, p.xn)

    def start_z(self):
        for d in (1, 3, 2):
            self.copy(0, d, False).start()

    def pass_z(self, d):
        self.copy(0, d, True).wait_recv()
        self.copy(1, d, False).start()
        self.copy(2, d, False).start()

    def pass_plane(self, d):
        self.copy(1, d, True).wait_recv()
        self.copy(3, d, False).start()
        self.copy(2, d, True).wait_recv()
        self.copy(4, d, False).start()

    def finish(self):
        for d in (1, 3, 2):
            self.copy(3, d, True).wait_recv()
            self.copy(4, d, True).wait_recv()

    def drain(self):
        for kind in range(5):
            for d in (1, 3, 2):
                self.copy(kind, d, False).wait_send()


class Swap:
    def __init__(self, source, whole, ssem, rsem, lsem, here, rows):
        self.source, self.whole, self.ssem, self.rsem, self.lsem = source, whole, ssem, rsem, lsem
        self.here, self.rows = here, rows

    def block(self, ctx):
        return self.whole.at[pl.ds(pl.multiple_of(ctx * self.rows, 16), self.rows)]

    def own(self):
        return pltpu.make_async_copy(self.source.at[self.here.x], self.block(self.here.ctx), self.lsem)

    def over(self, arriving):
        p = self.here
        ctx = (1 - p.x) * 2 + p.core if arriving else p.ctx
        return remote(self.source.at[1 - p.x], self.block(ctx), self.ssem.at[0], self.rsem.at[0], p.xn)

    def pair(self, arriving):
        p = self.here
        ctx = p.x * 2 + 1 - p.core if arriving else p.ctx
        return remote(self.source.at[p.x], self.block(ctx), self.ssem.at[1], self.rsem.at[1], p.sib)

    def forward(self, arriving):
        p = self.here
        ctx = (1 - p.x) * 2 + (1 - p.core if arriving else p.core)
        return remote(self.block(ctx), self.block(ctx), self.ssem.at[2], self.rsem.at[2], p.sib)

    def start(self):
        self.over(False).start()
        self.own().start()
        self.pair(False).start()

    def relay(self):
        self.over(True).wait_recv()
        self.forward(False).start()

    def finish(self):
        self.own().wait()
        self.pair(True).wait_recv()
        self.forward(True).wait_recv()

    def drain(self):
        self.over(False).wait_send()
        self.pair(False).wait_send()
        self.forward(False).wait_send()


def enter(partners):
    barrier = pltpu.get_barrier_semaphore()
    for partner in partners:
        pl.semaphore_signal(barrier, inc=1, device_id=partner, device_id_type=MESH)
    pl.semaphore_wait(barrier, len(partners))


class Reduce:
    def __init__(self, g, r1, r2, r3, r1z, r2z, rz, fin, gfin, ssem, rsem, lsem, here, z_first):
        self.g, self.r3, self.rz, self.fin, self.gfin = g, r3, rz, fin, gfin
        self.ones, self.twos = (r1z, r1), (r2z, r2)
        self.ssem, self.rsem, self.lsem, self.here, self.z_first = ssem, rsem, lsem, here, z_first
        self.width = g.shape[-1]
        self.lo = pl.ds(0, self.width // 2)
        self.hi = pl.ds(self.width // 2, self.width // 2)
        self.piece = g.shape[4]

    def rows_z(self, c):
        return pl.ds(self.here.z, 1) if c < self.z_first else pl.ds(0, self.here.z_count)

    def count(self, c):
        return 1 if c < self.z_first else self.here.z_count

    def r1(self, c):
        return self.ones[0].at[c] if c < self.z_first else self.ones[1].at[c - self.z_first]

    def r2(self, c):
        return self.twos[0].at[c] if c < self.z_first else self.twos[1].at[c - self.z_first]

    def link(self, c, index, src, dst, device):
        return remote(src, dst, self.ssem.at[c, index], self.rsem.at[c, index], device)

    def x1(self, c):
        p = self.here
        return self.link(c, 0, self.g.at[c, 1 - p.x, :, self.rows_z(c), :, self.lo], self.r1(c).at[0], p.xn)

    def y1(self, c):
        p = self.here
        return self.link(c, 1, self.g.at[c, :, 1 - p.y, self.rows_z(c), :, self.hi], self.r1(c).at[1], p.yn)

    def x2(self, c):
        p = self.here
        return self.link(c, 2, self.g.at[c, p.x, 1 - p.y, self.rows_z(c), :, self.lo], self.r2(c).at[0], p.yn)

    def y2(self, c):
        p = self.here
        return self.link(c, 3, self.g.at[c, 1 - p.x, p.y, self.rows_z(c), :, self.hi], self.r2(c).at[1], p.xn)

    def z1(self, c, d):
        p = self.here
        to = lax.rem(p.z + d, p.z_count)
        if c < self.z_first:
            return self.link(c, 3 + d, self.g.at[c, :, :, to], self.rz.at[c, d - 1], p.zn(d))
        return self.link(c, 3 + d, self.g.at[c, p.x, p.y, to], self.r3.at[c - self.z_first, d - 1], p.zn(d))

    def spread(self, c, which, arriving):
        p = self.here
        device, col = (
            (p.xn, p.y * 2 + 1 - p.x),
            (p.yn, (1 - p.y) * 2 + p.x),
            ((1 - p.y, (1 - p.x) * 2 + p.core, p.z), (1 - p.y) * 2 + 1 - p.x),
        )[which]
        col = col if arriving else p.col
        return self.link(c, 7 + which, self.fin.at[c], self.gfin.at[p.core, c, col], device)

    def keep(self, c):
        return pltpu.make_async_copy(self.fin.at[c], self.gfin.at[self.here.core, c, self.here.col], self.lsem.at[c])

    def pair(self, c, arriving):
        core = 1 - self.here.core if arriving else self.here.core
        return self.link(c, 10, self.gfin.at[core, c], self.gfin.at[core, c], self.here.sib)

    def start(self, c):
        if c < self.z_first:
            for d in (1, 3, 2):
                self.z1(c, d).start()
        else:
            self.plane(c)

    def gathered_z(self, c):
        p = self.here
        for d in (1, 3, 2):
            self.z1(c, d).wait_recv()
        for x in range(2):
            for y in range(2):
                total = self.g[c, x, y, p.z].astype(F32)
                for d in range(3):
                    total = total + self.rz[c, d, x, y].astype(F32)
                self.g[c, x, y, p.z] = total.astype(BF)
        self.plane(c)

    def plane(self, c):
        self.x1(c).start()
        self.y1(c).start()

    def second(self, c):
        p = self.here
        h = self.width // 2

        def zi(k):
            return p.z if c < self.z_first else k

        self.x1(c).wait_recv()

        def add_x(k, carry):
            for y in range(2):
                self.g[c, p.x, y, zi(k), :, :h] = (
                    self.g[c, p.x, y, zi(k), :, :h].astype(F32) + self.r1(c)[0, y, k].astype(F32)
                ).astype(BF)
            return carry

        lax.fori_loop(0, self.count(c), add_x, 0)
        self.x2(c).start()
        self.y1(c).wait_recv()

        def add_y(k, carry):
            for x in range(2):
                self.g[c, x, p.y, zi(k), :, h:] = (
                    self.g[c, x, p.y, zi(k), :, h:].astype(F32) + self.r1(c)[1, x, k].astype(F32)
                ).astype(BF)
            return carry

        lax.fori_loop(0, self.count(c), add_y, 0)
        self.y2(c).start()

    def third(self, c):
        p = self.here
        h = self.width // 2
        self.x2(c).wait_recv()
        self.y2(c).wait_recv()
        if c < self.z_first:
            self.fin[c, :, :h] = (self.g[c, p.x, p.y, p.z, :, :h].astype(F32) + self.r2(c)[0, 0].astype(F32)).astype(BF)
            self.fin[c, :, h:] = (self.g[c, p.x, p.y, p.z, :, h:].astype(F32) + self.r2(c)[1, 0].astype(F32)).astype(BF)
            self.publish(c)
            return

        def add(k, carry):
            self.g[c, p.x, p.y, k, :, :h] = (
                self.g[c, p.x, p.y, k, :, :h].astype(F32) + self.r2(c)[0, k].astype(F32)
            ).astype(BF)
            self.g[c, p.x, p.y, k, :, h:] = (
                self.g[c, p.x, p.y, k, :, h:].astype(F32) + self.r2(c)[1, k].astype(F32)
            ).astype(BF)
            return carry

        lax.fori_loop(0, p.z_count, add, 0)
        for d in (1, 3, 2):
            self.z1(c, d).start()

    def fourth(self, c):
        if c < self.z_first:
            return
        p = self.here
        for d in (1, 3, 2):
            self.z1(c, d).wait_recv()
        total = self.g[c, p.x, p.y, p.z].astype(F32)
        for d in range(3):
            total = total + self.r3[c - self.z_first, d].astype(F32)
        self.fin[c] = total.astype(BF)
        self.publish(c)

    def publish(self, c):
        for which in range(3):
            self.spread(c, which, False).start()
        self.keep(c).start()

    def fifth(self, c):
        for which in range(3):
            self.spread(c, which, True).wait_recv()
        self.keep(c).wait()
        self.pair(c, False).start()

    def last(self, c):
        self.pair(c, True).wait_recv()
        for copy in (self.x1(c), self.y1(c), self.x2(c), self.y2(c), self.pair(c, False)):
            copy.wait_send()
        for d in (1, 3, 2):
            self.z1(c, d).wait_send()
        for which in range(3):
            self.spread(c, which, False).wait_send()


def edges():
    starts, buckets = [], [15]
    lows = (8,) + BORDERS
    for b in range(14, 7, -1):
        starts.append(1 - lows[b - 7])
        buckets.append(b)
    for n in range(7, -1, -1):
        starts.append(-n)
        buckets.append(n)
    for n in range(1, 8):
        starts.append(n)
        buckets.append(16 + n)
    for b in range(8, 16):
        starts.append(lows[b - 8])
        buckets.append(16 + b)
    return starts, buckets


def gelu_parts(v):
    c0 = math.sqrt(2.0 / math.pi)
    sq = v * v
    th = jnp.tanh(v * (c0 + (c0 * 0.044715) * sq))
    half = 0.5 + 0.5 * th
    slope = half + (0.5 * v) * (1.0 - th * th) * (c0 + (3.0 * 0.044715 * c0) * sq)
    return v * half, slope


def layer_kernel(
    inputs, positions, wq, wk, wv, wo, win, wout, extra_in, cotangent,
    out_ref, igrad_ref, gfin, evec_out, probs_out,
    w, x_all, cot_all, extra, n_t, turned, q, k, v, mixed, linv, table, pool, bound, ka, va, p_slot, shards,
    y_in, t_in, o_send, o_in, slope, gmid, dk_acc, dv_acc, cat, stage, ig_in,
    hist, far_sum, gain_acc, e_src, e_in,
    g, r1, r2, r3, r1z, r2z, rz, fin,
    ssem, rsem, swap_s, swap_r, cot_s, cot_r, e_s, e_r, lsem, psem, y_s, y_r, t_s, t_r, o_s, o_r, out_s, out_r, u_s, u_r, ev_s, ev_r,
    g_s, g_r, g_l, osem,
):
    here = Place(lax.axis_size("fsdp"))
    p = here
    D, INNER = w.shape[0], wo.shape[0]
    half = INNER // 2
    ffh = win.shape[1] // 2
    shard = wq.shape[0]
    piece = shard // 4
    R = x_all.shape[0]
    heads = half // 64
    nt = R // T
    active = pool.at[:, pl.ds(0, ffh)]
    y_own = pool.at[:, pl.ds(ffh, D)]
    t_own = stage
    own_rows = pl.ds(pl.multiple_of(p.z * shard, 16), shard)
    half_cols = pl.ds(pl.multiple_of(p.core * half, 128), half)
    ff_cols = pl.ds(pl.multiple_of(p.core * ffh, 128), ffh)
    c_o, c_in, c_out, c_end = 3 * half, 4 * half, 4 * half + ffh, 4 * half + 2 * ffh

    loads = [
        pltpu.make_async_copy(wq.at[:, half_cols], w.at[own_rows, pl.ds(0, half)], lsem.at[0]),
        pltpu.make_async_copy(wk.at[:, half_cols], w.at[own_rows, pl.ds(half, half)], lsem.at[1]),
        pltpu.make_async_copy(wv.at[:, half_cols], w.at[own_rows, pl.ds(2 * half, half)], lsem.at[2]),
        pltpu.make_async_copy(win.at[:, ff_cols], w.at[own_rows, pl.ds(c_in, ffh)], lsem.at[3]),
        pltpu.make_async_copy(
            wo.at[pl.ds(pl.multiple_of(p.core * half, 16), half)], shards.at[pl.ds(ffh, half)], lsem.at[4]
        ),
        pltpu.make_async_copy(extra_in, extra.at[own_rows], lsem.at[6]),
    ]
    loads += [
        pltpu.make_async_copy(
            wout.at[pl.ds(pl.multiple_of(p.core * ffh + c * 512, 16), 512)],
            shards.at[pl.ds(c * 512, 512)],
            lsem.at[9 + c],
        )
        for c in range(ffh // 512)
    ]
    for load in loads:
        load.start()
    enter([p.sib, p.xn, p.yn, p.zn(1), p.zn(2), p.zn(3)])
    swap = Swap(inputs, x_all, swap_s, swap_r, lsem.at[7], here, inputs.shape[1])
    swap.start()
    cot_swap = Swap(cotangent, cot_all, cot_s, cot_r, lsem.at[8], here, inputs.shape[1])

    def extra_copy(d, arriving):
        zs = lax.rem(p.z + p.z_count - d, p.z_count) if arriving else p.z
        ref = extra.at[pl.ds(pl.multiple_of(zs * shard, 16), shard)]
        return remote(ref, ref, e_s.at[d - 1], e_r.at[d - 1], p.zn(d))

    loads[5].wait()
    for d in (1, 3, 2):
        extra_copy(d, False).start()
    gathers = [
        Gather(w, ssem, rsem, 0, 0, 7 * T, c_o, here, shard, piece),
        Gather(w, ssem, rsem, 1, c_o, c_o + 12 * T, c_out, here, shard, piece),
        Gather(w, ssem, rsem, 2, c_out, c_out + 10 * T, c_end, here, shard, piece),
    ]
    for load in loads[:3]:
        load.wait()
    gathers[0].start_z()

    loads[4].wait()
    w[own_rows, pl.ds(c_o, half)] = shards[ffh : ffh + half, :].astype(F32).T.astype(BF)
    for c in range(ffh // 512):
        loads[6 + c].wait()
        w[own_rows, pl.ds(c_out + c * 512, 512)] = shards[c * 512 : (c + 1) * 512, :].astype(F32).T.astype(BF)
    loads[3].wait()

    starts, classes = edges()
    lane = lax.broadcasted_iota(jnp.int32, (1, T), 1)
    pos = positions[pl.ds(p.x, 1), :]
    for a in range(nt):
        col = jnp.broadcast_to(pos[:, a * T : (a + 1) * T], (T, T)).T
        for d in range(3):
            b = a + d - 1
            if 0 <= b < nt:
                e = pos[:, b * T : (b + 1) * T] - col
                count = jnp.zeros((T, T), F32)
                for j, first in enumerate(starts):
                    below = jnp.sum(jnp.where(e < first, 1.0, 0.0), axis=1, keepdims=True)
                    count = jnp.where(lane == j, below, count)
                bound[a * T : (a + 1) * T, d * T : (d + 1) * T] = count.astype(BF)

    for d in (1, 3, 2):
        gathers[0].pass_z(d)
    gathers[1].start_z()
    gathers[2].start_z()

    for d in (1, 3, 2):
        extra_copy(d, True).wait_recv()
    buckets_per = 8
    rows = [extra[zs * shard : zs * shard + 16, :].astype(F32)[:buckets_per] for zs in range(4)]
    flat = jnp.concatenate(rows + [jnp.zeros((T - 32, T), F32)], axis=0)
    table[...] = flat.T
    gains = jnp.concatenate(
        [extra[t * T : (t + 1) * T, :].astype(F32).T[0:8] for t in range(D // T)], axis=1
    )
    gain_one, gain_two = gains[0:1], gains[1:2]

    for a in range(nt):
        col = jnp.broadcast_to(pos[:, a * T : (a + 1) * T], (T, T)).T
        for d in range(3):
            b = a + d - 1
            if 0 <= b < nt:
                idx = bucket_of(pos[:, b * T : (b + 1) * T] - col)
                for h in range(heads):
                    tab = jnp.broadcast_to(table[pl.ds(2 + p.core * heads + h, 1), :], (T, T))
                    pool[a * T : (a + 1) * T, (h * 3 + d) * T : (h * 3 + d + 1) * T] = jnp.take_along_axis(
                        tab, idx, axis=1
                    ).astype(BF)

    swap.relay()
    for d in (1, 3, 2):
        gathers[0].pass_plane(d)
    swap.finish()
    cot_swap.start()
    for c in range(4):
        rows = slice(c * (R // 4), (c + 1) * (R // 4))
        xf = x_all[rows, :].astype(F32)
        scale = lax.rsqrt(jnp.mean(xf * xf, axis=1, keepdims=True) + EPS)
        stage[rows, :] = (xf * scale * gain_one).astype(BF)
        n_t[:, rows] = (xf * scale * gain_one).T.astype(BF)
    gathers[0].finish()

    def project(c, carry):
        rows = pl.ds(pl.multiple_of(c * 256, 256), 256)
        for n, dest in enumerate((q, k, v)):
            out = dot_nn(stage[rows, :], w[:, n * half : (n + 1) * half]).astype(BF)
            for pair in range(half // T):
                dest[pair, rows, :] = out[:, pair * T : (pair + 1) * T]
        return carry

    lax.fori_loop(0, R // 256, project, 0)

    QT = 256
    sub = QT // T
    units = [(qi, h) for qi in range(R // QT) for h in range(2)]
    events = {}
    e = []
    for d in (1, 3, 2):
        e.append(lambda d=d: gathers[1].pass_z(d))
    for d in (1, 3, 2):
        e.append(lambda d=d: gathers[1].pass_plane(d))
    for d in (1, 3, 2):
        e.append(lambda d=d: gathers[2].pass_z(d))
    slots = [3, 4, 5, 9, 11, 13, 17, 18, 19]
    for s, f in zip(slots, e):
        events[s] = f

    lane = lax.broadcasted_iota(jnp.int32, (1, T), 1)

    def pair_step(hp, carry):
        lane_k = lax.broadcasted_iota(jnp.int32, (R, T), 1)
        tile_k = lax.broadcasted_iota(jnp.int32, (R, T), 0) // T
        for h in range(2):
            tab = table[pl.ds(2 + p.core * heads + hp * 2 + h, 1), :]
            inside = (lane_k < 64) if h == 0 else (lane_k >= 64)
            other = lane_k - 64 if h == 0 else lane_k
            far = jnp.where(tile_k < other - 1, tab[:, 15:16], jnp.where(tile_k > other + 1, tab[:, 31:32], 0.0))
            far = jnp.where(other < nt, far, 0.0)
            ka[h] = jnp.where(inside, k[hp].astype(F32), far).astype(BF)
            va[h] = jnp.where(inside, v[hp].astype(F32), 1.0).astype(BF)
        lane_q = lax.broadcasted_iota(jnp.int32, (QT, T), 1)
        tile_q = lax.broadcasted_iota(jnp.int32, (QT, T), 0) // T
        mixes = {}
        for n, (qi, h) in enumerate(units):
            for trip in range(heads // 2):
                if trip * len(units) + n in events:
                    pl.when(hp == trip)(events[trip * len(units) + n])
            rows = slice(qi * QT, (qi + 1) * QT)
            inside = (lane_q < 64) if h == 0 else (lane_q >= 64)
            other = lane_q - 64 if h == 0 else lane_q
            hot = jnp.where(other == tile_q + qi * sub, 1.0, 0.0)
            qm = jnp.where(inside, q[hp, rows, :].astype(F32), hot).astype(BF)
            s = dot_nt(qm, ka[h])
            strips = []
            for si in range(sub):
                a = qi * sub + si
                st = s[si * T : (si + 1) * T]
                lo, hi = max(a - 1, 0), min(a + 2, nt)
                parts = [st[:, : lo * T]] if lo > 0 else []
                lanes = pl.ds(pl.multiple_of((hp * 2 + h) * 3 * T + (lo - a + 1) * T, T), (hi - lo) * T)
                near = pool[a * T : (a + 1) * T, lanes]
                parts.append(st[:, lo * T : hi * T] + near.astype(F32))
                if hi < nt:
                    parts.append(st[:, hi * T :])
                strips.append(jnp.concatenate(parts, axis=1))
            s = jnp.concatenate(strips, axis=0)
            m = jnp.max(s, axis=1, keepdims=True)
            pb = jnp.exp2((s - m) * LOG2E).astype(BF)
            slot = n % 2
            store = pltpu.make_async_copy(p_slot.at[slot], probs_out.at[hp * 2 + h, pl.ds(qi * QT, QT)], psem.at[slot])
            if n < 2:
                pl.when(hp > 0)(store.wait)
            else:
                store.wait()
            p_slot[slot] = pb
            store.start()
            mixes[h] = dot_nn(pb, va[h])
            if h == 1:
                o = jnp.where(lane < 64, mixes[0], mixes[1])
                total = pltpu.roll(jnp.where(lane < 64, mixes[1], mixes[0]), 64, 1)
                inv = 1.0 / total
                mixed[hp, rows, :] = (o * inv).astype(BF)
                linv[hp, rows, :] = inv
        return carry

    lax.fori_loop(0, heads // 2, pair_step, 0)
    for slot in range(2):
        pltpu.make_async_copy(p_slot.at[slot], probs_out.at[0, pl.ds(0, QT)], psem.at[slot]).wait()


    B = 256
    blocks = R // B
    FW = 512
    cot_swap.relay()
    for d in (1, 3, 2):
        gathers[2].pass_plane(d)
    gathers[1].finish()

    def y_copy(i, arriving=False):
        rows = pl.ds(pl.multiple_of(i * B, B), B)
        return remote(y_own.at[rows], y_in.at[rows], y_s.at[i], y_r.at[i], p.sib)

    def t_copy(i):
        rows = pl.ds(pl.multiple_of(i * B, B), B)
        return remote(t_own.at[rows], t_in.at[rows], t_s.at[i], t_r.at[i], p.sib)

    def o_copy(n):
        return remote(o_send.at[n], o_in.at[n], o_s.at[n], o_r.at[n], p.sib)

    def project_out(i, carry):
        rows = pl.ds(pl.multiple_of(i * B, B), B)
        mx = jnp.concatenate([mixed[pair, rows, :] for pair in range(half // T)], axis=1)
        y_own[rows, :] = dot_nt(mx, w[:, c_o : c_o + half]).astype(BF)
        y_copy(i).start()
        return carry

    lax.fori_loop(0, blocks, project_out, 0)

    def middle_of(rows):
        mid = x_all[rows, :].astype(F32) + (y_own[rows, :].astype(F32) + y_in[rows, :].astype(F32))
        return mid, lax.rsqrt(jnp.mean(mid * mid, axis=1, keepdims=True) + EPS)

    def ffn_in(i, carry):
        rows = pl.ds(pl.multiple_of(i * B, B), B)
        y_copy(i).wait_recv()
        mid, scale = middle_of(rows)
        n2f = mid * scale * gain_two
        n2 = n2f.astype(BF)
        stage[rows, :] = n2
        for j in range(ffh // FW):
            hidden = dot_nn(n2, w[:, c_in + j * FW : c_in + (j + 1) * FW])
            act, slo = gelu_parts(hidden)
            active[rows, j * FW : (j + 1) * FW] = act.astype(BF)
            slope[rows, j * FW : (j + 1) * FW] = slo.astype(BF)
        return carry

    lax.fori_loop(0, blocks, ffn_in, 0)
    cot_swap.finish()
    for i in range(blocks):
        rows = slice(i * B, (i + 1) * B)
        turned[:, rows] = cot_all[rows, :].astype(F32).T.astype(BF)

    red = Reduce(g, r1, r2, r3, r1z, r2z, rz, fin, gfin, g_s, g_r, g_l, here, 2)

    def keep_pieces(c, lo, left, right):
        for n in range(0, right.shape[1], 2 * T):
            value = dot_nn(left, right[:, n : n + 2 * T])
            for zs in range(p.z_count):
                for col in range(4):
                    first_row = zs * shard + col * piece
                    g[c, col % 2, col // 2, zs, :, lo + n : lo + n + value.shape[1]] = value[first_row : first_row + piece].astype(BF)

    for c in range(ffh // FW):
        keep_pieces(c, 0, turned[...], active[:, c * FW : (c + 1) * FW])
        red.start(c)
    for i in range(blocks):
        rows = slice(i * B, (i + 1) * B)
        turned[:, rows] = stage[rows, :].astype(F32).T.astype(BF)
    gathers[2].finish()

    def ffn_back(i, carry):
        rows = pl.ds(pl.multiple_of(i * B, B), B)
        cot = cot_all[rows, :]
        for j in range(ffh // FW):
            grad = dot_nn(cot, w[:, c_out + j * FW : c_out + (j + 1) * FW])
            cols = slice(j * FW, (j + 1) * FW)
            slope[rows, cols] = (grad * slope[rows, cols].astype(F32)).astype(BF)
        t_own[rows, :] = dot_nt(slope[rows, :], w[:, c_in:c_out]).astype(BF)
        t_copy(i).start()
        o = dot_nt(active[rows, :], w[:, c_out:c_end])
        n = i // 2

        @pl.when(i % 2 == p.core)
        def _():
            gmid[n] = o

        @pl.when(i % 2 != p.core)
        def _():
            o_send[n] = o.astype(BF)
            o_copy(n).start()

        return carry

    lax.fori_loop(0, blocks, ffn_back, 0)
    red.second(2)
    for c in range(ffh // FW):
        keep_pieces(3 + c, 0, turned[...], slope[:, c * FW : (c + 1) * FW])
        red.start(3 + c)

    gain_acc[...] = jnp.zeros_like(gain_acc)

    def back_middle(i, carry):
        rows = pl.ds(pl.multiple_of(i * B, B), B)
        t_copy(i).wait_recv()
        mid, scale = middle_of(rows)
        t = t_own[rows, :].astype(F32) + t_in[rows, :].astype(F32)
        tg = t * gain_two
        dot = jnp.mean(tg * mid, axis=1, keepdims=True)
        gm = cot_all[rows, :].astype(F32) + scale * tg - (scale * scale * scale * dot) * mid
        gy = gm.astype(BF)
        turned[:, rows] = gm.T.astype(BF)
        grad = dot_nn(gy, w[:, c_o : c_o + half])
        for pair in range(half // T):
            slope[rows, D + pair * T : D + (pair + 1) * T] = (grad[:, pair * T : (pair + 1) * T] * linv[pair, rows, :]).astype(BF)
        n = i // 2

        @pl.when(i % 2 == p.core)
        def _():
            gain_acc[1:2, :] += jnp.sum(t * mid * scale, axis=0, keepdims=True)
            o_copy(n).wait_recv()
            slope[pl.ds(pl.multiple_of(n * B, B), B), :D] = (mid + gmid[n] + o_in[n].astype(F32)).astype(BF)
            gmid[n] = gm

        return carry

    lax.fori_loop(0, blocks, back_middle, 0)
    out_own = pltpu.make_async_copy(slope.at[pl.ds(pl.multiple_of(p.x * B, B), B), pl.ds(0, D)], out_ref.at[p.x], osem.at[0])
    out_over = remote(slope.at[pl.ds(pl.multiple_of((1 - p.x) * B, B), B), pl.ds(0, D)], out_ref.at[p.x], out_s.at[0], out_r.at[0], p.xn)
    out_there = remote(slope.at[pl.ds(pl.multiple_of((1 - p.x) * B, B), B), pl.ds(0, D)], out_ref.at[1 - p.x], out_s.at[0], out_r.at[0], p.xn)
    out_own.start()
    out_over.start()

    hist[...] = jnp.zeros_like(hist)
    far_sum[...] = jnp.zeros_like(far_sum)
    row_i = lax.broadcasted_iota(jnp.int32, (T, T), 0)
    col_i = lax.broadcasted_iota(jnp.int32, (T, T), 1)
    before = jnp.where(row_i < col_i, 1.0, 0.0).astype(BF)

    def p_load(hp, n):
        qi, h = units[n]
        return pltpu.make_async_copy(probs_out.at[hp * 2 + h, pl.ds(qi * QT, QT)], p_slot.at[n % 2], psem.at[n % 2])

    p_load(0, 0).start()
    stages = {
        0: [lambda: red.third(2)], 1: [lambda: red.second(3)], 4: [lambda: red.second(4)], 6: [lambda: red.third(3)],
        8: [lambda: red.second(5)], 9: [lambda: red.third(4)], 12: [lambda: red.third(5)], 13: [lambda: red.second(6)],
        14: [lambda: red.fourth(2)], 16: [lambda: red.fourth(3)], 17: [lambda: red.third(6)], 18: [lambda: red.fourth(4)],
        19: [lambda: red.fifth(2)], 20: [lambda: red.fourth(5), lambda: red.gathered_z(0)],
        21: [lambda: red.second(7)], 22: [lambda: red.fifth(3), lambda: red.gathered_z(1)], 23: [lambda: red.third(7)],
    }

    def lanes_of(m, hp):
        return pl.ds(pl.multiple_of(m * half + hp * T, T), T)

    def pair_back(hp, carry):
        lane_k = lax.broadcasted_iota(jnp.int32, (R, T), 1)
        tile_k = lax.broadcasted_iota(jnp.int32, (R, T), 0) // T
        for h in range(2):
            inside = (lane_k < 64) if h == 0 else (lane_k >= 64)
            other = lane_k - 64 if h == 0 else lane_k
            va[h] = jnp.where(inside, v[hp].astype(F32), jnp.where(other < 3, 1.0, 0.0)).astype(BF)
            ka[h] = jnp.where(inside, k[hp].astype(F32), jnp.where(other == tile_k, 1.0, 0.0)).astype(BF)
        dk_acc[...] = jnp.zeros_like(dk_acc)
        dv_acc[...] = jnp.zeros_like(dv_acc)
        lane_q = lax.broadcasted_iota(jnp.int32, (QT, T), 1)
        tile_q = lax.broadcasted_iota(jnp.int32, (QT, T), 0) // T
        dqs = {}
        for n, (qi, h) in enumerate(units):
            for trip in range(heads // 2):
                for step in stages.get(trip * len(units) + n, ()):
                    pl.when(hp == trip)(step)
            rows = slice(qi * QT, (qi + 1) * QT)
            inside = (lane_q < 64) if h == 0 else (lane_q >= 64)
            other = lane_q - 64 if h == 0 else lane_q
            do = slope[rows, pl.ds(pl.multiple_of(D + hp * T, T), T)].astype(F32)
            rd = jnp.sum(jnp.where(inside, do * mixed[hp, rows, :].astype(F32), 0.0), axis=1, keepdims=True)
            ra = rd.astype(BF).astype(F32)
            rb = (rd - ra).astype(BF).astype(F32)
            rc = rd - ra - rb
            dm = jnp.where(inside, do, 0.0)
            da = (dm - jnp.where(other == 0, ra, jnp.where(other == 1, rb, jnp.where(other == 2, rc, 0.0)))).astype(BF)
            dm = dm.astype(BF)
            qm = jnp.where(inside, q[hp, rows, :].astype(F32), 0.0).astype(BF)
            dp = dot_nt(da, va[h])
            p_load(hp, n).wait()
            if n + 1 < len(units):
                p_load(hp, n + 1).start()
            else:
                pl.when(hp < heads // 2 - 1)(lambda: p_load(hp + 1, 0).start())
            pb = p_slot[n % 2]
            ds = (pb.astype(F32) * dp).astype(BF)
            dqf = dot_nn(ds, ka[h])
            dqs[h] = dqf
            dk_acc[...] += dot_tn(qm, ds)
            dv_acc[...] += dot_tn(dm, pb)
            spare = jnp.where(inside, 0.0, dqf)
            tile = tile_q + qi * sub
            for m, cond in enumerate((other < tile - 1, jnp.logical_and(other > tile + 1, other < nt), other < nt)):
                far_sum[hp * 2 + h, m : m + 1, :] += jnp.sum(jnp.where(cond, spare, 0.0), axis=0, keepdims=True)
            for si in range(sub):
                a = qi * sub + si
                for d in range(3):
                    b = a + d - 1
                    if 0 <= b < nt:
                        block = ds[si * T : (si + 1) * T, b * T : (b + 1) * T]
                        sums = dot_nn(block, before)
                        idx = bound[a * T : (a + 1) * T, d * T : (d + 1) * T].astype(F32).astype(jnp.int32)
                        got = jnp.take_along_axis(sums, jnp.minimum(idx, T - 1), axis=1)
                        got = got + jnp.where(idx > T - 1, block[:, T - 1 : T].astype(F32), 0.0)
                        hist[hp * 2 + h] += jnp.sum(got.reshape(T // 8, 8, T), axis=0)
            if h == 1:
                cat[rows, lanes_of(0, hp)] = jnp.where(lane < 64, dqs[0], dqs[1]).astype(BF)
        cat[:, lanes_of(1, hp)] = dk_acc[...].T.astype(BF)
        cat[:, lanes_of(2, hp)] = dv_acc[...].T.astype(BF)
        c = 6 + hp
        for m in range(3):
            keep_pieces(c, m * T, n_t[...], cat[:, lanes_of(m, hp)])
        keep_pieces(c, 3 * T, turned[...], mixed[hp])
        for trip in range(heads // 2):
            pl.when(hp == trip)(functools.partial(red.start, 6 + trip))
        return carry

    lax.fori_loop(0, heads // 2, pair_back, 0)

    def u_copy(n):
        return remote(slope.at[pl.ds((2 + n) * B, B), pl.ds(0, D)], o_in.at[2 + n], u_s.at[n], u_r.at[n], p.sib)

    for n in range(2):
        rows = pl.ds(pl.multiple_of((2 * n + 1 - p.core) * B, B), B)
        slope[(2 + n) * B : (3 + n) * B, :D] = dot_nt(cat[rows, :], w[:, :c_o]).astype(BF)
        u_copy(n).start()
    red.second(0)
    red.second(1)
    red.fourth(6)
    red.fifth(4)
    red.fifth(5)
    for n in range(2):
        rows = pl.ds(pl.multiple_of((2 * n + p.core) * B, B), B)
        t = dot_nt(cat[rows, :], w[:, :c_o])
        u_copy(n).wait_recv()
        t = t + o_in[2 + n].astype(F32)
        xf = x_all[rows, :].astype(F32)
        scale = lax.rsqrt(jnp.mean(xf * xf, axis=1, keepdims=True) + EPS)
        tg = t * gain_one
        dot = jnp.mean(tg * xf, axis=1, keepdims=True)
        gmid[n] = gmid[n] + scale * tg - (scale * scale * scale * dot) * xf
        gain_acc[0:1, :] += jnp.sum(t * xf * scale, axis=0, keepdims=True)
    ig_own = pltpu.make_async_copy(gmid.at[p.x], igrad_ref.at[p.x], osem.at[1])
    ig_own.start()
    slope[:B, D:] = gmid[1 - p.x].astype(BF)
    ig_over = remote(slope.at[pl.ds(0, B), pl.ds(D, D)], ig_in, out_s.at[1], out_r.at[1], p.xn)
    ig_over.start()

    gains_rows = [gain_acc[m : m + 1, t * T : (t + 1) * T] for m in range(2) for t in range(D // T)]
    class_of = jnp.zeros((1, T), jnp.int32)
    for j, bkt in enumerate(classes):
        class_of = jnp.where(lane == bkt, j, class_of)
    used = jnp.logical_and(lane < 32, lane != 16)
    rows_h = []
    for h in range(heads):
        upto = jnp.sum(hist[h], axis=0, keepdims=True)
        sums = jnp.sum(far_sum[h], axis=1, keepdims=True)
        left, right, every = sums[0:1], sums[1:2], sums[2:3]
        near = every - left - right
        n_edges = len(starts)
        upto = jnp.where(lane < n_edges, upto, jnp.where(lane == n_edges, near, 0.0))
        below = jnp.where(lane == 0, 0.0, pltpu.roll(upto, 1, 1))
        per = upto - below + jnp.where(lane == 0, left, jnp.where(lane == n_edges, right, 0.0))
        rows_h.append(per)
    heads_rows = jnp.concatenate(rows_h + [jnp.zeros((8 - heads, T), F32)], axis=0)
    picked = jnp.take_along_axis(heads_rows, jnp.broadcast_to(class_of, (8, T)), axis=1)
    picked = jnp.where(used, picked, 0.0)[:heads]
    zero = jnp.zeros((heads, T), F32)
    first_half = jnp.where(p.core == 0, picked, zero)
    other_half = jnp.where(p.core == 0, zero, picked)
    e_src[0] = jnp.concatenate(gains_rows + [first_half, other_half], axis=0)

    def e_copy(n):
        device = (p.sib, p.xn, p.yn, p.zn(1), p.zn(2), p.zn(3))[n]
        return remote(e_src.at[min(n, 3)], e_in.at[n], ev_s.at[n], ev_r.at[n], device)

    for n in range(3):
        e_copy(n).start()
        e_copy(n).wait_recv()
        e_src[n + 1] = e_src[n] + e_in[n]
    for n in range(3, 6):
        e_copy(n).start()
    red.second(8)
    red.fourth(7)
    red.third(0)
    red.third(1)
    red.third(8)
    red.fifth(6)
    red.fifth(7)
    red.fifth(0)
    red.fifth(1)
    red.fourth(8)
    red.fifth(8)
    for n in range(3, 6):
        e_copy(n).wait_recv()
    e_src[4] = e_src[3] + e_in[3] + e_in[4] + e_in[5]
    ev_out = pltpu.make_async_copy(e_src.at[4], evec_out, osem.at[2])
    ev_out.start()
    ig_over.wait_recv()
    ig_own.wait()
    gmid[0] = ig_in[...].astype(F32)
    ig_there = pltpu.make_async_copy(gmid.at[0], igrad_ref.at[1 - p.x], osem.at[1])
    ig_there.start()
    out_own.wait()
    out_there.wait_recv()
    for c in range(g.shape[0]):
        red.last(c)
    for i in range(blocks):
        y_copy(i).wait_send()
        t_copy(i).wait_send()
    for n in range(2):
        o_copy(n).wait_send()
        u_copy(n).wait_send()
    out_over.wait_send()
    ig_over.wait_send()
    for n in range(6):
        e_copy(n).wait_send()
    for gather in gathers:
        gather.drain()
    swap.drain()
    cot_swap.drain()
    for d in (1, 3, 2):
        extra_copy(d, False).wait_send()
    ev_out.wait()
    ig_there.wait()


def layer(inputs, positions, wq, wk, wv, wo, win, wout, extra_in, cotangent):
    D, INNER, FF = win.shape[0] * lax.axis_size("fsdp"), wo.shape[0], win.shape[1]
    half, ffh, shard = INNER // 2, FF // 2, wq.shape[0]
    B = inputs.shape[1]
    R = inputs.shape[0] * B * 2
    heads, pairs = half // 64, half // T
    width = 4 * half + 2 * ffh
    piece, FW = shard // 4, 512
    nc = width // FW
    zf = 2
    sds = jax.ShapeDtypeStruct
    any_ = pl.BlockSpec(memory_space=pl.ANY)
    vm = pl.BlockSpec(memory_space=pltpu.VMEM)
    sem = pltpu.SemaphoreType.DMA
    V = pltpu.VMEM
    return pl.pallas_call(
        layer_kernel,
        in_specs=[any_, vm] + [any_] * 8,
        out_specs=[any_] * 5,
        out_shape=[
            sds(inputs.shape, BF), sds(inputs.shape, F32), sds((2, nc, 4, piece, FW), BF), sds((24, T), F32), sds((heads, R, R), BF),
        ],
        scratch_shapes=[
            V((D, width), BF), V((R, D), BF), V((R, D), BF), V((D, T), BF), V((D, R), BF), V((D, R), BF),
            V((pairs, R, T), BF), V((pairs, R, T), BF), V((pairs, R, T), BF), V((pairs, R, T), BF), V((pairs, R, T), F32), V((T, T), F32),
            V((R, heads * 3 * T), BF), V((R, 3 * T), BF),
            V((2, R, T), BF), V((2, R, T), BF), V((2, 256, R), BF), V((ffh + half, shard), BF),
            V((R, D), BF), V((R, D), BF), V((2, B, D), BF), V((4, B, D), BF),
            V((R, ffh), BF), V((2, B, D), F32), V((T, R), F32), V((T, R), F32),
            V((R, 3 * half), BF), V((R, D), BF), V((B, D), BF),
            V((heads, 8, T), F32), V((heads, 8, T), F32), V((8, D), F32), V((5, 24, T), F32), V((6, 24, T), F32),
            V((nc, 2, 2, 4, piece, FW), BF), V((nc - zf, 2, 2, 4, piece, FW // 2), BF), V((nc - zf, 2, 4, piece, FW // 2), BF),
            V((nc - zf, 3, piece, FW), BF), V((zf, 2, 2, 1, piece, FW // 2), BF), V((zf, 2, 1, piece, FW // 2), BF),
            V((zf, 3, 2, 2, piece, FW), BF), V((nc, piece, FW), BF),
            sem((3, 15)), sem((3, 15)), sem((3,)), sem((3,)), sem((3,)), sem((3,)), sem((3,)), sem((3,)), sem((12,)), sem((2,)),
            sem((4,)), sem((4,)), sem((4,)), sem((4,)), sem((2,)), sem((2,)), sem((2,)), sem((2,)), sem((2,)), sem((2,)), sem((6,)), sem((6,)),
            sem((nc, 11)), sem((nc, 11)), sem((nc,)), sem((3,)),
        ],
        compiler_params=pltpu.CompilerParams(collective_id=0, has_side_effects=True, vmem_limit_bytes=63 * 2**20),
        name="layer",
    )(inputs, positions, wq, wk, wv, wo, win, wout, extra_in, cotangent)


def fast_device(inputs, positions, w_query, w_key, w_value, w_output, gain_attn, rel_table, w_in, w_out, gain_ffn, cotangent):
    shard = gain_attn.shape[0]
    buckets, heads = rel_table.shape
    padded = jnp.pad(rel_table, ((0, shard - buckets), (0, T - 2 - heads)))
    extra = jnp.concatenate([gain_attn[:, None], gain_ffn[:, None], padded], axis=1)
    out, igrad, gfin, evec, _ = layer(inputs, positions, w_query, w_key, w_value, w_output, w_in, w_out, extra, cotangent)
    gf = gfin.reshape(2, gfin.shape[1], shard, -1).astype(jnp.float32)

    def wide(first, count):
        return jnp.concatenate([gf[core, c] for core in range(2) for c in range(first, first + count)], axis=1)

    def cols(m):
        return jnp.concatenate([gf[core, c][:, m * T : (m + 1) * T] for core in range(2) for c in range(6, 9)], axis=1)

    z = lax.axis_index("fsdp")
    tiles = evec.shape[1]
    gains = evec[:12].reshape(2, -1)
    g_gain = lax.dynamic_slice_in_dim(gains, z * shard, shard, 1)
    g_table = lax.dynamic_slice_in_dim(evec[12:24], z * buckets, buckets, 1).T
    return (
        out, igrad, cols(0), cols(1), cols(2), cols(3).T, g_gain[0], g_table, wide(3, 3), wide(0, 3).T, g_gain[1],
    )


def rms_norm(values, gain):
    return values * lax.rsqrt(jnp.mean(values * values, axis=-1, keepdims=True) + EPS) * gain


def bias_onehot(query_positions, key_places, bucket_count):
    buckets = bucket_of(key_places[:, None, :] - query_positions[:, :, None])
    labels = lax.broadcasted_iota(jnp.int32, (1, bucket_count, 1, 1), 1)
    return (buckets[:, None, :, :] == labels).astype(jnp.bfloat16)


def split_heads(rows, head_count):
    return rows.reshape(rows.shape[0], rows.shape[1], head_count, -1)


def block_scores(query_rows, key_rows, onehot, table_b):
    head_count = table_b.shape[1]
    scores = jnp.einsum(
        "sqhd,skhd->shqk",
        split_heads(query_rows, head_count),
        split_heads(key_rows, head_count),
        preferred_element_type=jnp.float32,
    )
    bias_term = jnp.einsum("sbqk,bh->shqk", onehot, table_b, preferred_element_type=jnp.float32)
    return scores + bias_term


def pair_grads(
    query_rows,
    grad_rows,
    logsum,
    row_products,
    query_positions,
    key_rows,
    value_rows,
    key_places,
    table_b,
):
    head_count = table_b.shape[1]
    onehot = bias_onehot(query_positions, key_places, table_b.shape[0])
    scores = block_scores(query_rows, key_rows, onehot, table_b)
    probs = jnp.exp(scores - logsum[..., None])
    grad_heads = split_heads(grad_rows, head_count)
    dprobs = jnp.einsum(
        "sqhd,skhd->shqk",
        grad_heads,
        split_heads(value_rows, head_count),
        preferred_element_type=jnp.float32,
    )
    grad_scores = (probs * (dprobs - row_products[..., None])).astype(jnp.bfloat16)
    grad_query = jnp.einsum(
        "shqk,skhd->sqhd",
        grad_scores,
        split_heads(key_rows, head_count),
        preferred_element_type=jnp.float32,
    )
    grad_key = jnp.einsum(
        "shqk,sqhd->skhd",
        grad_scores,
        split_heads(query_rows, head_count),
        preferred_element_type=jnp.float32,
    )
    grad_value = jnp.einsum(
        "shqk,sqhd->skhd",
        probs.astype(jnp.bfloat16),
        grad_heads,
        preferred_element_type=jnp.float32,
    )
    grad_table = jnp.einsum(
        "sbqk,shqk->bh", onehot, grad_scores, preferred_element_type=jnp.float32
    )
    return (
        grad_query.reshape(query_rows.shape),
        grad_key.reshape(key_rows.shape),
        grad_value.reshape(value_rows.shape),
        grad_table,
    )


def add_rows(whole, first_row, added_term):
    current = lax.dynamic_slice_in_dim(whole, first_row, added_term.shape[1], 1)
    return lax.dynamic_update_slice_in_dim(whole, current + added_term, first_row, 1)


def project_rows(left_operand, right_operand):
    return jnp.dot(left_operand, right_operand, preferred_element_type=jnp.float32)


def outer_sum(left_operand, right_operand):
    return jnp.einsum("nf,nd->fd", left_operand, right_operand, preferred_element_type=jnp.float32)


def general_device(
    inputs,
    positions,
    w_query,
    w_key,
    w_value,
    w_output,
    gain_attn,
    rel_table,
    w_in,
    w_out,
    gain_ffn,
    cotangent,
):
    groups, block_rows, model_width = inputs.shape
    head_count = rel_table.shape[1]
    tokens = groups * block_rows
    query_w, key_w, value_w, output_w, gain_one, table_b = (
        lax.all_gather(w_query, "fsdp", axis=0, tiled=True),
        lax.all_gather(w_key, "fsdp", axis=0, tiled=True),
        lax.all_gather(w_value, "fsdp", axis=0, tiled=True),
        lax.all_gather(w_output, "fsdp", axis=1, tiled=True),
        lax.all_gather(gain_attn, "fsdp", axis=0, tiled=True),
        lax.all_gather(rel_table, "fsdp", axis=0, tiled=True),
    )
    in_w, out_w, gain_two = (
        lax.all_gather(w_in, "fsdp", axis=0, tiled=True),
        lax.all_gather(w_out, "fsdp", axis=1, tiled=True),
        lax.all_gather(gain_ffn, "fsdp", axis=0, tiled=True),
    )
    gain_one_f = gain_one.astype(jnp.float32)
    gain_two_f = gain_two.astype(jnp.float32)
    own_first = lax.axis_index("ctx") * block_rows
    query_positions = lax.dynamic_slice_in_dim(positions, own_first, block_rows, 1)
    flat_inputs = inputs.reshape(tokens, model_width).astype(jnp.float32)
    normed = rms_norm(flat_inputs, gain_one_f).astype(jnp.bfloat16)
    queries = project_rows(normed, query_w).astype(jnp.bfloat16).reshape(groups, block_rows, -1)
    key_block = project_rows(normed, key_w).astype(jnp.bfloat16).reshape(groups, block_rows, -1)
    value_block = project_rows(normed, value_w).astype(jnp.bfloat16).reshape(groups, block_rows, -1)
    inner_width = queries.shape[2]
    head_size = inner_width // head_count
    start_state = (
        jnp.full((groups, head_count, block_rows), -1e30, jnp.float32),
        jnp.zeros((groups, head_count, block_rows), jnp.float32),
        jnp.zeros((groups, block_rows, head_count, head_size), jnp.float32),
    )
    key_piece = lax.all_gather(key_block, "ctx", axis=1, tiled=True)
    value_portion = lax.all_gather(value_block, "ctx", axis=1, tiled=True)
    piece_rows = key_piece.shape[1]
    step_rows = math.gcd(piece_rows, block_rows)

    def forward_inner_step(block_index, state):
        running, total, weighted = state
        offset = block_index * step_rows
        key_part = lax.dynamic_slice_in_dim(key_piece, offset, step_rows, 1)
        value_part = lax.dynamic_slice_in_dim(value_portion, offset, step_rows, 1)
        key_places = lax.dynamic_slice_in_dim(positions, offset, step_rows, 1)
        onehot = bias_onehot(query_positions, key_places, table_b.shape[0])
        scores = block_scores(queries, key_part, onehot, table_b)
        newest = jnp.maximum(running, jnp.max(scores, axis=-1))
        factor = jnp.exp(running - newest)
        weights = jnp.exp(scores - newest[..., None])
        total = total * factor + jnp.sum(weights, axis=-1)
        update = jnp.einsum(
            "shqk,skhd->sqhd",
            weights.astype(jnp.bfloat16),
            split_heads(value_part, head_count),
            preferred_element_type=jnp.float32,
        )
        weighted = weighted * jnp.transpose(factor, (0, 2, 1))[..., None] + update
        return (newest, total, weighted)

    running, total, weighted = lax.fori_loop(
        0, piece_rows // step_rows, forward_inner_step, start_state
    )
    logsum = running + jnp.log(total)
    mixed = weighted / jnp.transpose(total, (0, 2, 1))[..., None]
    mixed_b = mixed.reshape(tokens, inner_width).astype(jnp.bfloat16)
    middle = flat_inputs + project_rows(mixed_b, output_w)
    normed_two = rms_norm(middle, gain_two_f).astype(jnp.bfloat16)
    hidden = project_rows(normed_two, in_w)
    active = jax.nn.gelu(hidden).astype(jnp.bfloat16)
    result = middle + project_rows(active, out_w)
    output = result.astype(jnp.bfloat16).reshape(inputs.shape)
    grad_top = cotangent.reshape(tokens, model_width).astype(jnp.float32)
    grad_branch = grad_top.astype(jnp.bfloat16)
    grad_out_w = outer_sum(active, grad_branch)
    grad_active = lax.dot_general(
        grad_branch, out_w, (((1,), (1,)), ((), ())), preferred_element_type=jnp.float32
    )
    gelu_pull = jax.vjp(jax.nn.gelu, hidden)[1]
    grad_hidden = gelu_pull(grad_active)[0].astype(jnp.bfloat16)
    grad_in_w = outer_sum(normed_two, grad_hidden)
    grad_normed_two = lax.dot_general(
        grad_hidden, in_w, (((1,), (1,)), ((), ())), preferred_element_type=jnp.float32
    )
    norm_pull = jax.vjp(rms_norm, middle, gain_two_f)[1]
    grad_from_norm, grad_gain_two = norm_pull(grad_normed_two)
    grad_middle = grad_top + grad_from_norm
    ffn_parts = (
        lax.psum_scatter(
            grad_in_w.astype(jnp.bfloat16), "fsdp", scatter_dimension=0, tiled=True
        ).astype(jnp.float32),
        lax.psum_scatter(
            grad_out_w.astype(jnp.bfloat16), "fsdp", scatter_dimension=1, tiled=True
        ).astype(jnp.float32),
        lax.psum_scatter(
            grad_gain_two.astype(jnp.bfloat16), "fsdp", scatter_dimension=0, tiled=True
        ).astype(jnp.float32),
    )
    ffn_parts = (
        lax.psum(ffn_parts[0].astype(jnp.bfloat16), ("seq", "ctx")).astype(jnp.float32),
        lax.psum(ffn_parts[1].astype(jnp.bfloat16), ("seq", "ctx")).astype(jnp.float32),
        lax.psum(ffn_parts[2].astype(jnp.bfloat16), ("seq", "ctx")).astype(jnp.float32),
    )
    grad_y = grad_middle.astype(jnp.bfloat16)
    grad_output_w = outer_sum(mixed_b, grad_y)
    grad_mixed = (
        lax.dot_general(
            grad_y, output_w, (((1,), (1,)), ((), ())), preferred_element_type=jnp.float32
        )
        .astype(jnp.bfloat16)
        .reshape(groups, block_rows, inner_width)
    )
    row_products = jnp.transpose(
        jnp.sum(split_heads(grad_mixed.astype(jnp.float32), head_count) * mixed, axis=-1), (0, 2, 1)
    )
    table_zero = jnp.zeros(table_b.shape, jnp.float32)
    seq_rows = block_rows * lax.axis_size("ctx")
    whole_zero = jnp.zeros((groups, seq_rows, inner_width), jnp.float32)
    start_back = (
        jnp.zeros((groups, block_rows, inner_width), jnp.float32),
        whole_zero,
        whole_zero,
        table_zero,
    )
    keys_key_piece = lax.all_gather(key_block, "ctx", axis=1, tiled=True)
    keys_value_portion = lax.all_gather(value_block, "ctx", axis=1, tiled=True)
    piece_rows = keys_key_piece.shape[1]
    keys_step_rows = math.gcd(piece_rows, block_rows)

    def keys_inner_step(block_index, state):
        query_total, key_total, value_total, table_total = state
        offset = block_index * keys_step_rows
        key_part = lax.dynamic_slice_in_dim(keys_key_piece, offset, keys_step_rows, 1)
        value_part = lax.dynamic_slice_in_dim(keys_value_portion, offset, keys_step_rows, 1)
        key_places = lax.dynamic_slice_in_dim(positions, offset, keys_step_rows, 1)
        grad_q, grad_k, grad_v, grad_t = pair_grads(
            queries,
            grad_mixed,
            logsum,
            row_products,
            query_positions,
            key_part,
            value_part,
            key_places,
            table_b,
        )
        return (
            query_total + grad_q,
            add_rows(key_total, offset, grad_k),
            add_rows(value_total, offset, grad_v),
            table_total + grad_t,
        )

    grad_query, key_whole, value_whole, grad_table = lax.fori_loop(
        0, piece_rows // keys_step_rows, keys_inner_step, start_back
    )
    grad_key, grad_value = (
        lax.psum_scatter(
            key_whole.astype(jnp.bfloat16), "ctx", scatter_dimension=1, tiled=True
        ).astype(jnp.float32),
        lax.psum_scatter(
            value_whole.astype(jnp.bfloat16), "ctx", scatter_dimension=1, tiled=True
        ).astype(jnp.float32),
    )
    query_b = grad_query.reshape(tokens, inner_width).astype(jnp.bfloat16)
    key_b = grad_key.reshape(tokens, inner_width).astype(jnp.bfloat16)
    value_b = grad_value.reshape(tokens, inner_width).astype(jnp.bfloat16)
    grad_query_w = outer_sum(normed, query_b)
    grad_key_w = outer_sum(normed, key_b)
    grad_value_w = outer_sum(normed, value_b)
    contract = (((1,), (1,)), ((), ()))
    grad_normed = lax.dot_general(query_b, query_w, contract, preferred_element_type=jnp.float32)
    grad_normed = grad_normed + lax.dot_general(
        key_b, key_w, contract, preferred_element_type=jnp.float32
    )
    grad_normed = grad_normed + lax.dot_general(
        value_b, value_w, contract, preferred_element_type=jnp.float32
    )
    first_pull = jax.vjp(rms_norm, flat_inputs, gain_one_f)[1]
    grad_from_first, grad_gain_one = first_pull(grad_normed)
    input_grad = (grad_middle + grad_from_first).reshape(inputs.shape)
    attn_parts = (
        lax.psum_scatter(
            grad_query_w.astype(jnp.bfloat16), "fsdp", scatter_dimension=0, tiled=True
        ).astype(jnp.float32),
        lax.psum_scatter(
            grad_key_w.astype(jnp.bfloat16), "fsdp", scatter_dimension=0, tiled=True
        ).astype(jnp.float32),
        lax.psum_scatter(
            grad_value_w.astype(jnp.bfloat16), "fsdp", scatter_dimension=0, tiled=True
        ).astype(jnp.float32),
        lax.psum_scatter(
            grad_output_w.astype(jnp.bfloat16), "fsdp", scatter_dimension=1, tiled=True
        ).astype(jnp.float32),
        lax.psum_scatter(
            grad_gain_one.astype(jnp.bfloat16), "fsdp", scatter_dimension=0, tiled=True
        ).astype(jnp.float32),
        lax.psum_scatter(
            grad_table.astype(jnp.bfloat16), "fsdp", scatter_dimension=0, tiled=True
        ).astype(jnp.float32),
    )
    attn_parts = (
        lax.psum(attn_parts[0].astype(jnp.bfloat16), ("seq", "ctx")).astype(jnp.float32),
        lax.psum(attn_parts[1].astype(jnp.bfloat16), ("seq", "ctx")).astype(jnp.float32),
        lax.psum(attn_parts[2].astype(jnp.bfloat16), ("seq", "ctx")).astype(jnp.float32),
        lax.psum(attn_parts[3].astype(jnp.bfloat16), ("seq", "ctx")).astype(jnp.float32),
        lax.psum(attn_parts[4].astype(jnp.bfloat16), ("seq", "ctx")).astype(jnp.float32),
        lax.psum(attn_parts[5].astype(jnp.bfloat16), ("seq", "ctx")).astype(jnp.float32),
    )
    return (
        output,
        input_grad,
        attn_parts[0],
        attn_parts[1],
        attn_parts[2],
        attn_parts[3],
        attn_parts[4],
        attn_parts[5],
        ffn_parts[0],
        ffn_parts[1],
        ffn_parts[2],
    )


def solution(mesh):
    in_specs = (
        P(("seq", "fsdp"), "ctx", None),
        P(("seq", "fsdp"), None),
        P("fsdp", None),
        P("fsdp", None),
        P("fsdp", None),
        P(None, "fsdp"),
        P("fsdp"),
        P("fsdp", None),
        P("fsdp", None),
        P(None, "fsdp"),
        P("fsdp"),
        P(("seq", "fsdp"), "ctx", None),
    )
    out_specs = (
        P(("seq", "fsdp"), "ctx", None),
        P(("seq", "fsdp"), "ctx", None),
        P("fsdp", None),
        P("fsdp", None),
        P("fsdp", None),
        P(None, "fsdp"),
        P("fsdp"),
        P("fsdp", None),
        P("fsdp", None),
        P(None, "fsdp"),
        P("fsdp"),
    )
    fits = mesh.shape["seq"] == 2 and mesh.shape["ctx"] == 4 and mesh.shape["fsdp"] == 4
    per_device = fast_device if fits else general_device
    return jax.shard_map(
        per_device, mesh=mesh, in_specs=in_specs, out_specs=out_specs, check_vma=False
    )
```

```python
import functools
import math

import jax
import jax.numpy as jnp
from jax import lax
from jax.experimental import pallas as pl
from jax.experimental.pallas import tpu as pltpu
from jax.sharding import PartitionSpec as P

MESH = pl.DeviceIdType.MESH
F32 = jnp.float32
BF = jnp.bfloat16
EPS = 1e-06
BORDERS = (12, 16, 23, 32, 46, 64, 91)
LOG2E = math.log2(math.e)
T = 128


def dot_nn(a, b):
    return jnp.dot(a, b, preferred_element_type=F32)


def dot_nt(a, b):
    return lax.dot_general(a, b, (((1,), (1,)), ((), ())), preferred_element_type=F32)


def dot_tn(a, b):
    return lax.dot_general(a, b, (((0,), (0,)), ((), ())), preferred_element_type=F32)


def bucket_of(offset):
    magnitude = jnp.abs(offset)
    logbins = jnp.full_like(magnitude, 8)
    for border in BORDERS:
        logbins = logbins + jnp.where(magnitude >= border, 1, 0)
    return jnp.where(magnitude < 8, magnitude, logbins) + jnp.where(offset > 0, 16, 0)


def pick(values, index):
    return jnp.take_along_axis(values, index, axis=1, mode="promise_in_bounds")


class Place:
    def __init__(self, z_count):
        self.y = lax.axis_index("seq")
        self.ctx = lax.axis_index("ctx")
        self.z = lax.axis_index("fsdp")
        self.x = self.ctx // 2
        self.core = self.ctx % 2
        self.col = self.y * 2 + self.x
        self.z_count = z_count
        self.sib = (self.y, self.x * 2 + 1 - self.core, self.z)
        self.xn = (self.y, (1 - self.x) * 2 + self.core, self.z)
        self.yn = (1 - self.y, self.ctx, self.z)

    def zn(self, d):
        return (self.y, self.ctx, lax.rem(self.z + d, self.z_count))


def remote(src, dst, send, recv, device):
    return pltpu.make_async_remote_copy(
        src_ref=src, dst_ref=dst, send_sem=send, recv_sem=recv, device_id=device, device_id_type=MESH
    )


class Gather:
    def __init__(self, w, ssem, rsem, slot, lo, mid, hi, here, shard):
        self.w, self.ssem, self.rsem, self.slot = w, ssem, rsem, slot
        self.lo, self.mid, self.hi = lo, mid, hi
        self.here, self.shard, self.piece = here, shard, shard // 4

    def view(self, z, col, lo, hi):
        if self.mid is None:
            return self.w.at[pl.ds(pl.multiple_of(z * self.shard, 16), self.shard), pl.ds(lo, hi - lo)]
        first = pl.multiple_of(z * self.shard + col * self.piece, 16)
        return self.w.at[pl.ds(first, self.piece), pl.ds(lo, hi - lo)]

    def copy(self, kind, d, arriving):
        p = self.here
        zs = lax.rem(p.z + p.z_count - d, p.z_count)
        col_x, col_y, col_d = p.y * 2 + 1 - p.x, (1 - p.y) * 2 + p.x, (1 - p.y) * 2 + 1 - p.x
        index = kind * 3 + d - 1
        send, recv = self.ssem.at[self.slot, index], self.rsem.at[self.slot, index]
        if kind == 0:
            ref = self.view(zs if arriving else p.z, p.col, self.lo, self.hi)
            return remote(ref, ref, send, recv, p.zn(d))
        if kind == 1:
            ref = self.view(zs, col_x if arriving else p.col, self.lo, self.hi)
            return remote(ref, ref, send, recv, p.xn)
        if kind == 2:
            ref = self.view(zs, col_y if arriving else p.col, self.lo, self.hi)
            return remote(ref, ref, send, recv, p.yn)
        if kind == 3:
            ref = self.view(zs, col_d if arriving else col_x, self.lo, self.mid)
            return remote(ref, ref, send, recv, p.yn)
        ref = self.view(zs, col_d if arriving else col_y, self.mid, self.hi)
        return remote(ref, ref, send, recv, p.xn)

    def start(self):
        for d in (1, 3, 2):
            self.copy(0, d, False).start()

    def pass_z(self):
        for d in (1, 3, 2):
            self.copy(0, d, True).wait_recv()
            self.copy(1, d, False).start()
            self.copy(2, d, False).start()

    def pass_plane(self):
        for d in (1, 3, 2):
            self.copy(1, d, True).wait_recv()
            self.copy(3, d, False).start()
            self.copy(2, d, True).wait_recv()
            self.copy(4, d, False).start()

    def finish(self):
        for d in (1, 3, 2):
            if self.mid is None:
                self.copy(0, d, True).wait_recv()
            else:
                self.copy(3, d, True).wait_recv()
                self.copy(4, d, True).wait_recv()

    def drain(self):
        for kind in range(1 if self.mid is None else 5):
            for d in (1, 3, 2):
                self.copy(kind, d, False).wait_send()


class Swap:
    def __init__(self, source, whole, ssem, rsem, lsem, here, rows):
        self.source, self.whole, self.ssem, self.rsem, self.lsem = source, whole, ssem, rsem, lsem
        self.here, self.rows = here, rows

    def block(self, ctx):
        return self.whole.at[pl.ds(pl.multiple_of(ctx * self.rows, 16), self.rows)]

    def own(self):
        return pltpu.make_async_copy(self.source.at[self.here.x], self.block(self.here.ctx), self.lsem)

    def over(self, arriving):
        p = self.here
        ctx = (1 - p.x) * 2 + p.core if arriving else p.ctx
        return remote(self.source.at[1 - p.x], self.block(ctx), self.ssem.at[0], self.rsem.at[0], p.xn)

    def pair(self, arriving):
        p = self.here
        ctx = p.x * 2 + 1 - p.core if arriving else p.ctx
        return remote(self.source.at[p.x], self.block(ctx), self.ssem.at[1], self.rsem.at[1], p.sib)

    def forward(self, arriving):
        p = self.here
        ctx = (1 - p.x) * 2 + (1 - p.core if arriving else p.core)
        return remote(self.block(ctx), self.block(ctx), self.ssem.at[2], self.rsem.at[2], p.sib)

    def start(self):
        self.over(False).start()
        self.own().start()
        self.pair(False).start()

    def relay(self):
        self.over(True).wait_recv()
        self.forward(False).start()

    def finish(self):
        self.own().wait()
        self.pair(True).wait_recv()
        self.forward(True).wait_recv()

    def drain(self):
        self.over(False).wait_send()
        self.pair(False).wait_send()
        self.forward(False).wait_send()


def enter(partners):
    barrier = pltpu.get_barrier_semaphore()
    for partner in partners:
        pl.semaphore_signal(barrier, inc=1, device_id=partner, device_id_type=MESH)
    pl.semaphore_wait(barrier, len(partners))


class Reduce:
    def __init__(self, g, r1, r2, r3, r1z, r2z, rz, fin, gfin, ssem, rsem, lsem, here, z_first):
        self.g, self.r3, self.rz, self.fin, self.gfin = g, r3, rz, fin, gfin
        self.ones, self.twos = (r1z, r1), (r2z, r2)
        self.ssem, self.rsem, self.lsem, self.here, self.z_first = ssem, rsem, lsem, here, z_first
        self.width = g.shape[-1]
        self.lo = pl.ds(0, self.width // 2)
        self.hi = pl.ds(self.width // 2, self.width // 2)
        self.piece = g.shape[4]

    def rows_z(self, c):
        return pl.ds(self.here.z, 1) if c < self.z_first else pl.ds(0, self.here.z_count)

    def count(self, c):
        return 1 if c < self.z_first else self.here.z_count

    def r1(self, c):
        return self.ones[0].at[c] if c < self.z_first else self.ones[1].at[c - self.z_first]

    def r2(self, c):
        return self.twos[0].at[c] if c < self.z_first else self.twos[1].at[c - self.z_first]

    def link(self, c, index, src, dst, device):
        return remote(src, dst, self.ssem.at[c, index], self.rsem.at[c, index], device)

    def x1(self, c):
        p = self.here
        return self.link(c, 0, self.g.at[c, 1 - p.x, :, self.rows_z(c), :, self.lo], self.r1(c).at[0], p.xn)

    def y1(self, c):
        p = self.here
        return self.link(c, 1, self.g.at[c, :, 1 - p.y, self.rows_z(c), :, self.hi], self.r1(c).at[1], p.yn)

    def x2(self, c):
        p = self.here
        return self.link(c, 2, self.g.at[c, p.x, 1 - p.y, self.rows_z(c), :, self.lo], self.r2(c).at[0], p.yn)

    def y2(self, c):
        p = self.here
        return self.link(c, 3, self.g.at[c, 1 - p.x, p.y, self.rows_z(c), :, self.hi], self.r2(c).at[1], p.xn)

    def z1(self, c, d):
        p = self.here
        to = lax.rem(p.z + d, p.z_count)
        if c < self.z_first:
            return self.link(c, 3 + d, self.g.at[c, :, :, to], self.rz.at[c, d - 1], p.zn(d))
        return self.link(c, 3 + d, self.g.at[c, p.x, p.y, to], self.r3.at[c - self.z_first, d - 1], p.zn(d))

    def over_x(self, c, arriving):
        p = self.here
        col = p.y * 2 + 1 - p.x if arriving else p.col
        return self.link(c, 7, self.fin.at[c], self.gfin.at[p.core, c, col], p.xn)

    def over_y(self, c, arriving):
        p = self.here
        ref = self.gfin.at[p.core, c, pl.ds((1 - p.y if arriving else p.y) * 2, 2)]
        return self.link(c, 8, ref, ref, p.yn)

    def keep(self, c):
        return pltpu.make_async_copy(self.fin.at[c], self.gfin.at[self.here.core, c, self.here.col], self.lsem.at[c])

    def pair(self, c, arriving):
        core = 1 - self.here.core if arriving else self.here.core
        return self.link(c, 9, self.gfin.at[core, c], self.gfin.at[core, c], self.here.sib)

    def start(self, c):
        if c < self.z_first:
            for d in (1, 3, 2):
                self.z1(c, d).start()
        else:
            self.plane(c)

    def gathered_z(self, c):
        p = self.here
        for d in (1, 3, 2):
            self.z1(c, d).wait_recv()
        for x in range(2):
            for y in range(2):
                total = self.g[c, x, y, p.z].astype(F32)
                for d in range(3):
                    total = total + self.rz[c, d, x, y].astype(F32)
                self.g[c, x, y, p.z] = total.astype(BF)
        self.plane(c)

    def plane(self, c):
        self.x1(c).start()
        self.y1(c).start()

    def second(self, c):
        p = self.here
        h = self.width // 2

        def zi(k):
            return p.z if c < self.z_first else k

        self.x1(c).wait_recv()

        def add_x(k, carry):
            for y in range(2):
                self.g[c, p.x, y, zi(k), :, :h] = (
                    self.g[c, p.x, y, zi(k), :, :h].astype(F32) + self.r1(c)[0, y, k].astype(F32)
                ).astype(BF)
            return carry

        lax.fori_loop(0, self.count(c), add_x, 0)
        self.x2(c).start()
        self.y1(c).wait_recv()

        def add_y(k, carry):
            for x in range(2):
                self.g[c, x, p.y, zi(k), :, h:] = (
                    self.g[c, x, p.y, zi(k), :, h:].astype(F32) + self.r1(c)[1, x, k].astype(F32)
                ).astype(BF)
            return carry

        lax.fori_loop(0, self.count(c), add_y, 0)
        self.y2(c).start()

    def third(self, c):
        p = self.here
        h = self.width // 2
        self.x2(c).wait_recv()
        self.y2(c).wait_recv()
        if c < self.z_first:
            self.fin[c, :, :h] = (self.g[c, p.x, p.y, p.z, :, :h].astype(F32) + self.r2(c)[0, 0].astype(F32)).astype(BF)
            self.fin[c, :, h:] = (self.g[c, p.x, p.y, p.z, :, h:].astype(F32) + self.r2(c)[1, 0].astype(F32)).astype(BF)
            self.publish(c)
            return

        def add(k, carry):
            self.g[c, p.x, p.y, k, :, :h] = (
                self.g[c, p.x, p.y, k, :, :h].astype(F32) + self.r2(c)[0, k].astype(F32)
            ).astype(BF)
            self.g[c, p.x, p.y, k, :, h:] = (
                self.g[c, p.x, p.y, k, :, h:].astype(F32) + self.r2(c)[1, k].astype(F32)
            ).astype(BF)
            return carry

        lax.fori_loop(0, p.z_count, add, 0)
        for d in (1, 3, 2):
            self.z1(c, d).start()

    def fourth(self, c):
        if c < self.z_first:
            return
        p = self.here
        for d in (1, 3, 2):
            self.z1(c, d).wait_recv()
        total = self.g[c, p.x, p.y, p.z].astype(F32)
        for d in range(3):
            total = total + self.r3[c - self.z_first, d].astype(F32)
        self.fin[c] = total.astype(BF)
        self.publish(c)

    def publish(self, c):
        self.over_x(c, False).start()
        self.keep(c).start()

    def fifth(self, c):
        self.over_x(c, True).wait_recv()
        self.keep(c).wait()
        self.over_y(c, False).start()

    def sixth(self, c):
        self.over_y(c, True).wait_recv()
        self.pair(c, False).start()

    def last(self, c):
        self.pair(c, True).wait_recv()
        for copy in (self.x1(c), self.y1(c), self.x2(c), self.y2(c), self.over_x(c, False), self.over_y(c, False), self.pair(c, False)):
            copy.wait_send()
        for d in (1, 3, 2):
            self.z1(c, d).wait_send()


def edges():
    starts, buckets = [], [15]
    lows = (8,) + BORDERS
    for b in range(14, 7, -1):
        starts.append(1 - lows[b - 7])
        buckets.append(b)
    for n in range(7, -1, -1):
        starts.append(-n)
        buckets.append(n)
    for n in range(1, 8):
        starts.append(n)
        buckets.append(16 + n)
    for b in range(8, 16):
        starts.append(lows[b - 8])
        buckets.append(16 + b)
    return starts, buckets


def gelu_parts(v):
    c0 = math.sqrt(2.0 / math.pi)
    sq = v * v
    th = jnp.tanh(v * (c0 + (c0 * 0.044715) * sq))
    half = 0.5 + 0.5 * th
    slope = half + (0.5 * v) * (1.0 - th * th) * (c0 + (3.0 * 0.044715 * c0) * sq)
    return v * half, slope


def layer_kernel(
    inputs, positions, wq, wk, wv, wo_t, win, wout_t, extra_in, cotangent,
    out_ref, igrad_ref, gfin, evec_out, probs_out,
    w, x_all, cot_all, extra, n_t, turned, q, k, v, mixed, linv, table, pool, bound, ka, va, p_slot,
    y_in, t_in, o_send, o_in, slope, gmid, dk_acc, dv_acc, cat, stage, ig_in,
    hist, far_sum, gain_acc, e_src, e_in,
    g, r1, r2, r3, r1z, r2z, rz, fin,
    ssem, rsem, swap_s, swap_r, cot_s, cot_r, e_s, e_r, lsem, psem, y_s, y_r, t_s, t_r, o_s, o_r, out_s, out_r, u_s, u_r, ev_s, ev_r,
    g_s, g_r, g_l, osem,
):
    here = Place(lax.axis_size("fsdp"))
    p = here
    D, INNER = w.shape[0], wo_t.shape[1]
    half = INNER // 2
    ffh = win.shape[1] // 2
    shard = wq.shape[0]
    piece = shard // 4
    R = x_all.shape[0]
    heads = half // 64
    nt = R // T
    active = pool.at[:, pl.ds(0, ffh)]
    y_own = pool.at[:, pl.ds(ffh, D)]
    t_own = stage
    own_rows = pl.ds(pl.multiple_of(p.z * shard, 16), shard)
    half_cols = pl.ds(pl.multiple_of(p.core * half, 128), half)
    ff_cols = pl.ds(pl.multiple_of(p.core * ffh, 128), ffh)
    c_o, c_in, c_out, c_end = 3 * half, 4 * half, 4 * half + ffh, 4 * half + 2 * ffh

    loads = [
        pltpu.make_async_copy(wq.at[:, half_cols], w.at[own_rows, pl.ds(0, half)], lsem.at[0]),
        pltpu.make_async_copy(wk.at[:, half_cols], w.at[own_rows, pl.ds(half, half)], lsem.at[1]),
        pltpu.make_async_copy(wv.at[:, half_cols], w.at[own_rows, pl.ds(2 * half, half)], lsem.at[2]),
        pltpu.make_async_copy(win.at[:, ff_cols], w.at[own_rows, pl.ds(c_in, ffh)], lsem.at[3]),
        pltpu.make_async_copy(wo_t.at[:, half_cols], w.at[own_rows, pl.ds(c_o, half)], lsem.at[4]),
        pltpu.make_async_copy(wout_t.at[:, ff_cols], w.at[own_rows, pl.ds(c_out, ffh)], lsem.at[5]),
        pltpu.make_async_copy(extra_in, extra.at[own_rows], lsem.at[6]),
    ]
    for load in loads:
        load.start()
    enter([p.sib, p.xn, p.yn, p.zn(1), p.zn(2), p.zn(3)])
    swap = Swap(inputs, x_all, swap_s, swap_r, lsem.at[7], here, inputs.shape[1])
    swap.start()
    cot_swap = Swap(cotangent, cot_all, cot_s, cot_r, lsem.at[8], here, inputs.shape[1])

    def extra_copy(d, arriving):
        zs = lax.rem(p.z + p.z_count - d, p.z_count) if arriving else p.z
        ref = extra.at[pl.ds(pl.multiple_of(zs * shard, 16), shard)]
        return remote(ref, ref, e_s.at[d - 1], e_r.at[d - 1], p.zn(d))

    loads[6].wait()
    for d in (1, 3, 2):
        extra_copy(d, False).start()
    tracks = [(n * half, n * half + 2 * T, (n + 1) * half) for n in range(3)] + [(c_o, c_o + 2 * T, c_in)]
    tracks += [(lo, lo + 3 * T, lo + 4 * T) for lo in range(c_in, c_end - 4 * T, 4 * T)] + [(c_end - 4 * T, None, c_end)]
    gathers = [Gather(w, ssem, rsem, n, lo, mid, hi, here, shard) for n, (lo, mid, hi) in enumerate(tracks)]
    for n in range(3):
        loads[n].wait()
        gathers[n].start()
    for n in range(3, 6):
        loads[n].wait()
    for gather in gathers[3:]:
        gather.start()

    starts, classes = edges()
    lane = lax.broadcasted_iota(jnp.int32, (1, T), 1)
    pos = positions[pl.ds(p.x, 1), :]
    band = [(a, d) for a in range(nt) for d in range(3) if 0 <= a + d - 1 < nt]
    cols = {}
    early = {
        25: [gathers[1].pass_z],
        9: [gathers[0].pass_z],
        37: [gathers[0].pass_plane],
        43: [gathers[2].pass_plane],
        42: [swap.relay],
        44: [gathers[3].pass_z, gathers[4].pass_z],
        41: [gathers[1].pass_plane],
        27: [gathers[2].pass_z],
    }

    def offsets(a, d):
        if a not in cols:
            cols[a] = jnp.broadcast_to(pos[:, a * T : (a + 1) * T], (T, T)).T
        return pos[:, (a + d - 1) * T : (a + d) * T] - cols[a]

    edge = jnp.full((1, T), -(2**20), jnp.int32)
    for j, first in enumerate(starts):
        edge = jnp.where(lane == j, first, edge)
    ranks = {}

    def ranks_of(b):
        if b not in ranks:
            offsets(b, 1)
            base = pos[:, b * T : b * T + 1]
            above = cols[b] - base
            ranks[b] = base, [
                jnp.broadcast_to(jnp.sum(jnp.where(above < lane + m * T, 1.0, 0.0), axis=0, keepdims=True), (T, T)) for m in range(2)
            ]
        return ranks[b]

    for n, (a, d) in enumerate(band):
        for step in early.get(n, ()):
            step()
        offsets(a, 1)
        base, (low, high) = ranks_of(a + d - 1)
        at = jnp.clip(cols[a] + edge - base, 0, 2 * T - 1)
        count = jnp.where(at < T, pick(low, jnp.minimum(at, T - 1)), pick(high, jnp.maximum(at - T, 0)))
        bound[a * T : (a + 1) * T, d * T : (d + 1) * T] = count.astype(jnp.int32) - 1

    for d in (1, 3, 2):
        extra_copy(d, True).wait_recv()
    buckets_per = 8
    rows = [extra[zs * shard : zs * shard + 16, :].astype(F32)[:buckets_per] for zs in range(4)]
    flat = jnp.concatenate(rows + [jnp.zeros((T - 32, T), F32)], axis=0)
    table[...] = flat.T
    gains = jnp.concatenate(
        [extra[t * T : (t + 1) * T, :].astype(F32).T[0:8] for t in range(D // T)], axis=1
    )
    gain_one, gain_two = gains[0:1], gains[1:2]
    for n, (a, d) in enumerate(band):
        for step in early.get(len(band) + n, ()):
            step()
        idx = bucket_of(offsets(a, d))
        for h in range(heads):
            tab = jnp.broadcast_to(table[pl.ds(2 + p.core * heads + h, 1), :], (T, T))
            pool[a * T : (a + 1) * T, (h * 3 + d) * T : (h * 3 + d + 1) * T] = pick(tab, idx).astype(BF)
    for step in early.get(2 * len(band), ()):
        step()

    swap.finish()
    for c in range(4):
        rows = slice(c * (R // 4), (c + 1) * (R // 4))
        xf = x_all[rows, :].astype(F32)
        scale = lax.rsqrt(jnp.mean(xf * xf, axis=1, keepdims=True) + EPS)
        stage[rows, :] = (xf * scale * gain_one).astype(BF)
        n_t[:, rows] = (xf * scale * gain_one).T.astype(BF)
    for gather in gathers[:3]:
        gather.finish()

    def project(c, carry):
        rows = pl.ds(pl.multiple_of(c * 256, 256), 256)
        for n, dest in enumerate((q, k, v)):
            out = dot_nn(stage[rows, :], w[:, n * half : (n + 1) * half]).astype(BF)
            for pair in range(half // T):
                dest[pair, rows, :] = out[:, pair * T : (pair + 1) * T]
        return carry

    lax.fori_loop(0, R // 256, project, 0)

    QT = 256
    sub = QT // T
    units = R // QT
    ahead = {
        1: [gathers[5].pass_z],
        3: [gathers[6].pass_z],
        5: [gathers[4].pass_plane],
        13: [gathers[8].pass_z],
        4: [gathers[3].pass_plane, gathers[5].pass_plane],
        6: [gathers[6].pass_plane, cot_swap.start],
        9: [gathers[7].pass_z],
    }
    for step in ahead.get(-1, ()):
        step()

    def halves(h, lanes):
        return ((lanes < 64), lanes - 64) if h == 0 else ((lanes >= 64), lanes)

    def pair_step(hp, carry):
        lane_k = lax.broadcasted_iota(jnp.int32, (R, T), 1)
        tile_k = lax.broadcasted_iota(jnp.int32, (R, T), 0) // T
        for h in range(2):
            tab = table[pl.ds(2 + p.core * heads + hp * 2 + h, 1), :]
            inside, other = halves(h, lane_k)
            far = jnp.where(tile_k < other - 1, tab[:, 15:16], jnp.where(tile_k > other + 1, tab[:, 31:32], 0.0))
            far = jnp.where(other < nt, far, 0.0)
            ka[h] = jnp.where(inside, k[hp].astype(F32), far).astype(BF)
            va[h] = jnp.where(inside, v[hp].astype(F32), 1.0).astype(BF)
        lane_q = lax.broadcasted_iota(jnp.int32, (QT, T), 1)
        tile_q = lax.broadcasted_iota(jnp.int32, (QT, T), 0) // T
        for qi in range(units):
            for trip in range(heads // 2):
                if trip * units + qi in ahead:
                    pl.when(hp == trip)(lambda todo=ahead[trip * units + qi]: [step() for step in todo] and None)
            store = pltpu.make_async_copy(p_slot.at[qi % 2], probs_out.at[hp, :, pl.ds(qi * QT, QT)], psem.at[qi % 2])
            if qi < 2:
                pl.when(hp > 0)(store.wait)
            else:
                store.wait()
            rows = slice(qi * QT, (qi + 1) * QT)
            scores = []
            for h in range(2):
                inside, other = halves(h, lane_q)
                hot = jnp.where(other == tile_q + qi * sub, 1.0, 0.0)
                qm = jnp.where(inside, q[hp, rows, :].astype(F32), hot).astype(BF)
                scores.append(dot_nt(qm, ka[h]))
            mixes = []
            for h in range(2):
                strips = []
                for si in range(sub):
                    a = qi * sub + si
                    st = scores[h][si * T : (si + 1) * T]
                    lo, hi = max(a - 1, 0), min(a + 2, nt)
                    parts = [st[:, : lo * T]] if lo > 0 else []
                    lanes = pl.ds(pl.multiple_of((hp * 2 + h) * 3 * T + (lo - a + 1) * T, T), (hi - lo) * T)
                    near = pool[a * T : (a + 1) * T, lanes]
                    parts.append(st[:, lo * T : hi * T] + near.astype(F32))
                    if hi < nt:
                        parts.append(st[:, hi * T :])
                    strips.append(jnp.concatenate(parts, axis=1))
                sc = jnp.concatenate(strips, axis=0)
                m = jnp.max(sc, axis=1, keepdims=True)
                pb = jnp.exp2((sc - m) * LOG2E).astype(BF)
                p_slot[qi % 2, h] = pb
                mixes.append(dot_nn(pb, va[h]))
            store.start()
            o = jnp.where(lane < 64, mixes[0], mixes[1])
            total = pltpu.roll(jnp.where(lane < 64, mixes[1], mixes[0]), 64, 1)
            inv = 1.0 / total
            mixed[hp, rows, :] = (o * inv).astype(BF)
            linv[hp, rows, :] = inv
        return carry

    lax.fori_loop(0, heads // 2, pair_step, 0)
    for slot in range(2):
        pltpu.make_async_copy(p_slot.at[slot], probs_out.at[0, :, pl.ds(0, QT)], psem.at[slot]).wait()

    B = 256
    blocks = R // B
    FW = 512
    for step in ahead.get(3 * units, ()):
        step()
    for gather in gathers[3:7]:
        gather.finish()

    def y_copy(i, arriving=False):
        rows = pl.ds(pl.multiple_of(i * B, B), B)
        return remote(y_own.at[rows], y_in.at[rows], y_s.at[i], y_r.at[i], p.sib)

    def t_copy(i):
        rows = pl.ds(pl.multiple_of(i * B, B), B)
        return remote(t_own.at[rows], t_in.at[rows], t_s.at[i], t_r.at[i], p.sib)

    def o_copy(n):
        return remote(o_send.at[n], o_in.at[n], o_s.at[n], o_r.at[n], p.sib)

    def project_out(i, carry):
        rows = pl.ds(pl.multiple_of(i * B, B), B)
        mx = jnp.concatenate([mixed[pair, rows, :] for pair in range(half // T)], axis=1)
        y_own[rows, :] = dot_nt(mx, w[:, c_o : c_o + half]).astype(BF)
        y_copy(i).start()
        return carry

    lax.fori_loop(0, blocks, project_out, 0)
    for step in ahead.get(3 * units + 1, ()):
        step()

    def middle_of(rows):
        mid = x_all[rows, :].astype(F32) + (y_own[rows, :].astype(F32) + y_in[rows, :].astype(F32))
        return mid, lax.rsqrt(jnp.mean(mid * mid, axis=1, keepdims=True) + EPS)

    red = Reduce(g, r1, r2, r3, r1z, r2z, rz, fin, gfin, g_s, g_r, g_l, here, 2)
    between = {
        1: [gathers[7].pass_plane],
        3: [gathers[8].pass_plane],
        0: [cot_swap.relay],
    }

    def during(i, base, table):
        for n in range(blocks):
            if base + n in table:
                pl.when(i == n)(lambda todo=table[base + n]: [step() for step in todo] and None)

    def ffn_in(i, carry):
        rows = pl.ds(pl.multiple_of(i * B, B), B)
        y_copy(i).wait_recv()
        mid, scale = middle_of(rows)
        n2f = mid * scale * gain_two
        n2 = n2f.astype(BF)
        stage[rows, :] = n2
        for j in range(ffh // FW):
            hidden = dot_nn(n2, w[:, c_in + j * FW : c_in + (j + 1) * FW])
            act, slo = gelu_parts(hidden)
            active[rows, j * FW : (j + 1) * FW] = act.astype(BF)
            slope[rows, j * FW : (j + 1) * FW] = slo.astype(BF)
        during(i, 0, between)
        return carry

    lax.fori_loop(0, blocks, ffn_in, 0)
    cot_swap.finish()
    for i in range(blocks):
        rows = slice(i * B, (i + 1) * B)
        turned[:, rows] = cot_all[rows, :].astype(F32).T.astype(BF)


    def keep_pieces(c, lo, left, right):
        for n in range(0, right.shape[1], 2 * T):
            value = dot_nn(left, right[:, n : n + 2 * T])
            for zs in range(p.z_count):
                for col in range(4):
                    first_row = zs * shard + col * piece
                    g[c, col % 2, col // 2, zs, :, lo + n : lo + n + value.shape[1]] = value[first_row : first_row + piece].astype(BF)

    for c in range(ffh // FW):
        keep_pieces(c, 0, turned[...], active[:, c * FW : (c + 1) * FW])
        red.start(c)
        for step in between.get(4 + c, ()):
            step()
    for i in range(blocks):
        rows = slice(i * B, (i + 1) * B)
        turned[:, rows] = stage[rows, :].astype(F32).T.astype(BF)
    for gather in gathers[7:]:
        gather.finish()
    later = {
        2: [functools.partial(red.second, 2)],
        4: [functools.partial(red.third, 2)],
        10: [functools.partial(red.gathered_z, 0)],
    }

    def ffn_back(i, carry):
        rows = pl.ds(pl.multiple_of(i * B, B), B)
        cot = cot_all[rows, :]
        for j in range(ffh // FW):
            grad = dot_nn(cot, w[:, c_out + j * FW : c_out + (j + 1) * FW])
            cols = slice(j * FW, (j + 1) * FW)
            slope[rows, cols] = (grad * slope[rows, cols].astype(F32)).astype(BF)
        t_own[rows, :] = dot_nt(slope[rows, :], w[:, c_in:c_out]).astype(BF)
        t_copy(i).start()
        o = dot_nt(active[rows, :], w[:, c_out:c_end])
        n = i // 2

        @pl.when(i % 2 == p.core)
        def _():
            gmid[n] = o

        @pl.when(i % 2 != p.core)
        def _():
            o_send[n] = o.astype(BF)
            o_copy(n).start()

        during(i, 0, later)
        return carry

    lax.fori_loop(0, blocks, ffn_back, 0)
    for c in range(ffh // FW):
        keep_pieces(3 + c, 0, turned[...], slope[:, c * FW : (c + 1) * FW])
        for step in later.get(4 + c, ()):
            step()
        red.start(3 + c)

    gain_acc[...] = jnp.zeros_like(gain_acc)

    def back_middle(i, carry):
        rows = pl.ds(pl.multiple_of(i * B, B), B)
        t_copy(i).wait_recv()
        mid, scale = middle_of(rows)
        t = t_own[rows, :].astype(F32) + t_in[rows, :].astype(F32)
        tg = t * gain_two
        dot = jnp.mean(tg * mid, axis=1, keepdims=True)
        gm = cot_all[rows, :].astype(F32) + scale * tg - (scale * scale * scale * dot) * mid
        gy = gm.astype(BF)
        turned[:, rows] = gm.T.astype(BF)
        grad = dot_nn(gy, w[:, c_o : c_o + half])
        for pair in range(half // T):
            slope[rows, D + pair * T : D + (pair + 1) * T] = (grad[:, pair * T : (pair + 1) * T] * linv[pair, rows, :]).astype(BF)
        n = i // 2

        @pl.when(i % 2 == p.core)
        def _():
            gain_acc[1:2, :] += jnp.sum(t * mid * scale, axis=0, keepdims=True)
            o_copy(n).wait_recv()
            slope[pl.ds(pl.multiple_of(n * B, B), B), :D] = (mid + gmid[n] + o_in[n].astype(F32)).astype(BF)
            gmid[n] = gm

        during(i, 7, later)
        return carry

    lax.fori_loop(0, blocks, back_middle, 0)
    out_own = pltpu.make_async_copy(slope.at[pl.ds(pl.multiple_of(p.x * B, B), B), pl.ds(0, D)], out_ref.at[p.x], osem.at[0])
    out_over = remote(slope.at[pl.ds(pl.multiple_of((1 - p.x) * B, B), B), pl.ds(0, D)], out_ref.at[p.x], out_s.at[0], out_r.at[0], p.xn)
    out_there = remote(slope.at[pl.ds(pl.multiple_of((1 - p.x) * B, B), B), pl.ds(0, D)], out_ref.at[1 - p.x], out_s.at[0], out_r.at[0], p.xn)
    out_own.start()
    out_over.start()

    hist[...] = jnp.zeros_like(hist)
    far_sum[...] = jnp.zeros_like(far_sum)
    row_i = lax.broadcasted_iota(jnp.int32, (2 * T, 2 * T), 0)
    col_i = lax.broadcasted_iota(jnp.int32, (2 * T, 2 * T), 1)
    upto_incl = jnp.where(jnp.logical_and(row_i <= col_i, row_i // T == col_i // T), 1.0, 0.0).astype(BF)
    skip_left, skip_right = 96, 32

    def p_load(hp, qi):
        return pltpu.make_async_copy(probs_out.at[hp, :, pl.ds(qi * QT, QT)], p_slot.at[qi % 2], psem.at[qi % 2])

    p_load(0, 0).start()
    stages = {
        1: [functools.partial(red.second, 4)],
        9: [functools.partial(red.second, 5), functools.partial(red.gathered_z, 1)],
        11: [functools.partial(red.fourth, 2), functools.partial(red.second, 3), functools.partial(red.second, 7), functools.partial(red.second, 0), functools.partial(red.third, 4), functools.partial(red.second, 6)],
    }

    def lanes_of(m, hp):
        return pl.ds(pl.multiple_of(m * half + hp * T, T), T)

    def pair_back(hp, carry):
        lane_k = lax.broadcasted_iota(jnp.int32, (R, T), 1)
        tile_k = lax.broadcasted_iota(jnp.int32, (R, T), 0) // T
        for h in range(2):
            inside = (lane_k < 64) if h == 0 else (lane_k >= 64)
            other = lane_k - 64 if h == 0 else lane_k
            va[h] = jnp.where(inside, v[hp].astype(F32), jnp.where(other < 3, 1.0, 0.0)).astype(BF)
            ka[h] = jnp.where(inside, k[hp].astype(F32), jnp.where(other == tile_k, 1.0, 0.0)).astype(BF)
        dk_acc[...] = jnp.zeros_like(dk_acc)
        dv_acc[...] = jnp.zeros_like(dv_acc)
        lane_q = lax.broadcasted_iota(jnp.int32, (QT, T), 1)
        tile_q = lax.broadcasted_iota(jnp.int32, (QT, T), 0) // T
        for qi in range(units):
            for trip in range(heads // 2):
                if trip * units + qi in stages:
                    pl.when(hp == trip)(lambda todo=stages[trip * units + qi]: [step() for step in todo] and None)
            rows = slice(qi * QT, (qi + 1) * QT)
            p_load(hp, qi).wait()
            if qi + 1 < units:
                p_load(hp, qi + 1).start()
            else:
                pl.when(hp < heads // 2 - 1)(lambda: p_load(hp + 1, 0).start())
            do = slope[rows, pl.ds(pl.multiple_of(D + hp * T, T), T)].astype(F32)
            prod = do * mixed[hp, rows, :].astype(F32)
            qf = q[hp, rows, :].astype(F32)
            dps, dms, qms, dqs, grads = [], [], [], [], []
            for h in range(2):
                inside, other = halves(h, lane_q)
                rd = jnp.sum(jnp.where(inside, prod, 0.0), axis=1, keepdims=True)
                ra = rd.astype(BF).astype(F32)
                rb = (rd - ra).astype(BF).astype(F32)
                rc = rd - ra - rb
                dm = jnp.where(inside, do, 0.0)
                da = (dm - jnp.where(other == 0, ra, jnp.where(other == 1, rb, jnp.where(other == 2, rc, 0.0)))).astype(BF)
                dms.append(dm.astype(BF))
                qms.append(jnp.where(inside, qf, 0.0).astype(BF))
                dps.append(dot_nt(da, va[h]))
            for h in range(2):
                pb = p_slot[qi % 2, h]
                ds = (pb.astype(F32) * dps[h]).astype(BF)
                grads.append(ds)
                dqs.append(dot_nn(ds, ka[h]))
                dv_acc[...] += dot_tn(dms[h], pb)
                dk_acc[...] += dot_tn(qms[h], ds)
            cat[rows, lanes_of(0, hp)] = jnp.where(lane < 64, dqs[0], dqs[1]).astype(BF)
            in_tile = lax.broadcasted_iota(jnp.int32, (QT, T), 0) % T
            tile = tile_q + qi * sub
            for h in range(2):
                ds = grads[h]
                inside, other = halves(h, lane_q)
                spare = jnp.where(inside, 0.0, dqs[h])
                left = jnp.logical_or(other < tile - 1, jnp.logical_and(other == tile - 1, in_tile >= skip_left))
                right = jnp.logical_or(other > tile + 1, jnp.logical_and(other == tile + 1, in_tile < skip_right))
                for m, cond in enumerate((left, jnp.logical_and(right, other < nt), other < nt)):
                    far_sum[hp * 2 + h, m : m + 1, :] += jnp.sum(jnp.where(cond, spare, 0.0), axis=0, keepdims=True)
                found = jnp.zeros((8, T), F32)
                first_lane = min(max(qi * sub - 1, 0), nt - 4) * T
                sums_all = [dot_nn(ds[:, first_lane + m * 2 * T : first_lane + (m + 1) * 2 * T], upto_incl) for m in range(2)]
                for si in range(sub):
                    a = qi * sub + si
                    for d in range(3):
                        b = a + d - 1
                        if 0 <= b < nt:
                            r0, r1_ = (0, skip_left) if d == 0 else ((skip_right, T) if d == 2 else (0, T))
                            lane0 = b * T - first_lane
                            sums = sums_all[lane0 // (2 * T)][si * T + r0 : si * T + r1_, lane0 % (2 * T) : lane0 % (2 * T) + T]
                            idx = bound[a * T + r0 : a * T + r1_, d * T : (d + 1) * T]
                            got = jnp.where(idx >= 0, pick(sums, jnp.maximum(idx, 0)), 0.0)
                            found = found + jnp.sum(got.reshape((r1_ - r0) // 8, 8, T), axis=0)
                hist[hp * 2 + h] += found
        cat[:, lanes_of(1, hp)] = dk_acc[...].T.astype(BF)
        cat[:, lanes_of(2, hp)] = dv_acc[...].T.astype(BF)
        c = 6 + hp
        for m in range(3):
            keep_pieces(c, m * T, n_t[...], cat[:, lanes_of(m, hp)])
        keep_pieces(c, 3 * T, turned[...], mixed[hp])
        for trip in range(heads // 2):
            pl.when(hp == trip)(functools.partial(red.start, 6 + trip))
        return carry

    lax.fori_loop(0, heads // 2, pair_back, 0)

    def u_copy(n):
        return remote(slope.at[pl.ds((2 + n) * B, B), pl.ds(0, D)], o_in.at[2 + n], u_s.at[n], u_r.at[n], p.sib)

    for n in range(2):
        rows = pl.ds(pl.multiple_of((2 * n + 1 - p.core) * B, B), B)
        slope[(2 + n) * B : (3 + n) * B, :D] = dot_nt(cat[rows, :], w[:, :c_o]).astype(BF)
        u_copy(n).start()
    red.third(0)
    red.second(1)
    red.fifth(2)
    red.third(7)
    red.third(5)
    for n in range(2):
        rows = pl.ds(pl.multiple_of((2 * n + p.core) * B, B), B)
        t = dot_nt(cat[rows, :], w[:, :c_o])
        u_copy(n).wait_recv()
        t = t + o_in[2 + n].astype(F32)
        xf = x_all[rows, :].astype(F32)
        scale = lax.rsqrt(jnp.mean(xf * xf, axis=1, keepdims=True) + EPS)
        tg = t * gain_one
        dot = jnp.mean(tg * xf, axis=1, keepdims=True)
        gmid[n] = gmid[n] + scale * tg - (scale * scale * scale * dot) * xf
        gain_acc[0:1, :] += jnp.sum(t * xf * scale, axis=0, keepdims=True)
    ig_own = pltpu.make_async_copy(gmid.at[p.x], igrad_ref.at[p.x], osem.at[1])
    ig_own.start()
    slope[:B, D:] = gmid[1 - p.x].astype(BF)
    ig_over = remote(slope.at[pl.ds(0, B), pl.ds(D, D)], ig_in, out_s.at[1], out_r.at[1], p.xn)

    gains_rows = [gain_acc[m : m + 1, t * T : (t + 1) * T] for m in range(2) for t in range(D // T)]
    class_of = jnp.zeros((1, T), jnp.int32)
    for j, bkt in enumerate(classes):
        class_of = jnp.where(lane == bkt, j, class_of)
    used = jnp.logical_and(lane < 32, lane != 16)
    rows_h = []
    for h in range(heads):
        upto = jnp.sum(hist[h], axis=0, keepdims=True)
        sums = jnp.sum(far_sum[h], axis=1, keepdims=True)
        left, right, every = sums[0:1], sums[1:2], sums[2:3]
        near = every - left - right
        n_edges = len(starts)
        upto = jnp.where(lane < n_edges, upto, jnp.where(lane == n_edges, near, 0.0))
        below = jnp.where(lane == 0, 0.0, pltpu.roll(upto, 1, 1))
        per = upto - below + jnp.where(lane == 0, left, jnp.where(lane == n_edges, right, 0.0))
        rows_h.append(per)
    heads_rows = jnp.concatenate(rows_h + [jnp.zeros((8 - heads, T), F32)], axis=0)
    picked = jnp.take_along_axis(heads_rows, jnp.broadcast_to(class_of, (8, T)), axis=1)
    picked = jnp.where(used, picked, 0.0)[:heads]
    zero = jnp.zeros((heads, T), F32)
    first_half = jnp.where(p.core == 0, picked, zero)
    other_half = jnp.where(p.core == 0, zero, picked)
    e_src[0] = jnp.concatenate(gains_rows + [first_half, other_half], axis=0)

    def e_copy(n):
        device = (p.sib, p.xn, p.yn, p.zn(1), p.zn(2), p.zn(3))[n]
        return remote(e_src.at[min(n, 3)], e_in.at[n], ev_s.at[n], ev_r.at[n], device)

    red.third(6)
    ig_over.start()
    e_copy(0).start()
    e_copy(0).wait_recv()
    e_src[1] = e_src[0] + e_in[0]
    e_copy(1).start()
    red.fourth(4)
    red.fourth(5)
    red.sixth(2)
    red.fifth(0)
    red.third(3)
    red.second(8)
    e_copy(1).wait_recv()
    e_src[2] = e_src[1] + e_in[1]
    e_copy(2).start()
    red.fifth(4)
    red.fourth(6)
    e_copy(2).wait_recv()
    e_src[3] = e_src[2] + e_in[2]
    e_copy(3).start()
    e_copy(4).start()
    e_copy(5).start()
    red.third(1)
    red.fifth(5)
    red.third(8)
    red.fourth(7)
    red.fifth(6)
    red.fifth(1)
    red.sixth(4)
    red.fifth(7)
    red.fourth(3)
    red.sixth(0)
    red.fifth(3)
    red.fourth(8)
    red.sixth(6)
    red.fifth(8)
    red.sixth(7)
    red.sixth(1)
    red.sixth(5)
    red.sixth(3)
    red.sixth(8)
    for n in range(3, 6):
        e_copy(n).wait_recv()
    e_src[4] = e_src[3] + e_in[3] + e_in[4] + e_in[5]
    ev_out = pltpu.make_async_copy(e_src.at[4], evec_out, osem.at[2])
    ev_out.start()
    ig_over.wait_recv()
    ig_own.wait()
    gmid[0] = ig_in[...].astype(F32)
    ig_there = pltpu.make_async_copy(gmid.at[0], igrad_ref.at[1 - p.x], osem.at[1])
    ig_there.start()
    out_own.wait()
    out_there.wait_recv()
    for c in range(g.shape[0]):
        red.last(c)
    for i in range(blocks):
        y_copy(i).wait_send()
        t_copy(i).wait_send()
    for n in range(2):
        o_copy(n).wait_send()
        u_copy(n).wait_send()
    out_over.wait_send()
    ig_over.wait_send()
    for n in range(6):
        e_copy(n).wait_send()
    for gather in gathers:
        gather.drain()
    swap.drain()
    cot_swap.drain()
    for d in (1, 3, 2):
        extra_copy(d, False).wait_send()
    ev_out.wait()
    ig_there.wait()


def layer(inputs, positions, wq, wk, wv, wo_t, win, wout_t, extra_in, cotangent):
    D, INNER, FF = win.shape[0] * lax.axis_size("fsdp"), wo_t.shape[1], win.shape[1]
    half, ffh, shard = INNER // 2, FF // 2, wq.shape[0]
    B = inputs.shape[1]
    R = inputs.shape[0] * B * 2
    heads, pairs = half // 64, half // T
    width = 4 * half + 2 * ffh
    piece, FW = shard // 4, 512
    nc = width // FW
    zf = 2
    sds = jax.ShapeDtypeStruct
    any_ = pl.BlockSpec(memory_space=pl.ANY)
    vm = pl.BlockSpec(memory_space=pltpu.VMEM)
    sem = pltpu.SemaphoreType.DMA
    V = pltpu.VMEM
    return pl.pallas_call(
        layer_kernel,
        in_specs=[any_, vm] + [any_] * 8,
        out_specs=[any_] * 5,
        out_shape=[
            sds(inputs.shape, BF), sds(inputs.shape, F32), sds((2, nc, 4, piece, FW), BF), sds((24, T), F32), sds((pairs, 2, R, R), BF),
        ],
        scratch_shapes=[
            V((D, width), BF), V((R, D), BF), V((R, D), BF), V((D, T), BF), V((D, R), BF), V((D, R), BF),
            V((pairs, R, T), BF), V((pairs, R, T), BF), V((pairs, R, T), BF), V((pairs, R, T), BF), V((pairs, R, T), F32), V((T, T), F32),
            V((R, heads * 3 * T), BF), V((R, 3 * T), jnp.int32),
            V((2, R, T), BF), V((2, R, T), BF), V((2, 2, 256, R), BF),
            V((R, D), BF), V((R, D), BF), V((2, B, D), BF), V((4, B, D), BF),
            V((R, ffh), BF), V((2, B, D), F32), V((T, R), F32), V((T, R), F32),
            V((R, 3 * half), BF), V((R, D), BF), V((B, D), BF),
            V((heads, 8, T), F32), V((heads, 8, T), F32), V((8, D), F32), V((5, 24, T), F32), V((6, 24, T), F32),
            V((nc, 2, 2, 4, piece, FW), BF), V((nc - zf, 2, 2, 4, piece, FW // 2), BF), V((nc - zf, 2, 4, piece, FW // 2), BF),
            V((nc - zf, 3, piece, FW), BF), V((zf, 2, 2, 1, piece, FW // 2), BF), V((zf, 2, 1, piece, FW // 2), BF),
            V((zf, 3, 2, 2, piece, FW), BF), V((nc, piece, FW), BF),
            sem((10, 15)), sem((10, 15)), sem((3,)), sem((3,)), sem((3,)), sem((3,)), sem((3,)), sem((3,)), sem((12,)), sem((2,)),
            sem((4,)), sem((4,)), sem((4,)), sem((4,)), sem((2,)), sem((2,)), sem((2,)), sem((2,)), sem((2,)), sem((2,)), sem((6,)), sem((6,)),
            sem((nc, 10)), sem((nc, 10)), sem((nc,)), sem((3,)),
        ],
        compiler_params=pltpu.CompilerParams(collective_id=0, has_side_effects=True, vmem_limit_bytes=63 * 2**20),
        name="layer",
    )(inputs, positions, wq, wk, wv, wo_t, win, wout_t, extra_in, cotangent)


def fast_device(inputs, positions, w_query, w_key, w_value, w_output, gain_attn, rel_table, w_in, w_out, gain_ffn, cotangent):
    shard = gain_attn.shape[0]
    buckets, heads = rel_table.shape
    padded = jnp.pad(rel_table, ((0, shard - buckets), (0, T - 2 - heads)))
    extra = jnp.concatenate([gain_attn[:, None], gain_ffn[:, None], padded], axis=1)
    out, igrad, gfin, evec, _ = layer(inputs, positions, w_query, w_key, w_value, w_output.T, w_in, w_out.T, extra, cotangent)
    gf = gfin.reshape(2, gfin.shape[1], shard, -1).astype(jnp.float32)

    def wide(first, count):
        return jnp.concatenate([gf[core, c] for core in range(2) for c in range(first, first + count)], axis=1)

    def cols(m):
        return jnp.concatenate([gf[core, c][:, m * T : (m + 1) * T] for core in range(2) for c in range(6, 9)], axis=1)

    z = lax.axis_index("fsdp")
    tiles = evec.shape[1]
    gains = evec[:12].reshape(2, -1)
    g_gain = lax.dynamic_slice_in_dim(gains, z * shard, shard, 1)
    g_table = lax.dynamic_slice_in_dim(evec[12:24], z * buckets, buckets, 1).T
    return (
        out, igrad, cols(0), cols(1), cols(2), cols(3).T, g_gain[0], g_table, wide(3, 3), wide(0, 3).T, g_gain[1],
    )


def rms_norm(values, gain):
    return values * lax.rsqrt(jnp.mean(values * values, axis=-1, keepdims=True) + EPS) * gain


def bias_onehot(query_positions, key_places, bucket_count):
    buckets = bucket_of(key_places[:, None, :] - query_positions[:, :, None])
    labels = lax.broadcasted_iota(jnp.int32, (1, bucket_count, 1, 1), 1)
    return (buckets[:, None, :, :] == labels).astype(jnp.bfloat16)


def split_heads(rows, head_count):
    return rows.reshape(rows.shape[0], rows.shape[1], head_count, -1)


def block_scores(query_rows, key_rows, onehot, table_b):
    head_count = table_b.shape[1]
    scores = jnp.einsum(
        "sqhd,skhd->shqk",
        split_heads(query_rows, head_count),
        split_heads(key_rows, head_count),
        preferred_element_type=jnp.float32,
    )
    bias_term = jnp.einsum("sbqk,bh->shqk", onehot, table_b, preferred_element_type=jnp.float32)
    return scores + bias_term


def pair_grads(
    query_rows,
    grad_rows,
    logsum,
    row_products,
    query_positions,
    key_rows,
    value_rows,
    key_places,
    table_b,
):
    head_count = table_b.shape[1]
    onehot = bias_onehot(query_positions, key_places, table_b.shape[0])
    scores = block_scores(query_rows, key_rows, onehot, table_b)
    probs = jnp.exp(scores - logsum[..., None])
    grad_heads = split_heads(grad_rows, head_count)
    dprobs = jnp.einsum(
        "sqhd,skhd->shqk",
        grad_heads,
        split_heads(value_rows, head_count),
        preferred_element_type=jnp.float32,
    )
    grad_scores = (probs * (dprobs - row_products[..., None])).astype(jnp.bfloat16)
    grad_query = jnp.einsum(
        "shqk,skhd->sqhd",
        grad_scores,
        split_heads(key_rows, head_count),
        preferred_element_type=jnp.float32,
    )
    grad_key = jnp.einsum(
        "shqk,sqhd->skhd",
        grad_scores,
        split_heads(query_rows, head_count),
        preferred_element_type=jnp.float32,
    )
    grad_value = jnp.einsum(
        "shqk,sqhd->skhd",
        probs.astype(jnp.bfloat16),
        grad_heads,
        preferred_element_type=jnp.float32,
    )
    grad_table = jnp.einsum(
        "sbqk,shqk->bh", onehot, grad_scores, preferred_element_type=jnp.float32
    )
    return (
        grad_query.reshape(query_rows.shape),
        grad_key.reshape(key_rows.shape),
        grad_value.reshape(value_rows.shape),
        grad_table,
    )


def add_rows(whole, first_row, added_term):
    current = lax.dynamic_slice_in_dim(whole, first_row, added_term.shape[1], 1)
    return lax.dynamic_update_slice_in_dim(whole, current + added_term, first_row, 1)


def project_rows(left_operand, right_operand):
    return jnp.dot(left_operand, right_operand, preferred_element_type=jnp.float32)


def outer_sum(left_operand, right_operand):
    return jnp.einsum("nf,nd->fd", left_operand, right_operand, preferred_element_type=jnp.float32)


def general_device(
    inputs,
    positions,
    w_query,
    w_key,
    w_value,
    w_output,
    gain_attn,
    rel_table,
    w_in,
    w_out,
    gain_ffn,
    cotangent,
):
    groups, block_rows, model_width = inputs.shape
    head_count = rel_table.shape[1]
    tokens = groups * block_rows
    query_w, key_w, value_w, output_w, gain_one, table_b = (
        lax.all_gather(w_query, "fsdp", axis=0, tiled=True),
        lax.all_gather(w_key, "fsdp", axis=0, tiled=True),
        lax.all_gather(w_value, "fsdp", axis=0, tiled=True),
        lax.all_gather(w_output, "fsdp", axis=1, tiled=True),
        lax.all_gather(gain_attn, "fsdp", axis=0, tiled=True),
        lax.all_gather(rel_table, "fsdp", axis=0, tiled=True),
    )
    in_w, out_w, gain_two = (
        lax.all_gather(w_in, "fsdp", axis=0, tiled=True),
        lax.all_gather(w_out, "fsdp", axis=1, tiled=True),
        lax.all_gather(gain_ffn, "fsdp", axis=0, tiled=True),
    )
    gain_one_f = gain_one.astype(jnp.float32)
    gain_two_f = gain_two.astype(jnp.float32)
    own_first = lax.axis_index("ctx") * block_rows
    query_positions = lax.dynamic_slice_in_dim(positions, own_first, block_rows, 1)
    flat_inputs = inputs.reshape(tokens, model_width).astype(jnp.float32)
    normed = rms_norm(flat_inputs, gain_one_f).astype(jnp.bfloat16)
    queries = project_rows(normed, query_w).astype(jnp.bfloat16).reshape(groups, block_rows, -1)
    key_block = project_rows(normed, key_w).astype(jnp.bfloat16).reshape(groups, block_rows, -1)
    value_block = project_rows(normed, value_w).astype(jnp.bfloat16).reshape(groups, block_rows, -1)
    inner_width = queries.shape[2]
    head_size = inner_width // head_count
    start_state = (
        jnp.full((groups, head_count, block_rows), -1e30, jnp.float32),
        jnp.zeros((groups, head_count, block_rows), jnp.float32),
        jnp.zeros((groups, block_rows, head_count, head_size), jnp.float32),
    )
    key_piece = lax.all_gather(key_block, "ctx", axis=1, tiled=True)
    value_portion = lax.all_gather(value_block, "ctx", axis=1, tiled=True)
    piece_rows = key_piece.shape[1]
    step_rows = math.gcd(piece_rows, block_rows)

    def forward_inner_step(block_index, state):
        running, total, weighted = state
        offset = block_index * step_rows
        key_part = lax.dynamic_slice_in_dim(key_piece, offset, step_rows, 1)
        value_part = lax.dynamic_slice_in_dim(value_portion, offset, step_rows, 1)
        key_places = lax.dynamic_slice_in_dim(positions, offset, step_rows, 1)
        onehot = bias_onehot(query_positions, key_places, table_b.shape[0])
        scores = block_scores(queries, key_part, onehot, table_b)
        newest = jnp.maximum(running, jnp.max(scores, axis=-1))
        factor = jnp.exp(running - newest)
        weights = jnp.exp(scores - newest[..., None])
        total = total * factor + jnp.sum(weights, axis=-1)
        update = jnp.einsum(
            "shqk,skhd->sqhd",
            weights.astype(jnp.bfloat16),
            split_heads(value_part, head_count),
            preferred_element_type=jnp.float32,
        )
        weighted = weighted * jnp.transpose(factor, (0, 2, 1))[..., None] + update
        return (newest, total, weighted)

    running, total, weighted = lax.fori_loop(
        0, piece_rows // step_rows, forward_inner_step, start_state
    )
    logsum = running + jnp.log(total)
    mixed = weighted / jnp.transpose(total, (0, 2, 1))[..., None]
    mixed_b = mixed.reshape(tokens, inner_width).astype(jnp.bfloat16)
    middle = flat_inputs + project_rows(mixed_b, output_w)
    normed_two = rms_norm(middle, gain_two_f).astype(jnp.bfloat16)
    hidden = project_rows(normed_two, in_w)
    active = jax.nn.gelu(hidden).astype(jnp.bfloat16)
    result = middle + project_rows(active, out_w)
    output = result.astype(jnp.bfloat16).reshape(inputs.shape)
    grad_top = cotangent.reshape(tokens, model_width).astype(jnp.float32)
    grad_branch = grad_top.astype(jnp.bfloat16)
    grad_out_w = outer_sum(active, grad_branch)
    grad_active = lax.dot_general(
        grad_branch, out_w, (((1,), (1,)), ((), ())), preferred_element_type=jnp.float32
    )
    gelu_pull = jax.vjp(jax.nn.gelu, hidden)[1]
    grad_hidden = gelu_pull(grad_active)[0].astype(jnp.bfloat16)
    grad_in_w = outer_sum(normed_two, grad_hidden)
    grad_normed_two = lax.dot_general(
        grad_hidden, in_w, (((1,), (1,)), ((), ())), preferred_element_type=jnp.float32
    )
    norm_pull = jax.vjp(rms_norm, middle, gain_two_f)[1]
    grad_from_norm, grad_gain_two = norm_pull(grad_normed_two)
    grad_middle = grad_top + grad_from_norm
    ffn_parts = (
        lax.psum_scatter(
            grad_in_w.astype(jnp.bfloat16), "fsdp", scatter_dimension=0, tiled=True
        ).astype(jnp.float32),
        lax.psum_scatter(
            grad_out_w.astype(jnp.bfloat16), "fsdp", scatter_dimension=1, tiled=True
        ).astype(jnp.float32),
        lax.psum_scatter(
            grad_gain_two.astype(jnp.bfloat16), "fsdp", scatter_dimension=0, tiled=True
        ).astype(jnp.float32),
    )
    ffn_parts = (
        lax.psum(ffn_parts[0].astype(jnp.bfloat16), ("seq", "ctx")).astype(jnp.float32),
        lax.psum(ffn_parts[1].astype(jnp.bfloat16), ("seq", "ctx")).astype(jnp.float32),
        lax.psum(ffn_parts[2].astype(jnp.bfloat16), ("seq", "ctx")).astype(jnp.float32),
    )
    grad_y = grad_middle.astype(jnp.bfloat16)
    grad_output_w = outer_sum(mixed_b, grad_y)
    grad_mixed = (
        lax.dot_general(
            grad_y, output_w, (((1,), (1,)), ((), ())), preferred_element_type=jnp.float32
        )
        .astype(jnp.bfloat16)
        .reshape(groups, block_rows, inner_width)
    )
    row_products = jnp.transpose(
        jnp.sum(split_heads(grad_mixed.astype(jnp.float32), head_count) * mixed, axis=-1), (0, 2, 1)
    )
    table_zero = jnp.zeros(table_b.shape, jnp.float32)
    seq_rows = block_rows * lax.axis_size("ctx")
    whole_zero = jnp.zeros((groups, seq_rows, inner_width), jnp.float32)
    start_back = (
        jnp.zeros((groups, block_rows, inner_width), jnp.float32),
        whole_zero,
        whole_zero,
        table_zero,
    )
    keys_key_piece = lax.all_gather(key_block, "ctx", axis=1, tiled=True)
    keys_value_portion = lax.all_gather(value_block, "ctx", axis=1, tiled=True)
    piece_rows = keys_key_piece.shape[1]
    keys_step_rows = math.gcd(piece_rows, block_rows)

    def keys_inner_step(block_index, state):
        query_total, key_total, value_total, table_total = state
        offset = block_index * keys_step_rows
        key_part = lax.dynamic_slice_in_dim(keys_key_piece, offset, keys_step_rows, 1)
        value_part = lax.dynamic_slice_in_dim(keys_value_portion, offset, keys_step_rows, 1)
        key_places = lax.dynamic_slice_in_dim(positions, offset, keys_step_rows, 1)
        grad_q, grad_k, grad_v, grad_t = pair_grads(
            queries,
            grad_mixed,
            logsum,
            row_products,
            query_positions,
            key_part,
            value_part,
            key_places,
            table_b,
        )
        return (
            query_total + grad_q,
            add_rows(key_total, offset, grad_k),
            add_rows(value_total, offset, grad_v),
            table_total + grad_t,
        )

    grad_query, key_whole, value_whole, grad_table = lax.fori_loop(
        0, piece_rows // keys_step_rows, keys_inner_step, start_back
    )
    grad_key, grad_value = (
        lax.psum_scatter(
            key_whole.astype(jnp.bfloat16), "ctx", scatter_dimension=1, tiled=True
        ).astype(jnp.float32),
        lax.psum_scatter(
            value_whole.astype(jnp.bfloat16), "ctx", scatter_dimension=1, tiled=True
        ).astype(jnp.float32),
    )
    query_b = grad_query.reshape(tokens, inner_width).astype(jnp.bfloat16)
    key_b = grad_key.reshape(tokens, inner_width).astype(jnp.bfloat16)
    value_b = grad_value.reshape(tokens, inner_width).astype(jnp.bfloat16)
    grad_query_w = outer_sum(normed, query_b)
    grad_key_w = outer_sum(normed, key_b)
    grad_value_w = outer_sum(normed, value_b)
    contract = (((1,), (1,)), ((), ()))
    grad_normed = lax.dot_general(query_b, query_w, contract, preferred_element_type=jnp.float32)
    grad_normed = grad_normed + lax.dot_general(
        key_b, key_w, contract, preferred_element_type=jnp.float32
    )
    grad_normed = grad_normed + lax.dot_general(
        value_b, value_w, contract, preferred_element_type=jnp.float32
    )
    first_pull = jax.vjp(rms_norm, flat_inputs, gain_one_f)[1]
    grad_from_first, grad_gain_one = first_pull(grad_normed)
    input_grad = (grad_middle + grad_from_first).reshape(inputs.shape)
    attn_parts = (
        lax.psum_scatter(
            grad_query_w.astype(jnp.bfloat16), "fsdp", scatter_dimension=0, tiled=True
        ).astype(jnp.float32),
        lax.psum_scatter(
            grad_key_w.astype(jnp.bfloat16), "fsdp", scatter_dimension=0, tiled=True
        ).astype(jnp.float32),
        lax.psum_scatter(
            grad_value_w.astype(jnp.bfloat16), "fsdp", scatter_dimension=0, tiled=True
        ).astype(jnp.float32),
        lax.psum_scatter(
            grad_output_w.astype(jnp.bfloat16), "fsdp", scatter_dimension=1, tiled=True
        ).astype(jnp.float32),
        lax.psum_scatter(
            grad_gain_one.astype(jnp.bfloat16), "fsdp", scatter_dimension=0, tiled=True
        ).astype(jnp.float32),
        lax.psum_scatter(
            grad_table.astype(jnp.bfloat16), "fsdp", scatter_dimension=0, tiled=True
        ).astype(jnp.float32),
    )
    attn_parts = (
        lax.psum(attn_parts[0].astype(jnp.bfloat16), ("seq", "ctx")).astype(jnp.float32),
        lax.psum(attn_parts[1].astype(jnp.bfloat16), ("seq", "ctx")).astype(jnp.float32),
        lax.psum(attn_parts[2].astype(jnp.bfloat16), ("seq", "ctx")).astype(jnp.float32),
        lax.psum(attn_parts[3].astype(jnp.bfloat16), ("seq", "ctx")).astype(jnp.float32),
        lax.psum(attn_parts[4].astype(jnp.bfloat16), ("seq", "ctx")).astype(jnp.float32),
        lax.psum(attn_parts[5].astype(jnp.bfloat16), ("seq", "ctx")).astype(jnp.float32),
    )
    return (
        output,
        input_grad,
        attn_parts[0],
        attn_parts[1],
        attn_parts[2],
        attn_parts[3],
        attn_parts[4],
        attn_parts[5],
        ffn_parts[0],
        ffn_parts[1],
        ffn_parts[2],
    )


def solution(mesh):
    in_specs = (
        P(("seq", "fsdp"), "ctx", None),
        P(("seq", "fsdp"), None),
        P("fsdp", None),
        P("fsdp", None),
        P("fsdp", None),
        P(None, "fsdp"),
        P("fsdp"),
        P("fsdp", None),
        P("fsdp", None),
        P(None, "fsdp"),
        P("fsdp"),
        P(("seq", "fsdp"), "ctx", None),
    )
    out_specs = (
        P(("seq", "fsdp"), "ctx", None),
        P(("seq", "fsdp"), "ctx", None),
        P("fsdp", None),
        P("fsdp", None),
        P("fsdp", None),
        P(None, "fsdp"),
        P("fsdp"),
        P("fsdp", None),
        P("fsdp", None),
        P(None, "fsdp"),
        P("fsdp"),
    )
    fits = mesh.shape["seq"] == 2 and mesh.shape["ctx"] == 4 and mesh.shape["fsdp"] == 4
    per_device = fast_device if fits else general_device
    return jax.shard_map(
        per_device, mesh=mesh, in_specs=in_specs, out_specs=out_specs, check_vma=False
    )
```

```python
import functools
import math

import jax
import jax.numpy as jnp
from jax import lax
from jax.experimental import pallas as pl
from jax.experimental.pallas import tpu as pltpu
from jax.sharding import PartitionSpec as P

MESH = pl.DeviceIdType.MESH
F32 = jnp.float32
BF = jnp.bfloat16
EPS = 1e-06
BORDERS = (12, 16, 23, 32, 46, 64, 91)
LOG2E = math.log2(math.e)
T = 128


def dot_nn(a, b):
    return jnp.dot(a, b, preferred_element_type=F32)


def dot_nt(a, b):
    return lax.dot_general(a, b, (((1,), (1,)), ((), ())), preferred_element_type=F32)


def dot_tn(a, b):
    return lax.dot_general(a, b, (((0,), (0,)), ((), ())), preferred_element_type=F32)


def bucket_of(offset):
    magnitude = jnp.abs(offset)
    logbins = jnp.full_like(magnitude, 8)
    for border in BORDERS:
        logbins = logbins + jnp.where(magnitude >= border, 1, 0)
    return jnp.where(magnitude < 8, magnitude, logbins) + jnp.where(offset > 0, 16, 0)


def pick(values, index):
    return jnp.take_along_axis(values, index, axis=1, mode="promise_in_bounds")


class Place:
    def __init__(self, z_count):
        self.y = lax.axis_index("seq")
        self.ctx = lax.axis_index("ctx")
        self.z = lax.axis_index("fsdp")
        self.x = self.ctx // 2
        self.core = self.ctx % 2
        self.col = self.y * 2 + self.x
        self.z_count = z_count
        self.sib = (self.y, self.x * 2 + 1 - self.core, self.z)
        self.xn = (self.y, (1 - self.x) * 2 + self.core, self.z)
        self.yn = (1 - self.y, self.ctx, self.z)

    def zn(self, d):
        return (self.y, self.ctx, lax.rem(self.z + d, self.z_count))


def remote(src, dst, send, recv, device):
    return pltpu.make_async_remote_copy(
        src_ref=src, dst_ref=dst, send_sem=send, recv_sem=recv, device_id=device, device_id_type=MESH
    )


class Gather:
    def __init__(self, w, ssem, rsem, slot, lo, mid, hi, here, shard):
        self.w, self.ssem, self.rsem, self.slot = w, ssem, rsem, slot
        self.lo, self.mid, self.hi = lo, mid, hi
        self.here, self.shard, self.piece = here, shard, shard // 4

    def view(self, z, col, lo, hi):
        if self.mid is None:
            return self.w.at[pl.ds(pl.multiple_of(z * self.shard, 16), self.shard), pl.ds(lo, hi - lo)]
        first = pl.multiple_of(z * self.shard + col * self.piece, 16)
        return self.w.at[pl.ds(first, self.piece), pl.ds(lo, hi - lo)]

    def copy(self, kind, d, arriving):
        p = self.here
        zs = lax.rem(p.z + p.z_count - d, p.z_count)
        col_x, col_y, col_d = p.y * 2 + 1 - p.x, (1 - p.y) * 2 + p.x, (1 - p.y) * 2 + 1 - p.x
        index = kind * 3 + d - 1
        send, recv = self.ssem.at[self.slot, index], self.rsem.at[self.slot, index]
        if kind == 0:
            ref = self.view(zs if arriving else p.z, p.col, self.lo, self.hi)
            return remote(ref, ref, send, recv, p.zn(d))
        if kind == 1:
            ref = self.view(zs, col_x if arriving else p.col, self.lo, self.hi)
            return remote(ref, ref, send, recv, p.xn)
        if kind == 2:
            ref = self.view(zs, col_y if arriving else p.col, self.lo, self.hi)
            return remote(ref, ref, send, recv, p.yn)
        if kind == 3:
            ref = self.view(zs, col_d if arriving else col_x, self.lo, self.mid)
            return remote(ref, ref, send, recv, p.yn)
        ref = self.view(zs, col_d if arriving else col_y, self.mid, self.hi)
        return remote(ref, ref, send, recv, p.xn)

    def start(self):
        for d in (1, 3, 2):
            self.copy(0, d, False).start()

    def pass_z(self):
        for d in (1, 3, 2):
            self.copy(0, d, True).wait_recv()
            self.copy(1, d, False).start()
            self.copy(2, d, False).start()

    def pass_plane(self):
        for d in (1, 3, 2):
            self.copy(1, d, True).wait_recv()
            self.copy(3, d, False).start()
            self.copy(2, d, True).wait_recv()
            self.copy(4, d, False).start()

    def finish(self):
        for d in (1, 3, 2):
            if self.mid is None:
                self.copy(0, d, True).wait_recv()
            else:
                self.copy(3, d, True).wait_recv()
                self.copy(4, d, True).wait_recv()

    def drain(self):
        for kind in range(1 if self.mid is None else 5):
            for d in (1, 3, 2):
                self.copy(kind, d, False).wait_send()


class Swap:
    def __init__(self, source, whole, ssem, rsem, lsem, here, rows):
        self.source, self.whole, self.ssem, self.rsem, self.lsem = source, whole, ssem, rsem, lsem
        self.here, self.rows = here, rows

    def block(self, ctx):
        return self.whole.at[pl.ds(pl.multiple_of(ctx * self.rows, 16), self.rows)]

    def own(self):
        return pltpu.make_async_copy(self.source.at[self.here.x], self.block(self.here.ctx), self.lsem)

    def over(self, arriving):
        p = self.here
        ctx = (1 - p.x) * 2 + p.core if arriving else p.ctx
        return remote(self.source.at[1 - p.x], self.block(ctx), self.ssem.at[0], self.rsem.at[0], p.xn)

    def pair(self, arriving):
        p = self.here
        ctx = p.x * 2 + 1 - p.core if arriving else p.ctx
        return remote(self.source.at[p.x], self.block(ctx), self.ssem.at[1], self.rsem.at[1], p.sib)

    def forward(self, arriving):
        p = self.here
        ctx = (1 - p.x) * 2 + (1 - p.core if arriving else p.core)
        return remote(self.block(ctx), self.block(ctx), self.ssem.at[2], self.rsem.at[2], p.sib)

    def start(self):
        self.over(False).start()
        self.own().start()
        self.pair(False).start()

    def relay(self):
        self.over(True).wait_recv()
        self.forward(False).start()

    def finish(self):
        self.own().wait()
        self.pair(True).wait_recv()
        self.forward(True).wait_recv()

    def drain(self):
        self.over(False).wait_send()
        self.pair(False).wait_send()
        self.forward(False).wait_send()


def enter(partners):
    barrier = pltpu.get_barrier_semaphore()
    for partner in partners:
        pl.semaphore_signal(barrier, inc=1, device_id=partner, device_id_type=MESH)
    pl.semaphore_wait(barrier, len(partners))


class Reduce:
    def __init__(self, g, r1, r2, r3, r1z, r2z, rz, fin, gfin, ssem, rsem, lsem, here, z_first):
        self.g, self.r3, self.rz, self.fin, self.gfin = g, r3, rz, fin, gfin
        self.ones, self.twos = (r1z, r1), (r2z, r2)
        self.ssem, self.rsem, self.lsem, self.here, self.z_first = ssem, rsem, lsem, here, z_first
        self.width = g.shape[-1]
        self.lo = pl.ds(0, self.width // 2)
        self.hi = pl.ds(self.width // 2, self.width // 2)
        self.piece = g.shape[4]

    def rows_z(self, c):
        return pl.ds(self.here.z, 1) if c < self.z_first else pl.ds(0, self.here.z_count)

    def count(self, c):
        return 1 if c < self.z_first else self.here.z_count

    def r1(self, c):
        return self.ones[0].at[c] if c < self.z_first else self.ones[1].at[c - self.z_first]

    def r2(self, c):
        return self.twos[0].at[c] if c < self.z_first else self.twos[1].at[c - self.z_first]

    def link(self, c, index, src, dst, device):
        return remote(src, dst, self.ssem.at[c, index], self.rsem.at[c, index], device)

    def x1(self, c):
        p = self.here
        return self.link(c, 0, self.g.at[c, 1 - p.x, :, self.rows_z(c), :, self.lo], self.r1(c).at[0], p.xn)

    def y1(self, c):
        p = self.here
        return self.link(c, 1, self.g.at[c, :, 1 - p.y, self.rows_z(c), :, self.hi], self.r1(c).at[1], p.yn)

    def x2(self, c):
        p = self.here
        return self.link(c, 2, self.g.at[c, p.x, 1 - p.y, self.rows_z(c), :, self.lo], self.r2(c).at[0], p.yn)

    def y2(self, c):
        p = self.here
        return self.link(c, 3, self.g.at[c, 1 - p.x, p.y, self.rows_z(c), :, self.hi], self.r2(c).at[1], p.xn)

    def z1(self, c, d):
        p = self.here
        to = lax.rem(p.z + d, p.z_count)
        if c < self.z_first:
            return self.link(c, 3 + d, self.g.at[c, :, :, to], self.rz.at[c, d - 1], p.zn(d))
        return self.link(c, 3 + d, self.g.at[c, p.x, p.y, to], self.r3.at[c - self.z_first, d - 1], p.zn(d))

    def over_x(self, c, arriving):
        p = self.here
        col = p.y * 2 + 1 - p.x if arriving else p.col
        return self.link(c, 7, self.fin.at[c], self.gfin.at[p.core, c, col], p.xn)

    def over_y(self, c, arriving):
        p = self.here
        ref = self.gfin.at[p.core, c, pl.ds((1 - p.y if arriving else p.y) * 2, 2)]
        return self.link(c, 8, ref, ref, p.yn)

    def keep(self, c):
        return pltpu.make_async_copy(self.fin.at[c], self.gfin.at[self.here.core, c, self.here.col], self.lsem.at[c])

    def pair(self, c, arriving):
        core = 1 - self.here.core if arriving else self.here.core
        return self.link(c, 9, self.gfin.at[core, c], self.gfin.at[core, c], self.here.sib)

    def start(self, c):
        if c < self.z_first:
            for d in (1, 3, 2):
                self.z1(c, d).start()
        else:
            self.plane(c)

    def gathered_z(self, c):
        p = self.here
        for d in (1, 3, 2):
            self.z1(c, d).wait_recv()
        for x in range(2):
            for y in range(2):
                total = self.g[c, x, y, p.z].astype(F32)
                for d in range(3):
                    total = total + self.rz[c, d, x, y].astype(F32)
                self.g[c, x, y, p.z] = total.astype(BF)
        self.plane(c)

    def plane(self, c):
        self.x1(c).start()
        self.y1(c).start()

    def second(self, c):
        p = self.here
        h = self.width // 2

        def zi(k):
            return p.z if c < self.z_first else k

        self.x1(c).wait_recv()

        def add_x(k, carry):
            for y in range(2):
                self.g[c, p.x, y, zi(k), :, :h] = (
                    self.g[c, p.x, y, zi(k), :, :h].astype(F32) + self.r1(c)[0, y, k].astype(F32)
                ).astype(BF)
            return carry

        lax.fori_loop(0, self.count(c), add_x, 0)
        self.x2(c).start()
        self.y1(c).wait_recv()

        def add_y(k, carry):
            for x in range(2):
                self.g[c, x, p.y, zi(k), :, h:] = (
                    self.g[c, x, p.y, zi(k), :, h:].astype(F32) + self.r1(c)[1, x, k].astype(F32)
                ).astype(BF)
            return carry

        lax.fori_loop(0, self.count(c), add_y, 0)
        self.y2(c).start()

    def third(self, c):
        p = self.here
        h = self.width // 2
        self.x2(c).wait_recv()
        self.y2(c).wait_recv()
        if c < self.z_first:
            self.fin[c, :, :h] = (self.g[c, p.x, p.y, p.z, :, :h].astype(F32) + self.r2(c)[0, 0].astype(F32)).astype(BF)
            self.fin[c, :, h:] = (self.g[c, p.x, p.y, p.z, :, h:].astype(F32) + self.r2(c)[1, 0].astype(F32)).astype(BF)
            self.publish(c)
            return

        def add(k, carry):
            self.g[c, p.x, p.y, k, :, :h] = (
                self.g[c, p.x, p.y, k, :, :h].astype(F32) + self.r2(c)[0, k].astype(F32)
            ).astype(BF)
            self.g[c, p.x, p.y, k, :, h:] = (
                self.g[c, p.x, p.y, k, :, h:].astype(F32) + self.r2(c)[1, k].astype(F32)
            ).astype(BF)
            return carry

        lax.fori_loop(0, p.z_count, add, 0)
        for d in (1, 3, 2):
            self.z1(c, d).start()

    def fourth(self, c):
        if c < self.z_first:
            return
        p = self.here
        for d in (1, 3, 2):
            self.z1(c, d).wait_recv()
        total = self.g[c, p.x, p.y, p.z].astype(F32)
        for d in range(3):
            total = total + self.r3[c - self.z_first, d].astype(F32)
        self.fin[c] = total.astype(BF)
        self.publish(c)

    def publish(self, c):
        self.over_x(c, False).start()
        self.keep(c).start()

    def fifth(self, c):
        self.over_x(c, True).wait_recv()
        self.keep(c).wait()
        self.over_y(c, False).start()

    def sixth(self, c):
        self.over_y(c, True).wait_recv()
        self.pair(c, False).start()

    def last(self, c):
        self.pair(c, True).wait_recv()
        for copy in (self.x1(c), self.y1(c), self.x2(c), self.y2(c), self.over_x(c, False), self.over_y(c, False), self.pair(c, False)):
            copy.wait_send()
        for d in (1, 3, 2):
            self.z1(c, d).wait_send()


def edges():
    starts, buckets = [], [15]
    lows = (8,) + BORDERS
    for b in range(14, 7, -1):
        starts.append(1 - lows[b - 7])
        buckets.append(b)
    for n in range(7, -1, -1):
        starts.append(-n)
        buckets.append(n)
    for n in range(1, 8):
        starts.append(n)
        buckets.append(16 + n)
    for b in range(8, 16):
        starts.append(lows[b - 8])
        buckets.append(16 + b)
    return starts, buckets


def gelu_parts(v):
    c0 = math.sqrt(2.0 / math.pi)
    sq = v * v
    th = jnp.tanh(v * (c0 + (c0 * 0.044715) * sq))
    half = 0.5 + 0.5 * th
    slope = half + (0.5 * v) * (1.0 - th * th) * (c0 + (3.0 * 0.044715 * c0) * sq)
    return v * half, slope


def layer_kernel(
    inputs, positions, wq, wk, wv, wo_t, win, wout_t, extra_in, cotangent,
    out_ref, igrad_ref, gfin, evec_out, probs_out,
    w, x_all, cot_all, extra, n_t, turned, q, k, v, mixed, linv, table, pool, bound, ka, va, p_slot,
    y_in, t_in, o_send, o_in, slope, gmid, dk_acc, dv_acc, cat, stage, ig_in,
    hist, far_sum, gain_acc, e_src, e_in,
    g, r1, r2, r3, r1z, r2z, rz, fin,
    ssem, rsem, swap_s, swap_r, cot_s, cot_r, e_s, e_r, lsem, psem, y_s, y_r, t_s, t_r, o_s, o_r, out_s, out_r, u_s, u_r, ev_s, ev_r,
    g_s, g_r, g_l, osem,
):
    here = Place(lax.axis_size("fsdp"))
    p = here
    D, INNER = w.shape[0], wo_t.shape[1]
    half = INNER // 2
    ffh = win.shape[1] // 2
    shard = wq.shape[0]
    piece = shard // 4
    R = x_all.shape[0]
    heads = half // 64
    nt = R // T
    active = pool.at[:, pl.ds(0, ffh)]
    y_own = pool.at[:, pl.ds(ffh, D)]
    t_own = stage
    own_rows = pl.ds(pl.multiple_of(p.z * shard, 16), shard)
    half_cols = pl.ds(pl.multiple_of(p.core * half, 128), half)
    ff_cols = pl.ds(pl.multiple_of(p.core * ffh, 128), ffh)
    c_o, c_in, c_out, c_end = 3 * half, 4 * half, 4 * half + ffh, 4 * half + 2 * ffh

    loads = [
        pltpu.make_async_copy(wq.at[:, half_cols], w.at[own_rows, pl.ds(0, half)], lsem.at[0]),
        pltpu.make_async_copy(wk.at[:, half_cols], w.at[own_rows, pl.ds(half, half)], lsem.at[1]),
        pltpu.make_async_copy(wv.at[:, half_cols], w.at[own_rows, pl.ds(2 * half, half)], lsem.at[2]),
        pltpu.make_async_copy(win.at[:, ff_cols], w.at[own_rows, pl.ds(c_in, ffh)], lsem.at[3]),
        pltpu.make_async_copy(wo_t.at[:, half_cols], w.at[own_rows, pl.ds(c_o, half)], lsem.at[4]),
        pltpu.make_async_copy(wout_t.at[:, ff_cols], w.at[own_rows, pl.ds(c_out, ffh)], lsem.at[5]),
        pltpu.make_async_copy(extra_in, extra.at[own_rows], lsem.at[6]),
    ]
    for load in loads:
        load.start()
    enter([p.sib, p.xn, p.yn, p.zn(1), p.zn(2), p.zn(3)])
    swap = Swap(inputs, x_all, swap_s, swap_r, lsem.at[7], here, inputs.shape[1])
    swap.start()
    cot_swap = Swap(cotangent, cot_all, cot_s, cot_r, lsem.at[8], here, inputs.shape[1])

    def extra_copy(d, arriving):
        zs = lax.rem(p.z + p.z_count - d, p.z_count) if arriving else p.z
        ref = extra.at[pl.ds(pl.multiple_of(zs * shard, 16), shard)]
        return remote(ref, ref, e_s.at[d - 1], e_r.at[d - 1], p.zn(d))

    loads[6].wait()
    for d in (1, 3, 2):
        extra_copy(d, False).start()
    tracks = [(n * half, n * half + 2 * T, (n + 1) * half) for n in range(3)] + [(c_o, c_o + 2 * T, c_in)]
    tracks += [(lo, lo + 3 * T, lo + 4 * T) for lo in range(c_in, c_end - 4 * T, 4 * T)] + [(c_end - 4 * T, None, c_end)]
    gathers = [Gather(w, ssem, rsem, n, lo, mid, hi, here, shard) for n, (lo, mid, hi) in enumerate(tracks)]
    for n in range(3):
        loads[n].wait()
        gathers[n].start()
    for n in range(3, 6):
        loads[n].wait()
    for gather in gathers[3:]:
        gather.start()

    starts, classes = edges()
    lane = lax.broadcasted_iota(jnp.int32, (1, T), 1)
    pos = positions[pl.ds(p.x, 1), :]
    band = [(a, d) for a in range(nt) for d in range(3) if 0 <= a + d - 1 < nt]
    cols = {}
    early = {
        36: [gathers[0].pass_plane, gathers[1].pass_plane],
        40: [swap.relay],
        34: [gathers[1].pass_z, gathers[2].pass_z],
        43: [gathers[2].pass_plane],
        23: [gathers[0].pass_z],
        44: [gathers[3].pass_z, gathers[4].pass_z],
    }

    def offsets(a, d):
        if a not in cols:
            cols[a] = jnp.broadcast_to(pos[:, a * T : (a + 1) * T], (T, T)).T
        return pos[:, (a + d - 1) * T : (a + d) * T] - cols[a]

    edge = jnp.full((1, T), -(2**20), jnp.int32)
    for j, first in enumerate(starts):
        edge = jnp.where(lane == j, first, edge)
    ranks = {}

    def ranks_of(b):
        if b not in ranks:
            offsets(b, 1)
            base = pos[:, b * T : b * T + 1]
            above = cols[b] - base
            ranks[b] = base, [
                jnp.broadcast_to(jnp.sum(jnp.where(above < lane + m * T, 1.0, 0.0), axis=0, keepdims=True), (T, T)) for m in range(2)
            ]
        return ranks[b]

    for n, (a, d) in enumerate(band):
        for step in early.get(n, ()):
            step()
        offsets(a, 1)
        base, (low, high) = ranks_of(a + d - 1)
        at = jnp.clip(cols[a] + edge - base, 0, 2 * T - 1)
        count = jnp.where(at < T, pick(low, jnp.minimum(at, T - 1)), pick(high, jnp.maximum(at - T, 0)))
        bound[a * T : (a + 1) * T, d * T : (d + 1) * T] = count.astype(jnp.int32) - 1

    for d in (1, 3, 2):
        extra_copy(d, True).wait_recv()
    buckets_per = 8
    rows = [extra[zs * shard : zs * shard + 16, :].astype(F32)[:buckets_per] for zs in range(4)]
    flat = jnp.concatenate(rows + [jnp.zeros((T - 32, T), F32)], axis=0)
    table[...] = flat.T
    gains = jnp.concatenate(
        [extra[t * T : (t + 1) * T, :].astype(F32).T[0:8] for t in range(D // T)], axis=1
    )
    gain_one, gain_two = gains[0:1], gains[1:2]
    for n, (a, d) in enumerate(band):
        for step in early.get(len(band) + n, ()):
            step()
        idx = bucket_of(offsets(a, d))
        for h in range(heads):
            tab = jnp.broadcast_to(table[pl.ds(2 + p.core * heads + h, 1), :], (T, T))
            pool[a * T : (a + 1) * T, (h * 3 + d) * T : (h * 3 + d + 1) * T] = pick(tab, idx).astype(BF)
    for step in early.get(2 * len(band), ()):
        step()

    swap.finish()
    for c in range(4):
        rows = slice(c * (R // 4), (c + 1) * (R // 4))
        xf = x_all[rows, :].astype(F32)
        scale = lax.rsqrt(jnp.mean(xf * xf, axis=1, keepdims=True) + EPS)
        stage[rows, :] = (xf * scale * gain_one).astype(BF)
        n_t[:, rows] = (xf * scale * gain_one).T.astype(BF)
    for gather in gathers[:3]:
        gather.finish()

    def project(c, carry):
        rows = pl.ds(pl.multiple_of(c * 256, 256), 256)
        for n, dest in enumerate((q, k, v)):
            out = dot_nn(stage[rows, :], w[:, n * half : (n + 1) * half]).astype(BF)
            for pair in range(half // T):
                dest[pair, rows, :] = out[:, pair * T : (pair + 1) * T]
        return carry

    lax.fori_loop(0, R // 256, project, 0)

    QT = 256
    sub = QT // T
    units = R // QT
    ahead = {
        1: [gathers[5].pass_z],
        3: [gathers[6].pass_z],
        5: [gathers[4].pass_plane],
        13: [cot_swap.relay, gathers[8].pass_z],
        4: [gathers[3].pass_plane, gathers[5].pass_plane],
        6: [gathers[6].pass_plane, cot_swap.start],
        8: [gathers[7].pass_z],
    }
    for step in ahead.get(-1, ()):
        step()

    def halves(h, lanes):
        return ((lanes < 64), lanes - 64) if h == 0 else ((lanes >= 64), lanes)

    def pair_step(hp, carry):
        lane_k = lax.broadcasted_iota(jnp.int32, (R, T), 1)
        tile_k = lax.broadcasted_iota(jnp.int32, (R, T), 0) // T
        for h in range(2):
            tab = table[pl.ds(2 + p.core * heads + hp * 2 + h, 1), :]
            inside, other = halves(h, lane_k)
            far = jnp.where(tile_k < other - 1, tab[:, 15:16], jnp.where(tile_k > other + 1, tab[:, 31:32], 0.0))
            far = jnp.where(other < nt, far, 0.0)
            ka[h] = jnp.where(inside, k[hp].astype(F32), far).astype(BF)
            va[h] = jnp.where(inside, v[hp].astype(F32), 1.0).astype(BF)
        lane_q = lax.broadcasted_iota(jnp.int32, (QT, T), 1)
        tile_q = lax.broadcasted_iota(jnp.int32, (QT, T), 0) // T
        for qi in range(units):
            for trip in range(heads // 2):
                if trip * units + qi in ahead:
                    pl.when(hp == trip)(lambda todo=ahead[trip * units + qi]: [step() for step in todo] and None)
            store = pltpu.make_async_copy(p_slot.at[qi % 2], probs_out.at[hp, :, pl.ds(qi * QT, QT)], psem.at[qi % 2])
            if qi < 2:
                pl.when(hp > 0)(store.wait)
            else:
                store.wait()
            rows = slice(qi * QT, (qi + 1) * QT)
            scores = []
            for h in range(2):
                inside, other = halves(h, lane_q)
                hot = jnp.where(other == tile_q + qi * sub, 1.0, 0.0)
                qm = jnp.where(inside, q[hp, rows, :].astype(F32), hot).astype(BF)
                scores.append(dot_nt(qm, ka[h]))
            mixes = []
            for h in range(2):
                strips = []
                for si in range(sub):
                    a = qi * sub + si
                    st = scores[h][si * T : (si + 1) * T]
                    lo, hi = max(a - 1, 0), min(a + 2, nt)
                    parts = [st[:, : lo * T]] if lo > 0 else []
                    lanes = pl.ds(pl.multiple_of((hp * 2 + h) * 3 * T + (lo - a + 1) * T, T), (hi - lo) * T)
                    near = pool[a * T : (a + 1) * T, lanes]
                    parts.append(st[:, lo * T : hi * T] + near.astype(F32))
                    if hi < nt:
                        parts.append(st[:, hi * T :])
                    strips.append(jnp.concatenate(parts, axis=1))
                sc = jnp.concatenate(strips, axis=0)
                m = jnp.max(sc, axis=1, keepdims=True)
                pb = jnp.exp2((sc - m) * LOG2E).astype(BF)
                p_slot[qi % 2, h] = pb
                mixes.append(dot_nn(pb, va[h]))
            store.start()
            o = jnp.where(lane < 64, mixes[0], mixes[1])
            total = pltpu.roll(jnp.where(lane < 64, mixes[1], mixes[0]), 64, 1)
            inv = 1.0 / total
            mixed[hp, rows, :] = (o * inv).astype(BF)
            linv[hp, rows, :] = inv
        return carry

    lax.fori_loop(0, heads // 2, pair_step, 0)
    for slot in range(2):
        pltpu.make_async_copy(p_slot.at[slot], probs_out.at[0, :, pl.ds(0, QT)], psem.at[slot]).wait()

    B = 256
    blocks = R // B
    FW = 512
    for step in ahead.get(3 * units, ()):
        step()
    for gather in gathers[3:7]:
        gather.finish()

    def y_copy(i, arriving=False):
        rows = pl.ds(pl.multiple_of(i * B, B), B)
        return remote(y_own.at[rows], y_in.at[rows], y_s.at[i], y_r.at[i], p.sib)

    def t_copy(i):
        rows = pl.ds(pl.multiple_of(i * B, B), B)
        return remote(t_own.at[rows], t_in.at[rows], t_s.at[i], t_r.at[i], p.sib)

    def o_copy(n):
        return remote(o_send.at[n], o_in.at[n], o_s.at[n], o_r.at[n], p.sib)

    def project_out(i, carry):
        rows = pl.ds(pl.multiple_of(i * B, B), B)
        mx = jnp.concatenate([mixed[pair, rows, :] for pair in range(half // T)], axis=1)
        y_own[rows, :] = dot_nt(mx, w[:, c_o : c_o + half]).astype(BF)
        y_copy(i).start()
        return carry

    lax.fori_loop(0, blocks, project_out, 0)
    for step in ahead.get(3 * units + 1, ()):
        step()

    def middle_of(rows):
        mid = x_all[rows, :].astype(F32) + (y_own[rows, :].astype(F32) + y_in[rows, :].astype(F32))
        return mid, lax.rsqrt(jnp.mean(mid * mid, axis=1, keepdims=True) + EPS)

    red = Reduce(g, r1, r2, r3, r1z, r2z, rz, fin, gfin, g_s, g_r, g_l, here, 2)
    between = {
        1: [gathers[7].pass_plane],
        3: [gathers[8].pass_plane],
    }

    def during(i, base, table):
        for n in range(blocks):
            if base + n in table:
                pl.when(i == n)(lambda todo=table[base + n]: [step() for step in todo] and None)

    def ffn_in(i, carry):
        rows = pl.ds(pl.multiple_of(i * B, B), B)
        y_copy(i).wait_recv()
        mid, scale = middle_of(rows)
        n2f = mid * scale * gain_two
        n2 = n2f.astype(BF)
        stage[rows, :] = n2
        for j in range(ffh // FW):
            hidden = dot_nn(n2, w[:, c_in + j * FW : c_in + (j + 1) * FW])
            act, slo = gelu_parts(hidden)
            active[rows, j * FW : (j + 1) * FW] = act.astype(BF)
            slope[rows, j * FW : (j + 1) * FW] = slo.astype(BF)
        during(i, 0, between)
        return carry

    lax.fori_loop(0, blocks, ffn_in, 0)
    cot_swap.finish()
    for i in range(blocks):
        rows = slice(i * B, (i + 1) * B)
        turned[:, rows] = cot_all[rows, :].astype(F32).T.astype(BF)


    def keep_pieces(c, lo, left, right):
        for n in range(0, right.shape[1], 2 * T):
            value = dot_nn(left, right[:, n : n + 2 * T])
            for zs in range(p.z_count):
                for col in range(4):
                    first_row = zs * shard + col * piece
                    g[c, col % 2, col // 2, zs, :, lo + n : lo + n + value.shape[1]] = value[first_row : first_row + piece].astype(BF)

    for c in range(ffh // FW):
        keep_pieces(c, 0, turned[...], active[:, c * FW : (c + 1) * FW])
        red.start(c)
        for step in between.get(4 + c, ()):
            step()
    for i in range(blocks):
        rows = slice(i * B, (i + 1) * B)
        turned[:, rows] = stage[rows, :].astype(F32).T.astype(BF)
    for gather in gathers[7:]:
        gather.finish()
    later = {
        2: [functools.partial(red.second, 2)],
        9: [functools.partial(red.second, 3)],
    }

    def ffn_back(i, carry):
        rows = pl.ds(pl.multiple_of(i * B, B), B)
        cot = cot_all[rows, :]
        for j in range(ffh // FW):
            grad = dot_nn(cot, w[:, c_out + j * FW : c_out + (j + 1) * FW])
            cols = slice(j * FW, (j + 1) * FW)
            slope[rows, cols] = (grad * slope[rows, cols].astype(F32)).astype(BF)
        t_own[rows, :] = dot_nt(slope[rows, :], w[:, c_in:c_out]).astype(BF)
        t_copy(i).start()
        o = dot_nt(active[rows, :], w[:, c_out:c_end])
        n = i // 2

        @pl.when(i % 2 == p.core)
        def _():
            gmid[n] = o

        @pl.when(i % 2 != p.core)
        def _():
            o_send[n] = o.astype(BF)
            o_copy(n).start()

        during(i, 0, later)
        return carry

    lax.fori_loop(0, blocks, ffn_back, 0)
    for c in range(ffh // FW):
        keep_pieces(3 + c, 0, turned[...], slope[:, c * FW : (c + 1) * FW])
        for step in later.get(4 + c, ()):
            step()
        red.start(3 + c)

    gain_acc[...] = jnp.zeros_like(gain_acc)

    def back_middle(i, carry):
        rows = pl.ds(pl.multiple_of(i * B, B), B)
        t_copy(i).wait_recv()
        mid, scale = middle_of(rows)
        t = t_own[rows, :].astype(F32) + t_in[rows, :].astype(F32)
        tg = t * gain_two
        dot = jnp.mean(tg * mid, axis=1, keepdims=True)
        gm = cot_all[rows, :].astype(F32) + scale * tg - (scale * scale * scale * dot) * mid
        gy = gm.astype(BF)
        turned[:, rows] = gm.T.astype(BF)
        grad = dot_nn(gy, w[:, c_o : c_o + half])
        for pair in range(half // T):
            slope[rows, D + pair * T : D + (pair + 1) * T] = (grad[:, pair * T : (pair + 1) * T] * linv[pair, rows, :]).astype(BF)
        n = i // 2

        @pl.when(i % 2 == p.core)
        def _():
            gain_acc[1:2, :] += jnp.sum(t * mid * scale, axis=0, keepdims=True)
            o_copy(n).wait_recv()
            slope[pl.ds(pl.multiple_of(n * B, B), B), :D] = (mid + gmid[n] + o_in[n].astype(F32)).astype(BF)
            gmid[n] = gm

        during(i, 7, later)
        return carry

    lax.fori_loop(0, blocks, back_middle, 0)
    out_own = pltpu.make_async_copy(slope.at[pl.ds(pl.multiple_of(p.x * B, B), B), pl.ds(0, D)], out_ref.at[p.x], osem.at[0])
    out_over = remote(slope.at[pl.ds(pl.multiple_of((1 - p.x) * B, B), B), pl.ds(0, D)], out_ref.at[p.x], out_s.at[0], out_r.at[0], p.xn)
    out_there = remote(slope.at[pl.ds(pl.multiple_of((1 - p.x) * B, B), B), pl.ds(0, D)], out_ref.at[1 - p.x], out_s.at[0], out_r.at[0], p.xn)
    out_own.start()
    out_over.start()

    hist[...] = jnp.zeros_like(hist)
    far_sum[...] = jnp.zeros_like(far_sum)
    row_i = lax.broadcasted_iota(jnp.int32, (2 * T, 2 * T), 0)
    col_i = lax.broadcasted_iota(jnp.int32, (2 * T, 2 * T), 1)
    upto_incl = jnp.where(jnp.logical_and(row_i <= col_i, row_i // T == col_i // T), 1.0, 0.0).astype(BF)
    skip_left, skip_right = 96, 32

    def p_load(hp, qi):
        return pltpu.make_async_copy(probs_out.at[hp, :, pl.ds(qi * QT, QT)], p_slot.at[qi % 2], psem.at[qi % 2])

    p_load(0, 0).start()
    stages = {
        4: [functools.partial(red.second, 4)],
        5: [functools.partial(red.gathered_z, 0)],
        6: [functools.partial(red.third, 2)],
        7: [functools.partial(red.third, 3)],
        8: [functools.partial(red.second, 6), functools.partial(red.fourth, 2), functools.partial(red.third, 4), functools.partial(red.second, 5)],
        11: [functools.partial(red.fourth, 3), functools.partial(red.second, 7), functools.partial(red.second, 0)],
    }

    def lanes_of(m, hp):
        return pl.ds(pl.multiple_of(m * half + hp * T, T), T)

    def pair_back(hp, carry):
        lane_k = lax.broadcasted_iota(jnp.int32, (R, T), 1)
        tile_k = lax.broadcasted_iota(jnp.int32, (R, T), 0) // T
        for h in range(2):
            inside = (lane_k < 64) if h == 0 else (lane_k >= 64)
            other = lane_k - 64 if h == 0 else lane_k
            va[h] = jnp.where(inside, v[hp].astype(F32), jnp.where(other < 3, 1.0, 0.0)).astype(BF)
            ka[h] = jnp.where(inside, k[hp].astype(F32), jnp.where(other == tile_k, 1.0, 0.0)).astype(BF)
        dk_acc[...] = jnp.zeros_like(dk_acc)
        dv_acc[...] = jnp.zeros_like(dv_acc)
        lane_q = lax.broadcasted_iota(jnp.int32, (QT, T), 1)
        tile_q = lax.broadcasted_iota(jnp.int32, (QT, T), 0) // T
        for qi in range(units):
            for trip in range(heads // 2):
                if trip * units + qi in stages:
                    pl.when(hp == trip)(lambda todo=stages[trip * units + qi]: [step() for step in todo] and None)
            rows = slice(qi * QT, (qi + 1) * QT)
            p_load(hp, qi).wait()
            if qi + 1 < units:
                p_load(hp, qi + 1).start()
            else:
                pl.when(hp < heads // 2 - 1)(lambda: p_load(hp + 1, 0).start())
            do = slope[rows, pl.ds(pl.multiple_of(D + hp * T, T), T)].astype(F32)
            prod = do * mixed[hp, rows, :].astype(F32)
            qf = q[hp, rows, :].astype(F32)
            dps, dms, qms, dqs, grads = [], [], [], [], []
            for h in range(2):
                inside, other = halves(h, lane_q)
                rd = jnp.sum(jnp.where(inside, prod, 0.0), axis=1, keepdims=True)
                ra = rd.astype(BF).astype(F32)
                rb = (rd - ra).astype(BF).astype(F32)
                rc = rd - ra - rb
                dm = jnp.where(inside, do, 0.0)
                da = (dm - jnp.where(other == 0, ra, jnp.where(other == 1, rb, jnp.where(other == 2, rc, 0.0)))).astype(BF)
                dms.append(dm.astype(BF))
                qms.append(jnp.where(inside, qf, 0.0).astype(BF))
                dps.append(dot_nt(da, va[h]))
            for h in range(2):
                pb = p_slot[qi % 2, h]
                ds = (pb.astype(F32) * dps[h]).astype(BF)
                grads.append(ds)
                dqs.append(dot_nn(ds, ka[h]))
                dv_acc[...] += dot_tn(dms[h], pb)
                dk_acc[...] += dot_tn(qms[h], ds)
            cat[rows, lanes_of(0, hp)] = jnp.where(lane < 64, dqs[0], dqs[1]).astype(BF)
            in_tile = lax.broadcasted_iota(jnp.int32, (QT, T), 0) % T
            tile = tile_q + qi * sub
            for h in range(2):
                ds = grads[h]
                inside, other = halves(h, lane_q)
                spare = jnp.where(inside, 0.0, dqs[h])
                left = jnp.logical_or(other < tile - 1, jnp.logical_and(other == tile - 1, in_tile >= skip_left))
                right = jnp.logical_or(other > tile + 1, jnp.logical_and(other == tile + 1, in_tile < skip_right))
                for m, cond in enumerate((left, jnp.logical_and(right, other < nt), other < nt)):
                    far_sum[hp * 2 + h, m : m + 1, :] += jnp.sum(jnp.where(cond, spare, 0.0), axis=0, keepdims=True)
                found = jnp.zeros((8, T), F32)
                first_lane = min(max(qi * sub - 1, 0), nt - 4) * T
                sums_all = [dot_nn(ds[:, first_lane + m * 2 * T : first_lane + (m + 1) * 2 * T], upto_incl) for m in range(2)]
                for si in range(sub):
                    a = qi * sub + si
                    for d in range(3):
                        b = a + d - 1
                        if 0 <= b < nt:
                            r0, r1_ = (0, skip_left) if d == 0 else ((skip_right, T) if d == 2 else (0, T))
                            lane0 = b * T - first_lane
                            sums = sums_all[lane0 // (2 * T)][si * T + r0 : si * T + r1_, lane0 % (2 * T) : lane0 % (2 * T) + T]
                            idx = bound[a * T + r0 : a * T + r1_, d * T : (d + 1) * T]
                            got = jnp.where(idx >= 0, pick(sums, jnp.maximum(idx, 0)), 0.0)
                            found = found + jnp.sum(got.reshape((r1_ - r0) // 8, 8, T), axis=0)
                hist[hp * 2 + h] += found
        cat[:, lanes_of(1, hp)] = dk_acc[...].T.astype(BF)
        cat[:, lanes_of(2, hp)] = dv_acc[...].T.astype(BF)
        c = 6 + hp
        for m in range(3):
            keep_pieces(c, m * T, n_t[...], cat[:, lanes_of(m, hp)])
        keep_pieces(c, 3 * T, turned[...], mixed[hp])
        for trip in range(heads // 2):
            pl.when(hp == trip)(functools.partial(red.start, 6 + trip))
        return carry

    lax.fori_loop(0, heads // 2, pair_back, 0)

    def u_copy(n):
        return remote(slope.at[pl.ds((2 + n) * B, B), pl.ds(0, D)], o_in.at[2 + n], u_s.at[n], u_r.at[n], p.sib)

    for n in range(2):
        rows = pl.ds(pl.multiple_of((2 * n + 1 - p.core) * B, B), B)
        slope[(2 + n) * B : (3 + n) * B, :D] = dot_nt(cat[rows, :], w[:, :c_o]).astype(BF)
        u_copy(n).start()
    red.fifth(2)
    red.fifth(3)
    red.fourth(4)
    red.third(6)
    for n in range(2):
        rows = pl.ds(pl.multiple_of((2 * n + p.core) * B, B), B)
        t = dot_nt(cat[rows, :], w[:, :c_o])
        u_copy(n).wait_recv()
        t = t + o_in[2 + n].astype(F32)
        xf = x_all[rows, :].astype(F32)
        scale = lax.rsqrt(jnp.mean(xf * xf, axis=1, keepdims=True) + EPS)
        tg = t * gain_one
        dot = jnp.mean(tg * xf, axis=1, keepdims=True)
        gmid[n] = gmid[n] + scale * tg - (scale * scale * scale * dot) * xf
        gain_acc[0:1, :] += jnp.sum(t * xf * scale, axis=0, keepdims=True)
    ig_own = pltpu.make_async_copy(gmid.at[p.x], igrad_ref.at[p.x], osem.at[1])
    ig_own.start()
    slope[:B, D:] = gmid[1 - p.x].astype(BF)
    ig_over = remote(slope.at[pl.ds(0, B), pl.ds(D, D)], ig_in, out_s.at[1], out_r.at[1], p.xn)

    gains_rows = [gain_acc[m : m + 1, t * T : (t + 1) * T] for m in range(2) for t in range(D // T)]
    class_of = jnp.zeros((1, T), jnp.int32)
    for j, bkt in enumerate(classes):
        class_of = jnp.where(lane == bkt, j, class_of)
    used = jnp.logical_and(lane < 32, lane != 16)
    rows_h = []
    for h in range(heads):
        upto = jnp.sum(hist[h], axis=0, keepdims=True)
        sums = jnp.sum(far_sum[h], axis=1, keepdims=True)
        left, right, every = sums[0:1], sums[1:2], sums[2:3]
        near = every - left - right
        n_edges = len(starts)
        upto = jnp.where(lane < n_edges, upto, jnp.where(lane == n_edges, near, 0.0))
        below = jnp.where(lane == 0, 0.0, pltpu.roll(upto, 1, 1))
        per = upto - below + jnp.where(lane == 0, left, jnp.where(lane == n_edges, right, 0.0))
        rows_h.append(per)
    heads_rows = jnp.concatenate(rows_h + [jnp.zeros((8 - heads, T), F32)], axis=0)
    picked = jnp.take_along_axis(heads_rows, jnp.broadcast_to(class_of, (8, T)), axis=1)
    picked = jnp.where(used, picked, 0.0)[:heads]
    zero = jnp.zeros((heads, T), F32)
    first_half = jnp.where(p.core == 0, picked, zero)
    other_half = jnp.where(p.core == 0, zero, picked)
    e_src[0] = jnp.concatenate(gains_rows + [first_half, other_half], axis=0)

    def e_copy(n):
        device = (p.sib, p.xn, p.yn, p.zn(1), p.zn(2), p.zn(3))[n]
        return remote(e_src.at[min(n, 3)], e_in.at[n], ev_s.at[n], ev_r.at[n], device)

    ig_over.start()
    e_copy(0).start()
    e_copy(0).wait_recv()
    e_src[1] = e_src[0] + e_in[0]
    e_copy(1).start()
    red.third(5)
    red.third(0)
    red.fifth(4)
    red.gathered_z(1)
    red.sixth(2)
    red.second(8)
    red.fourth(6)
    red.third(7)
    e_copy(1).wait_recv()
    e_src[2] = e_src[1] + e_in[1]
    e_copy(2).start()
    red.sixth(3)
    red.fourth(7)
    e_copy(2).wait_recv()
    e_src[3] = e_src[2] + e_in[2]
    e_copy(3).start()
    e_copy(4).start()
    e_copy(5).start()
    red.fifth(0)
    red.fourth(5)
    red.second(1)
    red.third(8)
    red.fifth(6)
    red.fifth(7)
    red.fifth(5)
    red.third(1)
    red.sixth(6)
    red.fourth(8)
    red.fifth(1)
    red.sixth(7)
    red.fifth(8)
    red.sixth(5)
    red.sixth(0)
    red.sixth(1)
    red.sixth(4)
    red.sixth(8)
    for n in range(3, 6):
        e_copy(n).wait_recv()
    e_src[4] = e_src[3] + e_in[3] + e_in[4] + e_in[5]
    ev_out = pltpu.make_async_copy(e_src.at[4], evec_out, osem.at[2])
    ev_out.start()
    ig_over.wait_recv()
    ig_own.wait()
    gmid[0] = ig_in[...].astype(F32)
    ig_there = pltpu.make_async_copy(gmid.at[0], igrad_ref.at[1 - p.x], osem.at[1])
    ig_there.start()
    out_own.wait()
    out_there.wait_recv()
    for c in range(g.shape[0]):
        red.last(c)
    for i in range(blocks):
        y_copy(i).wait_send()
        t_copy(i).wait_send()
    for n in range(2):
        o_copy(n).wait_send()
        u_copy(n).wait_send()
    out_over.wait_send()
    ig_over.wait_send()
    for n in range(6):
        e_copy(n).wait_send()
    for gather in gathers:
        gather.drain()
    swap.drain()
    cot_swap.drain()
    for d in (1, 3, 2):
        extra_copy(d, False).wait_send()
    ev_out.wait()
    ig_there.wait()


def layer(inputs, positions, wq, wk, wv, wo_t, win, wout_t, extra_in, cotangent):
    D, INNER, FF = win.shape[0] * lax.axis_size("fsdp"), wo_t.shape[1], win.shape[1]
    half, ffh, shard = INNER // 2, FF // 2, wq.shape[0]
    B = inputs.shape[1]
    R = inputs.shape[0] * B * 2
    heads, pairs = half // 64, half // T
    width = 4 * half + 2 * ffh
    piece, FW = shard // 4, 512
    nc = width // FW
    zf = 2
    sds = jax.ShapeDtypeStruct
    any_ = pl.BlockSpec(memory_space=pl.ANY)
    vm = pl.BlockSpec(memory_space=pltpu.VMEM)
    sem = pltpu.SemaphoreType.DMA
    V = pltpu.VMEM
    return pl.pallas_call(
        layer_kernel,
        in_specs=[any_, vm] + [any_] * 8,
        out_specs=[any_] * 5,
        out_shape=[
            sds(inputs.shape, BF), sds(inputs.shape, F32), sds((2, nc, 4, piece, FW), BF), sds((24, T), F32), sds((pairs, 2, R, R), BF),
        ],
        scratch_shapes=[
            V((D, width), BF), V((R, D), BF), V((R, D), BF), V((D, T), BF), V((D, R), BF), V((D, R), BF),
            V((pairs, R, T), BF), V((pairs, R, T), BF), V((pairs, R, T), BF), V((pairs, R, T), BF), V((pairs, R, T), F32), V((T, T), F32),
            V((R, heads * 3 * T), BF), V((R, 3 * T), jnp.int32),
            V((2, R, T), BF), V((2, R, T), BF), V((2, 2, 256, R), BF),
            V((R, D), BF), V((R, D), BF), V((2, B, D), BF), V((4, B, D), BF),
            V((R, ffh), BF), V((2, B, D), F32), V((T, R), F32), V((T, R), F32),
            V((R, 3 * half), BF), V((R, D), BF), V((B, D), BF),
            V((heads, 8, T), F32), V((heads, 8, T), F32), V((8, D), F32), V((5, 24, T), F32), V((6, 24, T), F32),
            V((nc, 2, 2, 4, piece, FW), BF), V((nc - zf, 2, 2, 4, piece, FW // 2), BF), V((nc - zf, 2, 4, piece, FW // 2), BF),
            V((nc - zf, 3, piece, FW), BF), V((zf, 2, 2, 1, piece, FW // 2), BF), V((zf, 2, 1, piece, FW // 2), BF),
            V((zf, 3, 2, 2, piece, FW), BF), V((nc, piece, FW), BF),
            sem((10, 15)), sem((10, 15)), sem((3,)), sem((3,)), sem((3,)), sem((3,)), sem((3,)), sem((3,)), sem((12,)), sem((2,)),
            sem((4,)), sem((4,)), sem((4,)), sem((4,)), sem((2,)), sem((2,)), sem((2,)), sem((2,)), sem((2,)), sem((2,)), sem((6,)), sem((6,)),
            sem((nc, 10)), sem((nc, 10)), sem((nc,)), sem((3,)),
        ],
        compiler_params=pltpu.CompilerParams(collective_id=0, has_side_effects=True, vmem_limit_bytes=63 * 2**20),
        name="layer",
    )(inputs, positions, wq, wk, wv, wo_t, win, wout_t, extra_in, cotangent)


def finish_kernel(gfin, out_in, ig_in, wq, wk, wv, wo_t, win, wout_t, out, ig, gv, fa, fw, ob, ib, lsem, osem):
    cores, chunks, cols, piece, width = gv.shape
    half, third = fa.shape[2] // 2, fw.shape[2] // 2
    order = [(part, core) for part in range(3) for core in range(cores)]
    loads = [
        pltpu.make_async_copy(gfin.at[core, pl.ds(part * 3, 3)], gv.at[core, pl.ds(part * 3, 3)], lsem.at[n])
        for n, (part, core) in enumerate(order)
    ]
    through = [
        (pltpu.make_async_copy(a, b, lsem.at[len(order) + n]), pltpu.make_async_copy(b, c, osem.at[n]))
        for n, (a, b, c) in enumerate(((ig_in, ib, ig), (out_in, ob, out)))
    ]
    loads[0].start()
    for load, _ in through:
        load.start()
    for load in loads[1:]:
        load.start()
    stores = []
    for n, (part, core) in enumerate(order):
        loads[n].wait()

        def widen(col, carry):
            rows = pl.ds(pl.multiple_of(col * piece, 16), piece)
            for c in range(3):
                value = gv[core, part * 3 + c, col].astype(F32)
                if part < 2:
                    first = core * third + c * width
                    fw[part, rows, first : first + width] = value
                else:
                    first = core * half + c * T
                    for m in range(4):
                        fa[m, rows, first : first + T] = value[:, m * T : (m + 1) * T]
            return carry

        lax.fori_loop(0, cols, widen, 0)
        if part < 2:
            lanes = pl.ds(core * third, third)
            stores.append(pltpu.make_async_copy(fw.at[part, :, lanes], (wout_t, win)[part].at[:, lanes], osem.at[2 + n]))
            stores[-1].start()
        if n == 0:
            for load, store in through:
                load.wait()
                store.start()
                stores.append(store)
    for m, ref in enumerate((wq, wk, wv, wo_t)):
        stores.append(pltpu.make_async_copy(fa.at[m], ref, osem.at[6 + m]))
        stores[-1].start()
    for store in stores:
        store.wait()


def finish(gfin, out, igrad):
    cores, chunks, cols, piece, width = gfin.shape
    shard, d, ff = cols * piece, cols * piece * 4, cores * 3 * width
    sds = jax.ShapeDtypeStruct
    any_ = pl.BlockSpec(memory_space=pl.ANY)
    return pl.pallas_call(
        finish_kernel,
        in_specs=[any_] * 3,
        out_specs=[any_] * 8,
        out_shape=[sds((shard, d), F32)] * 4 + [sds((shard, ff), F32)] * 2 + [sds(out.shape, BF), sds(igrad.shape, F32)],
        scratch_shapes=[
            pltpu.VMEM(gfin.shape, BF), pltpu.VMEM((4, shard, d), F32), pltpu.VMEM((2, shard, ff), F32),
            pltpu.VMEM(out.shape, BF), pltpu.VMEM(igrad.shape, F32),
            pltpu.SemaphoreType.DMA((8,)), pltpu.SemaphoreType.DMA((10,)),
        ],
        compiler_params=pltpu.CompilerParams(vmem_limit_bytes=60 * 2**20),
        name="finish",
    )(gfin, out, igrad)


def fast_device(inputs, positions, w_query, w_key, w_value, w_output, gain_attn, rel_table, w_in, w_out, gain_ffn, cotangent):
    shard = gain_attn.shape[0]
    buckets, heads = rel_table.shape
    padded = jnp.pad(rel_table, ((0, shard - buckets), (0, T - 2 - heads)))
    extra = jnp.concatenate([gain_attn[:, None], gain_ffn[:, None], padded], axis=1)
    out, igrad, gfin, evec, _ = layer(inputs, positions, w_query, w_key, w_value, w_output.T, w_in, w_out.T, extra, cotangent)
    g_q, g_k, g_v, g_o, g_in, g_out, out, igrad = finish(gfin, out, igrad)
    z = lax.axis_index("fsdp")
    tiles = evec.shape[1]
    gains = evec[:12].reshape(2, -1)
    g_gain = lax.dynamic_slice_in_dim(gains, z * shard, shard, 1)
    g_table = lax.dynamic_slice_in_dim(evec[12:24], z * buckets, buckets, 1).T
    return out, igrad, g_q, g_k, g_v, g_o.T, g_gain[0], g_table, g_in, g_out.T, g_gain[1]


def rms_norm(values, gain):
    return values * lax.rsqrt(jnp.mean(values * values, axis=-1, keepdims=True) + EPS) * gain


def bias_onehot(query_positions, key_places, bucket_count):
    buckets = bucket_of(key_places[:, None, :] - query_positions[:, :, None])
    labels = lax.broadcasted_iota(jnp.int32, (1, bucket_count, 1, 1), 1)
    return (buckets[:, None, :, :] == labels).astype(jnp.bfloat16)


def split_heads(rows, head_count):
    return rows.reshape(rows.shape[0], rows.shape[1], head_count, -1)


def block_scores(query_rows, key_rows, onehot, table_b):
    head_count = table_b.shape[1]
    scores = jnp.einsum(
        "sqhd,skhd->shqk",
        split_heads(query_rows, head_count),
        split_heads(key_rows, head_count),
        preferred_element_type=jnp.float32,
    )
    bias_term = jnp.einsum("sbqk,bh->shqk", onehot, table_b, preferred_element_type=jnp.float32)
    return scores + bias_term


def pair_grads(
    query_rows,
    grad_rows,
    logsum,
    row_products,
    query_positions,
    key_rows,
    value_rows,
    key_places,
    table_b,
):
    head_count = table_b.shape[1]
    onehot = bias_onehot(query_positions, key_places, table_b.shape[0])
    scores = block_scores(query_rows, key_rows, onehot, table_b)
    probs = jnp.exp(scores - logsum[..., None])
    grad_heads = split_heads(grad_rows, head_count)
    dprobs = jnp.einsum(
        "sqhd,skhd->shqk",
        grad_heads,
        split_heads(value_rows, head_count),
        preferred_element_type=jnp.float32,
    )
    grad_scores = (probs * (dprobs - row_products[..., None])).astype(jnp.bfloat16)
    grad_query = jnp.einsum(
        "shqk,skhd->sqhd",
        grad_scores,
        split_heads(key_rows, head_count),
        preferred_element_type=jnp.float32,
    )
    grad_key = jnp.einsum(
        "shqk,sqhd->skhd",
        grad_scores,
        split_heads(query_rows, head_count),
        preferred_element_type=jnp.float32,
    )
    grad_value = jnp.einsum(
        "shqk,sqhd->skhd",
        probs.astype(jnp.bfloat16),
        grad_heads,
        preferred_element_type=jnp.float32,
    )
    grad_table = jnp.einsum(
        "sbqk,shqk->bh", onehot, grad_scores, preferred_element_type=jnp.float32
    )
    return (
        grad_query.reshape(query_rows.shape),
        grad_key.reshape(key_rows.shape),
        grad_value.reshape(value_rows.shape),
        grad_table,
    )


def add_rows(whole, first_row, added_term):
    current = lax.dynamic_slice_in_dim(whole, first_row, added_term.shape[1], 1)
    return lax.dynamic_update_slice_in_dim(whole, current + added_term, first_row, 1)


def project_rows(left_operand, right_operand):
    return jnp.dot(left_operand, right_operand, preferred_element_type=jnp.float32)


def outer_sum(left_operand, right_operand):
    return jnp.einsum("nf,nd->fd", left_operand, right_operand, preferred_element_type=jnp.float32)


def general_device(
    inputs,
    positions,
    w_query,
    w_key,
    w_value,
    w_output,
    gain_attn,
    rel_table,
    w_in,
    w_out,
    gain_ffn,
    cotangent,
):
    groups, block_rows, model_width = inputs.shape
    head_count = rel_table.shape[1]
    tokens = groups * block_rows
    query_w, key_w, value_w, output_w, gain_one, table_b = (
        lax.all_gather(w_query, "fsdp", axis=0, tiled=True),
        lax.all_gather(w_key, "fsdp", axis=0, tiled=True),
        lax.all_gather(w_value, "fsdp", axis=0, tiled=True),
        lax.all_gather(w_output, "fsdp", axis=1, tiled=True),
        lax.all_gather(gain_attn, "fsdp", axis=0, tiled=True),
        lax.all_gather(rel_table, "fsdp", axis=0, tiled=True),
    )
    in_w, out_w, gain_two = (
        lax.all_gather(w_in, "fsdp", axis=0, tiled=True),
        lax.all_gather(w_out, "fsdp", axis=1, tiled=True),
        lax.all_gather(gain_ffn, "fsdp", axis=0, tiled=True),
    )
    gain_one_f = gain_one.astype(jnp.float32)
    gain_two_f = gain_two.astype(jnp.float32)
    own_first = lax.axis_index("ctx") * block_rows
    query_positions = lax.dynamic_slice_in_dim(positions, own_first, block_rows, 1)
    flat_inputs = inputs.reshape(tokens, model_width).astype(jnp.float32)
    normed = rms_norm(flat_inputs, gain_one_f).astype(jnp.bfloat16)
    queries = project_rows(normed, query_w).astype(jnp.bfloat16).reshape(groups, block_rows, -1)
    key_block = project_rows(normed, key_w).astype(jnp.bfloat16).reshape(groups, block_rows, -1)
    value_block = project_rows(normed, value_w).astype(jnp.bfloat16).reshape(groups, block_rows, -1)
    inner_width = queries.shape[2]
    head_size = inner_width // head_count
    start_state = (
        jnp.full((groups, head_count, block_rows), -1e30, jnp.float32),
        jnp.zeros((groups, head_count, block_rows), jnp.float32),
        jnp.zeros((groups, block_rows, head_count, head_size), jnp.float32),
    )
    key_piece = lax.all_gather(key_block, "ctx", axis=1, tiled=True)
    value_portion = lax.all_gather(value_block, "ctx", axis=1, tiled=True)
    piece_rows = key_piece.shape[1]
    step_rows = math.gcd(piece_rows, block_rows)

    def forward_inner_step(block_index, state):
        running, total, weighted = state
        offset = block_index * step_rows
        key_part = lax.dynamic_slice_in_dim(key_piece, offset, step_rows, 1)
        value_part = lax.dynamic_slice_in_dim(value_portion, offset, step_rows, 1)
        key_places = lax.dynamic_slice_in_dim(positions, offset, step_rows, 1)
        onehot = bias_onehot(query_positions, key_places, table_b.shape[0])
        scores = block_scores(queries, key_part, onehot, table_b)
        newest = jnp.maximum(running, jnp.max(scores, axis=-1))
        factor = jnp.exp(running - newest)
        weights = jnp.exp(scores - newest[..., None])
        total = total * factor + jnp.sum(weights, axis=-1)
        update = jnp.einsum(
            "shqk,skhd->sqhd",
            weights.astype(jnp.bfloat16),
            split_heads(value_part, head_count),
            preferred_element_type=jnp.float32,
        )
        weighted = weighted * jnp.transpose(factor, (0, 2, 1))[..., None] + update
        return (newest, total, weighted)

    running, total, weighted = lax.fori_loop(
        0, piece_rows // step_rows, forward_inner_step, start_state
    )
    logsum = running + jnp.log(total)
    mixed = weighted / jnp.transpose(total, (0, 2, 1))[..., None]
    mixed_b = mixed.reshape(tokens, inner_width).astype(jnp.bfloat16)
    middle = flat_inputs + project_rows(mixed_b, output_w)
    normed_two = rms_norm(middle, gain_two_f).astype(jnp.bfloat16)
    hidden = project_rows(normed_two, in_w)
    active = jax.nn.gelu(hidden).astype(jnp.bfloat16)
    result = middle + project_rows(active, out_w)
    output = result.astype(jnp.bfloat16).reshape(inputs.shape)
    grad_top = cotangent.reshape(tokens, model_width).astype(jnp.float32)
    grad_branch = grad_top.astype(jnp.bfloat16)
    grad_out_w = outer_sum(active, grad_branch)
    grad_active = lax.dot_general(
        grad_branch, out_w, (((1,), (1,)), ((), ())), preferred_element_type=jnp.float32
    )
    gelu_pull = jax.vjp(jax.nn.gelu, hidden)[1]
    grad_hidden = gelu_pull(grad_active)[0].astype(jnp.bfloat16)
    grad_in_w = outer_sum(normed_two, grad_hidden)
    grad_normed_two = lax.dot_general(
        grad_hidden, in_w, (((1,), (1,)), ((), ())), preferred_element_type=jnp.float32
    )
    norm_pull = jax.vjp(rms_norm, middle, gain_two_f)[1]
    grad_from_norm, grad_gain_two = norm_pull(grad_normed_two)
    grad_middle = grad_top + grad_from_norm
    ffn_parts = (
        lax.psum_scatter(
            grad_in_w.astype(jnp.bfloat16), "fsdp", scatter_dimension=0, tiled=True
        ).astype(jnp.float32),
        lax.psum_scatter(
            grad_out_w.astype(jnp.bfloat16), "fsdp", scatter_dimension=1, tiled=True
        ).astype(jnp.float32),
        lax.psum_scatter(
            grad_gain_two.astype(jnp.bfloat16), "fsdp", scatter_dimension=0, tiled=True
        ).astype(jnp.float32),
    )
    ffn_parts = (
        lax.psum(ffn_parts[0].astype(jnp.bfloat16), ("seq", "ctx")).astype(jnp.float32),
        lax.psum(ffn_parts[1].astype(jnp.bfloat16), ("seq", "ctx")).astype(jnp.float32),
        lax.psum(ffn_parts[2].astype(jnp.bfloat16), ("seq", "ctx")).astype(jnp.float32),
    )
    grad_y = grad_middle.astype(jnp.bfloat16)
    grad_output_w = outer_sum(mixed_b, grad_y)
    grad_mixed = (
        lax.dot_general(
            grad_y, output_w, (((1,), (1,)), ((), ())), preferred_element_type=jnp.float32
        )
        .astype(jnp.bfloat16)
        .reshape(groups, block_rows, inner_width)
    )
    row_products = jnp.transpose(
        jnp.sum(split_heads(grad_mixed.astype(jnp.float32), head_count) * mixed, axis=-1), (0, 2, 1)
    )
    table_zero = jnp.zeros(table_b.shape, jnp.float32)
    seq_rows = block_rows * lax.axis_size("ctx")
    whole_zero = jnp.zeros((groups, seq_rows, inner_width), jnp.float32)
    start_back = (
        jnp.zeros((groups, block_rows, inner_width), jnp.float32),
        whole_zero,
        whole_zero,
        table_zero,
    )
    keys_key_piece = lax.all_gather(key_block, "ctx", axis=1, tiled=True)
    keys_value_portion = lax.all_gather(value_block, "ctx", axis=1, tiled=True)
    piece_rows = keys_key_piece.shape[1]
    keys_step_rows = math.gcd(piece_rows, block_rows)

    def keys_inner_step(block_index, state):
        query_total, key_total, value_total, table_total = state
        offset = block_index * keys_step_rows
        key_part = lax.dynamic_slice_in_dim(keys_key_piece, offset, keys_step_rows, 1)
        value_part = lax.dynamic_slice_in_dim(keys_value_portion, offset, keys_step_rows, 1)
        key_places = lax.dynamic_slice_in_dim(positions, offset, keys_step_rows, 1)
        grad_q, grad_k, grad_v, grad_t = pair_grads(
            queries,
            grad_mixed,
            logsum,
            row_products,
            query_positions,
            key_part,
            value_part,
            key_places,
            table_b,
        )
        return (
            query_total + grad_q,
            add_rows(key_total, offset, grad_k),
            add_rows(value_total, offset, grad_v),
            table_total + grad_t,
        )

    grad_query, key_whole, value_whole, grad_table = lax.fori_loop(
        0, piece_rows // keys_step_rows, keys_inner_step, start_back
    )
    grad_key, grad_value = (
        lax.psum_scatter(
            key_whole.astype(jnp.bfloat16), "ctx", scatter_dimension=1, tiled=True
        ).astype(jnp.float32),
        lax.psum_scatter(
            value_whole.astype(jnp.bfloat16), "ctx", scatter_dimension=1, tiled=True
        ).astype(jnp.float32),
    )
    query_b = grad_query.reshape(tokens, inner_width).astype(jnp.bfloat16)
    key_b = grad_key.reshape(tokens, inner_width).astype(jnp.bfloat16)
    value_b = grad_value.reshape(tokens, inner_width).astype(jnp.bfloat16)
    grad_query_w = outer_sum(normed, query_b)
    grad_key_w = outer_sum(normed, key_b)
    grad_value_w = outer_sum(normed, value_b)
    contract = (((1,), (1,)), ((), ()))
    grad_normed = lax.dot_general(query_b, query_w, contract, preferred_element_type=jnp.float32)
    grad_normed = grad_normed + lax.dot_general(
        key_b, key_w, contract, preferred_element_type=jnp.float32
    )
    grad_normed = grad_normed + lax.dot_general(
        value_b, value_w, contract, preferred_element_type=jnp.float32
    )
    first_pull = jax.vjp(rms_norm, flat_inputs, gain_one_f)[1]
    grad_from_first, grad_gain_one = first_pull(grad_normed)
    input_grad = (grad_middle + grad_from_first).reshape(inputs.shape)
    attn_parts = (
        lax.psum_scatter(
            grad_query_w.astype(jnp.bfloat16), "fsdp", scatter_dimension=0, tiled=True
        ).astype(jnp.float32),
        lax.psum_scatter(
            grad_key_w.astype(jnp.bfloat16), "fsdp", scatter_dimension=0, tiled=True
        ).astype(jnp.float32),
        lax.psum_scatter(
            grad_value_w.astype(jnp.bfloat16), "fsdp", scatter_dimension=0, tiled=True
        ).astype(jnp.float32),
        lax.psum_scatter(
            grad_output_w.astype(jnp.bfloat16), "fsdp", scatter_dimension=1, tiled=True
        ).astype(jnp.float32),
        lax.psum_scatter(
            grad_gain_one.astype(jnp.bfloat16), "fsdp", scatter_dimension=0, tiled=True
        ).astype(jnp.float32),
        lax.psum_scatter(
            grad_table.astype(jnp.bfloat16), "fsdp", scatter_dimension=0, tiled=True
        ).astype(jnp.float32),
    )
    attn_parts = (
        lax.psum(attn_parts[0].astype(jnp.bfloat16), ("seq", "ctx")).astype(jnp.float32),
        lax.psum(attn_parts[1].astype(jnp.bfloat16), ("seq", "ctx")).astype(jnp.float32),
        lax.psum(attn_parts[2].astype(jnp.bfloat16), ("seq", "ctx")).astype(jnp.float32),
        lax.psum(attn_parts[3].astype(jnp.bfloat16), ("seq", "ctx")).astype(jnp.float32),
        lax.psum(attn_parts[4].astype(jnp.bfloat16), ("seq", "ctx")).astype(jnp.float32),
        lax.psum(attn_parts[5].astype(jnp.bfloat16), ("seq", "ctx")).astype(jnp.float32),
    )
    return (
        output,
        input_grad,
        attn_parts[0],
        attn_parts[1],
        attn_parts[2],
        attn_parts[3],
        attn_parts[4],
        attn_parts[5],
        ffn_parts[0],
        ffn_parts[1],
        ffn_parts[2],
    )


def solution(mesh):
    in_specs = (
        P(("seq", "fsdp"), "ctx", None),
        P(("seq", "fsdp"), None),
        P("fsdp", None),
        P("fsdp", None),
        P("fsdp", None),
        P(None, "fsdp"),
        P("fsdp"),
        P("fsdp", None),
        P("fsdp", None),
        P(None, "fsdp"),
        P("fsdp"),
        P(("seq", "fsdp"), "ctx", None),
    )
    out_specs = (
        P(("seq", "fsdp"), "ctx", None),
        P(("seq", "fsdp"), "ctx", None),
        P("fsdp", None),
        P("fsdp", None),
        P("fsdp", None),
        P(None, "fsdp"),
        P("fsdp"),
        P("fsdp", None),
        P("fsdp", None),
        P(None, "fsdp"),
        P("fsdp"),
    )
    fits = mesh.shape["seq"] == 2 and mesh.shape["ctx"] == 4 and mesh.shape["fsdp"] == 4
    per_device = fast_device if fits else general_device
    return jax.shard_map(
        per_device, mesh=mesh, in_specs=in_specs, out_specs=out_specs, check_vma=False
    )
```

```python
import functools
import math

import jax
import jax.numpy as jnp
from jax import lax
from jax.experimental import pallas as pl
from jax.experimental.pallas import tpu as pltpu
from jax.sharding import PartitionSpec as P

MESH = pl.DeviceIdType.MESH
F32 = jnp.float32
BF = jnp.bfloat16
EPS = 1e-06
BORDERS = (12, 16, 23, 32, 46, 64, 91)
LOG2E = math.log2(math.e)
T = 128


def dot_nn(a, b):
    return jnp.dot(a, b, preferred_element_type=F32)


def dot_nt(a, b):
    return lax.dot_general(a, b, (((1,), (1,)), ((), ())), preferred_element_type=F32)


def dot_tn(a, b):
    return lax.dot_general(a, b, (((0,), (0,)), ((), ())), preferred_element_type=F32)


def bucket_of(offset):
    magnitude = jnp.abs(offset)
    logbins = jnp.full_like(magnitude, 8)
    for border in BORDERS:
        logbins = logbins + jnp.where(magnitude >= border, 1, 0)
    return jnp.where(magnitude < 8, magnitude, logbins) + jnp.where(offset > 0, 16, 0)


def pick(values, index):
    return jnp.take_along_axis(values, index, axis=1, mode="promise_in_bounds")


class Place:
    def __init__(self, z_count):
        self.y = lax.axis_index("seq")
        self.ctx = lax.axis_index("ctx")
        self.z = lax.axis_index("fsdp")
        self.x = self.ctx // 2
        self.core = self.ctx % 2
        self.col = self.y * 2 + self.x
        self.z_count = z_count
        self.sib = (self.y, self.x * 2 + 1 - self.core, self.z)
        self.xn = (self.y, (1 - self.x) * 2 + self.core, self.z)
        self.yn = (1 - self.y, self.ctx, self.z)

    def zn(self, d):
        return (self.y, self.ctx, lax.rem(self.z + d, self.z_count))


def remote(src, dst, send, recv, device):
    return pltpu.make_async_remote_copy(
        src_ref=src, dst_ref=dst, send_sem=send, recv_sem=recv, device_id=device, device_id_type=MESH
    )


class Gather:
    def __init__(self, w, ssem, rsem, slot, lo, mid, hi, here, shard):
        self.w, self.ssem, self.rsem, self.slot = w, ssem, rsem, slot
        self.lo, self.mid, self.hi = lo, mid, hi
        self.here, self.shard, self.piece = here, shard, shard // 4

    def view(self, z, col, lo, hi):
        if self.mid is None:
            return self.w.at[pl.ds(pl.multiple_of(z * self.shard, 16), self.shard), pl.ds(lo, hi - lo)]
        first = pl.multiple_of(z * self.shard + col * self.piece, 16)
        return self.w.at[pl.ds(first, self.piece), pl.ds(lo, hi - lo)]

    def copy(self, kind, d, arriving):
        p = self.here
        zs = lax.rem(p.z + p.z_count - d, p.z_count)
        col_x, col_y, col_d = p.y * 2 + 1 - p.x, (1 - p.y) * 2 + p.x, (1 - p.y) * 2 + 1 - p.x
        index = kind * 3 + d - 1
        send, recv = self.ssem.at[self.slot, index], self.rsem.at[self.slot, index]
        if kind == 0:
            ref = self.view(zs if arriving else p.z, p.col, self.lo, self.hi)
            return remote(ref, ref, send, recv, p.zn(d))
        if kind == 1:
            ref = self.view(zs, col_x if arriving else p.col, self.lo, self.hi)
            return remote(ref, ref, send, recv, p.xn)
        if kind == 2:
            ref = self.view(zs, col_y if arriving else p.col, self.lo, self.hi)
            return remote(ref, ref, send, recv, p.yn)
        if kind == 3:
            ref = self.view(zs, col_d if arriving else col_x, self.lo, self.mid)
            return remote(ref, ref, send, recv, p.yn)
        ref = self.view(zs, col_d if arriving else col_y, self.mid, self.hi)
        return remote(ref, ref, send, recv, p.xn)

    def start(self):
        for d in (1, 3, 2):
            self.copy(0, d, False).start()

    def pass_z(self):
        for d in (1, 3, 2):
            self.copy(0, d, True).wait_recv()
            self.copy(1, d, False).start()
            self.copy(2, d, False).start()

    def pass_plane(self):
        for d in (1, 3, 2):
            self.copy(1, d, True).wait_recv()
            self.copy(3, d, False).start()
            self.copy(2, d, True).wait_recv()
            self.copy(4, d, False).start()

    def finish(self):
        for d in (1, 3, 2):
            if self.mid is None:
                self.copy(0, d, True).wait_recv()
            else:
                self.copy(3, d, True).wait_recv()
                self.copy(4, d, True).wait_recv()

    def drain(self):
        for kind in range(1 if self.mid is None else 5):
            for d in (1, 3, 2):
                self.copy(kind, d, False).wait_send()


class Swap:
    def __init__(self, source, whole, ssem, rsem, lsem, here, rows):
        self.source, self.whole, self.ssem, self.rsem, self.lsem = source, whole, ssem, rsem, lsem
        self.here, self.rows = here, rows

    def block(self, ctx):
        return self.whole.at[pl.ds(pl.multiple_of(ctx * self.rows, 16), self.rows)]

    def own(self):
        return pltpu.make_async_copy(self.source.at[self.here.x], self.block(self.here.ctx), self.lsem)

    def over(self, arriving):
        p = self.here
        ctx = (1 - p.x) * 2 + p.core if arriving else p.ctx
        return remote(self.source.at[1 - p.x], self.block(ctx), self.ssem.at[0], self.rsem.at[0], p.xn)

    def pair(self, arriving):
        p = self.here
        ctx = p.x * 2 + 1 - p.core if arriving else p.ctx
        return remote(self.source.at[p.x], self.block(ctx), self.ssem.at[1], self.rsem.at[1], p.sib)

    def forward(self, arriving):
        p = self.here
        ctx = (1 - p.x) * 2 + (1 - p.core if arriving else p.core)
        return remote(self.block(ctx), self.block(ctx), self.ssem.at[2], self.rsem.at[2], p.sib)

    def start(self):
        self.over(False).start()
        self.own().start()
        self.pair(False).start()

    def relay(self):
        self.over(True).wait_recv()
        self.forward(False).start()

    def finish(self):
        self.own().wait()
        self.pair(True).wait_recv()
        self.forward(True).wait_recv()

    def drain(self):
        self.over(False).wait_send()
        self.pair(False).wait_send()
        self.forward(False).wait_send()


def enter(partners):
    barrier = pltpu.get_barrier_semaphore()
    for partner in partners:
        pl.semaphore_signal(barrier, inc=1, device_id=partner, device_id_type=MESH)
    pl.semaphore_wait(barrier, len(partners))


class Reduce:
    def __init__(self, g, r1, r2, r3, r1z, r2z, rz, fin, gfin, ssem, rsem, lsem, here, z_first):
        self.g, self.r3, self.rz, self.fin, self.gfin = g, r3, rz, fin, gfin
        self.ones, self.twos = (r1z, r1), (r2z, r2)
        self.ssem, self.rsem, self.lsem, self.here, self.z_first = ssem, rsem, lsem, here, z_first
        self.width = g.shape[-1]
        self.lo = pl.ds(0, self.width // 2)
        self.hi = pl.ds(self.width // 2, self.width // 2)
        self.piece = g.shape[4]

    def rows_z(self, c):
        return pl.ds(self.here.z, 1) if c < self.z_first else pl.ds(0, self.here.z_count)

    def count(self, c):
        return 1 if c < self.z_first else self.here.z_count

    def r1(self, c):
        return self.ones[0].at[c] if c < self.z_first else self.ones[1].at[c - self.z_first]

    def r2(self, c):
        return self.twos[0].at[c] if c < self.z_first else self.twos[1].at[c - self.z_first]

    def link(self, c, index, src, dst, device):
        return remote(src, dst, self.ssem.at[c, index], self.rsem.at[c, index], device)

    def x1(self, c):
        p = self.here
        return self.link(c, 0, self.g.at[c, 1 - p.x, :, self.rows_z(c), :, self.lo], self.r1(c).at[0], p.xn)

    def y1(self, c):
        p = self.here
        return self.link(c, 1, self.g.at[c, :, 1 - p.y, self.rows_z(c), :, self.hi], self.r1(c).at[1], p.yn)

    def x2(self, c):
        p = self.here
        return self.link(c, 2, self.g.at[c, p.x, 1 - p.y, self.rows_z(c), :, self.lo], self.r2(c).at[0], p.yn)

    def y2(self, c):
        p = self.here
        return self.link(c, 3, self.g.at[c, 1 - p.x, p.y, self.rows_z(c), :, self.hi], self.r2(c).at[1], p.xn)

    def z1(self, c, d):
        p = self.here
        to = lax.rem(p.z + d, p.z_count)
        if c < self.z_first:
            return self.link(c, 3 + d, self.g.at[c, :, :, to], self.rz.at[c, d - 1], p.zn(d))
        return self.link(c, 3 + d, self.g.at[c, p.x, p.y, to], self.r3.at[c - self.z_first, d - 1], p.zn(d))

    def over_x(self, c, arriving):
        p = self.here
        col = p.y * 2 + 1 - p.x if arriving else p.col
        return self.link(c, 7, self.fin.at[c], self.gfin.at[p.core, c, col], p.xn)

    def over_y(self, c, arriving):
        p = self.here
        ref = self.gfin.at[p.core, c, pl.ds((1 - p.y if arriving else p.y) * 2, 2)]
        return self.link(c, 8, ref, ref, p.yn)

    def keep(self, c):
        return pltpu.make_async_copy(self.fin.at[c], self.gfin.at[self.here.core, c, self.here.col], self.lsem.at[c])

    def pair(self, c, arriving):
        core = 1 - self.here.core if arriving else self.here.core
        return self.link(c, 9, self.gfin.at[core, c], self.gfin.at[core, c], self.here.sib)

    def start(self, c):
        if c < self.z_first:
            for d in (1, 3, 2):
                self.z1(c, d).start()
        else:
            self.plane(c)

    def gathered_z(self, c):
        p = self.here
        for d in (1, 3, 2):
            self.z1(c, d).wait_recv()
        for x in range(2):
            for y in range(2):
                total = self.g[c, x, y, p.z].astype(F32)
                for d in range(3):
                    total = total + self.rz[c, d, x, y].astype(F32)
                self.g[c, x, y, p.z] = total.astype(BF)
        self.plane(c)

    def plane(self, c):
        self.x1(c).start()
        self.y1(c).start()

    def second(self, c):
        p = self.here
        h = self.width // 2

        def zi(k):
            return p.z if c < self.z_first else k

        self.x1(c).wait_recv()

        def add_x(k, carry):
            for y in range(2):
                self.g[c, p.x, y, zi(k), :, :h] = (
                    self.g[c, p.x, y, zi(k), :, :h].astype(F32) + self.r1(c)[0, y, k].astype(F32)
                ).astype(BF)
            return carry

        lax.fori_loop(0, self.count(c), add_x, 0)
        self.x2(c).start()
        self.y1(c).wait_recv()

        def add_y(k, carry):
            for x in range(2):
                self.g[c, x, p.y, zi(k), :, h:] = (
                    self.g[c, x, p.y, zi(k), :, h:].astype(F32) + self.r1(c)[1, x, k].astype(F32)
                ).astype(BF)
            return carry

        lax.fori_loop(0, self.count(c), add_y, 0)
        self.y2(c).start()

    def third(self, c):
        p = self.here
        h = self.width // 2
        self.x2(c).wait_recv()
        self.y2(c).wait_recv()
        if c < self.z_first:
            self.fin[c, :, :h] = (self.g[c, p.x, p.y, p.z, :, :h].astype(F32) + self.r2(c)[0, 0].astype(F32)).astype(BF)
            self.fin[c, :, h:] = (self.g[c, p.x, p.y, p.z, :, h:].astype(F32) + self.r2(c)[1, 0].astype(F32)).astype(BF)
            self.publish(c)
            return

        def add(k, carry):
            self.g[c, p.x, p.y, k, :, :h] = (
                self.g[c, p.x, p.y, k, :, :h].astype(F32) + self.r2(c)[0, k].astype(F32)
            ).astype(BF)
            self.g[c, p.x, p.y, k, :, h:] = (
                self.g[c, p.x, p.y, k, :, h:].astype(F32) + self.r2(c)[1, k].astype(F32)
            ).astype(BF)
            return carry

        lax.fori_loop(0, p.z_count, add, 0)
        for d in (1, 3, 2):
            self.z1(c, d).start()

    def fourth(self, c):
        if c < self.z_first:
            return
        p = self.here
        for d in (1, 3, 2):
            self.z1(c, d).wait_recv()
        total = self.g[c, p.x, p.y, p.z].astype(F32)
        for d in range(3):
            total = total + self.r3[c - self.z_first, d].astype(F32)
        self.fin[c] = total.astype(BF)
        self.publish(c)

    def publish(self, c):
        self.over_x(c, False).start()
        self.keep(c).start()

    def fifth(self, c):
        self.over_x(c, True).wait_recv()
        self.keep(c).wait()
        self.over_y(c, False).start()

    def sixth(self, c):
        self.over_y(c, True).wait_recv()
        self.pair(c, False).start()

    def last(self, c):
        self.pair(c, True).wait_recv()
        for copy in (self.x1(c), self.y1(c), self.x2(c), self.y2(c), self.over_x(c, False), self.over_y(c, False), self.pair(c, False)):
            copy.wait_send()
        for d in (1, 3, 2):
            self.z1(c, d).wait_send()


def edges():
    starts, buckets = [], [15]
    lows = (8,) + BORDERS
    for b in range(14, 7, -1):
        starts.append(1 - lows[b - 7])
        buckets.append(b)
    for n in range(7, -1, -1):
        starts.append(-n)
        buckets.append(n)
    for n in range(1, 8):
        starts.append(n)
        buckets.append(16 + n)
    for b in range(8, 16):
        starts.append(lows[b - 8])
        buckets.append(16 + b)
    return starts, buckets


def gelu_parts(v):
    c0 = math.sqrt(2.0 / math.pi)
    sq = v * v
    th = jnp.tanh(v * (c0 + (c0 * 0.044715) * sq))
    half = 0.5 + 0.5 * th
    slope = half + (0.5 * v) * (1.0 - th * th) * (c0 + (3.0 * 0.044715 * c0) * sq)
    return v * half, slope


def layer_kernel(
    inputs, positions, wq, wk, wv, wo_t, win, wout_t, extra_in, cotangent,
    out_ref, igrad_ref, gfin, evec_out, probs_out,
    w, x_all, cot_all, extra, n_t, turned, q, k, v, mixed, linv, table, pool, bound, ka, va, p_slot,
    y_in, t_in, o_send, o_in, slope, gmid, dk_acc, dv_acc, cat, stage, ig_in,
    hist, far_sum, gain_acc, e_src, e_in,
    g, r1, r2, r3, r1z, r2z, rz, fin,
    ssem, rsem, swap_s, swap_r, cot_s, cot_r, e_s, e_r, lsem, psem, y_s, y_r, t_s, t_r, o_s, o_r, out_s, out_r, u_s, u_r, ev_s, ev_r,
    g_s, g_r, g_l, osem,
):
    here = Place(lax.axis_size("fsdp"))
    p = here
    D, INNER = w.shape[0], wo_t.shape[1]
    half = INNER // 2
    ffh = win.shape[1] // 2
    shard = wq.shape[0]
    piece = shard // 4
    R = x_all.shape[0]
    heads = half // 64
    nt = R // T
    active = pool.at[:, pl.ds(0, ffh)]
    y_own = pool.at[:, pl.ds(ffh, D)]
    t_own = stage
    own_rows = pl.ds(pl.multiple_of(p.z * shard, 16), shard)
    half_cols = pl.ds(pl.multiple_of(p.core * half, 128), half)
    ff_cols = pl.ds(pl.multiple_of(p.core * ffh, 128), ffh)
    c_o, c_in, c_out, c_end = 3 * half, 4 * half, 4 * half + ffh, 4 * half + 2 * ffh

    loads = [
        pltpu.make_async_copy(wq.at[:, half_cols], w.at[own_rows, pl.ds(0, half)], lsem.at[0]),
        pltpu.make_async_copy(wk.at[:, half_cols], w.at[own_rows, pl.ds(half, half)], lsem.at[1]),
        pltpu.make_async_copy(wv.at[:, half_cols], w.at[own_rows, pl.ds(2 * half, half)], lsem.at[2]),
        pltpu.make_async_copy(win.at[:, ff_cols], w.at[own_rows, pl.ds(c_in, ffh)], lsem.at[3]),
        pltpu.make_async_copy(wo_t.at[:, half_cols], w.at[own_rows, pl.ds(c_o, half)], lsem.at[4]),
        pltpu.make_async_copy(wout_t.at[:, ff_cols], w.at[own_rows, pl.ds(c_out, ffh)], lsem.at[5]),
        pltpu.make_async_copy(extra_in, extra.at[own_rows], lsem.at[6]),
    ]
    for load in loads:
        load.start()
    enter([p.sib, p.xn, p.yn, p.zn(1), p.zn(2), p.zn(3)])
    swap = Swap(inputs, x_all, swap_s, swap_r, lsem.at[7], here, inputs.shape[1])
    swap.start()
    cot_swap = Swap(cotangent, cot_all, cot_s, cot_r, lsem.at[8], here, inputs.shape[1])

    def extra_copy(d, arriving):
        zs = lax.rem(p.z + p.z_count - d, p.z_count) if arriving else p.z
        ref = extra.at[pl.ds(pl.multiple_of(zs * shard, 16), shard)]
        return remote(ref, ref, e_s.at[d - 1], e_r.at[d - 1], p.zn(d))

    loads[6].wait()
    for d in (1, 3, 2):
        extra_copy(d, False).start()
    tracks = [(n * half, n * half + 2 * T, (n + 1) * half) for n in range(3)] + [(c_o, c_o + 2 * T, c_in)]
    tracks += [(lo, lo + 3 * T, lo + 4 * T) for lo in range(c_in, c_end - 4 * T, 4 * T)] + [(c_end - 4 * T, None, c_end)]
    gathers = [Gather(w, ssem, rsem, n, lo, mid, hi, here, shard) for n, (lo, mid, hi) in enumerate(tracks)]
    for n in range(3):
        loads[n].wait()
        gathers[n].start()
    for n in range(3, 6):
        loads[n].wait()
    for gather in gathers[3:]:
        gather.start()

    starts, classes = edges()
    lane = lax.broadcasted_iota(jnp.int32, (1, T), 1)
    pos = positions[pl.ds(p.x, 1), :]
    band = [(a, d) for a in range(nt) for d in range(3) if 0 <= a + d - 1 < nt]
    cols = {}
    early = {
        36: [gathers[0].pass_plane, gathers[1].pass_plane],
        40: [swap.relay],
        34: [gathers[1].pass_z, gathers[2].pass_z],
        43: [gathers[2].pass_plane],
        23: [gathers[0].pass_z],
        44: [gathers[3].pass_z, gathers[4].pass_z],
    }

    def offsets(a, d):
        if a not in cols:
            cols[a] = jnp.broadcast_to(pos[:, a * T : (a + 1) * T], (T, T)).T
        return pos[:, (a + d - 1) * T : (a + d) * T] - cols[a]

    edge = jnp.full((1, T), -(2**20), jnp.int32)
    for j, first in enumerate(starts):
        edge = jnp.where(lane == j, first, edge)
    ranks = {}

    def ranks_of(b):
        if b not in ranks:
            offsets(b, 1)
            base = pos[:, b * T : b * T + 1]
            above = cols[b] - base
            ranks[b] = base, [
                jnp.broadcast_to(jnp.sum(jnp.where(above < lane + m * T, 1.0, 0.0), axis=0, keepdims=True), (T, T)) for m in range(2)
            ]
        return ranks[b]

    for n, (a, d) in enumerate(band):
        for step in early.get(n, ()):
            step()
        offsets(a, 1)
        base, (low, high) = ranks_of(a + d - 1)
        at = jnp.clip(cols[a] + edge - base, 0, 2 * T - 1)
        count = jnp.where(at < T, pick(low, jnp.minimum(at, T - 1)), pick(high, jnp.maximum(at - T, 0)))
        bound[a * T : (a + 1) * T, d * T : (d + 1) * T] = count.astype(jnp.int32) - 1

    for d in (1, 3, 2):
        extra_copy(d, True).wait_recv()
    buckets_per = 8
    rows = [extra[zs * shard : zs * shard + 16, :].astype(F32)[:buckets_per] for zs in range(4)]
    flat = jnp.concatenate(rows + [jnp.zeros((T - 32, T), F32)], axis=0)
    table[...] = flat.T
    gains = jnp.concatenate(
        [extra[t * T : (t + 1) * T, :].astype(F32).T[0:8] for t in range(D // T)], axis=1
    )
    gain_one, gain_two = gains[0:1], gains[1:2]
    for n, (a, d) in enumerate(band):
        for step in early.get(len(band) + n, ()):
            step()
        idx = bucket_of(offsets(a, d))
        for h in range(heads):
            tab = jnp.broadcast_to(table[pl.ds(2 + p.core * heads + h, 1), :], (T, T))
            pool[a * T : (a + 1) * T, (h * 3 + d) * T : (h * 3 + d + 1) * T] = pick(tab, idx).astype(BF)
    for step in early.get(2 * len(band), ()):
        step()

    swap.finish()
    for c in range(4):
        rows = slice(c * (R // 4), (c + 1) * (R // 4))
        xf = x_all[rows, :].astype(F32)
        scale = lax.rsqrt(jnp.mean(xf * xf, axis=1, keepdims=True) + EPS)
        stage[rows, :] = (xf * scale * gain_one).astype(BF)
        n_t[:, rows] = (xf * scale * gain_one).T.astype(BF)
    for gather in gathers[:3]:
        gather.finish()

    def project(c, carry):
        rows = pl.ds(pl.multiple_of(c * 256, 256), 256)
        for n, dest in enumerate((q, k, v)):
            out = dot_nn(stage[rows, :], w[:, n * half : (n + 1) * half]).astype(BF)
            for pair in range(half // T):
                dest[pair, rows, :] = out[:, pair * T : (pair + 1) * T]
        return carry

    lax.fori_loop(0, R // 256, project, 0)

    QT = 256
    sub = QT // T
    units = R // QT
    ahead = {
        1: [gathers[5].pass_z],
        3: [gathers[6].pass_z],
        5: [gathers[4].pass_plane],
        13: [cot_swap.relay, gathers[8].pass_z],
        4: [gathers[3].pass_plane, gathers[5].pass_plane],
        6: [gathers[6].pass_plane, cot_swap.start],
        8: [gathers[7].pass_z],
    }
    for step in ahead.get(-1, ()):
        step()

    def halves(h, lanes):
        return ((lanes < 64), lanes - 64) if h == 0 else ((lanes >= 64), lanes)

    def pair_step(hp, carry):
        lane_k = lax.broadcasted_iota(jnp.int32, (R, T), 1)
        tile_k = lax.broadcasted_iota(jnp.int32, (R, T), 0) // T
        for h in range(2):
            tab = table[pl.ds(2 + p.core * heads + hp * 2 + h, 1), :]
            inside, other = halves(h, lane_k)
            far = jnp.where(tile_k < other - 1, tab[:, 15:16], jnp.where(tile_k > other + 1, tab[:, 31:32], 0.0))
            far = jnp.where(other < nt, far, 0.0)
            ka[h] = jnp.where(inside, k[hp].astype(F32), far).astype(BF)
            va[h] = jnp.where(inside, v[hp].astype(F32), 1.0).astype(BF)
        lane_q = lax.broadcasted_iota(jnp.int32, (QT, T), 1)
        tile_q = lax.broadcasted_iota(jnp.int32, (QT, T), 0) // T
        for qi in range(units):
            for trip in range(heads // 2):
                if trip * units + qi in ahead:
                    pl.when(hp == trip)(lambda todo=ahead[trip * units + qi]: [step() for step in todo] and None)
            store = pltpu.make_async_copy(p_slot.at[qi % 2], probs_out.at[hp, :, pl.ds(qi * QT, QT)], psem.at[qi % 2])
            if qi < 2:
                pl.when(hp > 0)(store.wait)
            else:
                store.wait()
            rows = slice(qi * QT, (qi + 1) * QT)
            scores = []
            for h in range(2):
                inside, other = halves(h, lane_q)
                hot = jnp.where(other == tile_q + qi * sub, 1.0, 0.0)
                qm = jnp.where(inside, q[hp, rows, :].astype(F32), hot).astype(BF)
                scores.append(dot_nt(qm, ka[h]))
            mixes = []
            for h in range(2):
                strips = []
                for si in range(sub):
                    a = qi * sub + si
                    st = scores[h][si * T : (si + 1) * T]
                    lo, hi = max(a - 1, 0), min(a + 2, nt)
                    parts = [st[:, : lo * T]] if lo > 0 else []
                    lanes = pl.ds(pl.multiple_of((hp * 2 + h) * 3 * T + (lo - a + 1) * T, T), (hi - lo) * T)
                    near = pool[a * T : (a + 1) * T, lanes]
                    parts.append(st[:, lo * T : hi * T] + near.astype(F32))
                    if hi < nt:
                        parts.append(st[:, hi * T :])
                    strips.append(jnp.concatenate(parts, axis=1))
                sc = jnp.concatenate(strips, axis=0)
                m = jnp.max(sc, axis=1, keepdims=True)
                pb = jnp.exp2((sc - m) * LOG2E).astype(BF)
                p_slot[qi % 2, h] = pb
                mixes.append(dot_nn(pb, va[h]))
            store.start()
            o = jnp.where(lane < 64, mixes[0], mixes[1])
            total = pltpu.roll(jnp.where(lane < 64, mixes[1], mixes[0]), 64, 1)
            inv = 1.0 / total
            mixed[hp, rows, :] = (o * inv).astype(BF)
            linv[hp, rows, :] = inv
        return carry

    lax.fori_loop(0, heads // 2, pair_step, 0)
    for slot in range(2):
        pltpu.make_async_copy(p_slot.at[slot], probs_out.at[0, :, pl.ds(0, QT)], psem.at[slot]).wait()

    B = 256
    blocks = R // B
    FW = 512
    for step in ahead.get(3 * units, ()):
        step()
    for gather in gathers[3:7]:
        gather.finish()

    def y_copy(i, arriving=False):
        rows = pl.ds(pl.multiple_of(i * B, B), B)
        return remote(y_own.at[rows], y_in.at[rows], y_s.at[i], y_r.at[i], p.sib)

    def t_copy(i):
        rows = pl.ds(pl.multiple_of(i * B, B), B)
        return remote(t_own.at[rows], t_in.at[rows], t_s.at[i], t_r.at[i], p.sib)

    def o_copy(n):
        return remote(o_send.at[n], o_in.at[n], o_s.at[n], o_r.at[n], p.sib)

    def project_out(i, carry):
        rows = pl.ds(pl.multiple_of(i * B, B), B)
        mx = jnp.concatenate([mixed[pair, rows, :] for pair in range(half // T)], axis=1)
        y_own[rows, :] = dot_nt(mx, w[:, c_o : c_o + half]).astype(BF)
        y_copy(i).start()
        return carry

    lax.fori_loop(0, blocks, project_out, 0)
    for step in ahead.get(3 * units + 1, ()):
        step()

    def middle_of(rows):
        mid = x_all[rows, :].astype(F32) + (y_own[rows, :].astype(F32) + y_in[rows, :].astype(F32))
        return mid, lax.rsqrt(jnp.mean(mid * mid, axis=1, keepdims=True) + EPS)

    red = Reduce(g, r1, r2, r3, r1z, r2z, rz, fin, gfin, g_s, g_r, g_l, here, 2)
    between = {
        1: [gathers[7].pass_plane],
        3: [gathers[8].pass_plane],
    }

    def during(i, base, table):
        for n in range(blocks):
            if base + n in table:
                pl.when(i == n)(lambda todo=table[base + n]: [step() for step in todo] and None)

    def ffn_in(i, carry):
        rows = pl.ds(pl.multiple_of(i * B, B), B)
        y_copy(i).wait_recv()
        mid, scale = middle_of(rows)
        n2f = mid * scale * gain_two
        n2 = n2f.astype(BF)
        stage[rows, :] = n2
        for j in range(ffh // FW):
            hidden = dot_nn(n2, w[:, c_in + j * FW : c_in + (j + 1) * FW])
            act, slo = gelu_parts(hidden)
            active[rows, j * FW : (j + 1) * FW] = act.astype(BF)
            slope[rows, j * FW : (j + 1) * FW] = slo.astype(BF)
        during(i, 0, between)
        return carry

    lax.fori_loop(0, blocks, ffn_in, 0)
    cot_swap.finish()
    for i in range(blocks):
        rows = slice(i * B, (i + 1) * B)
        turned[:, rows] = cot_all[rows, :].astype(F32).T.astype(BF)


    def keep_pieces(c, lo, left, right):
        for n in range(0, right.shape[1], 2 * T):
            value = dot_nn(left, right[:, n : n + 2 * T])
            for zs in range(p.z_count):
                for col in range(4):
                    first_row = zs * shard + col * piece
                    g[c, col % 2, col // 2, zs, :, lo + n : lo + n + value.shape[1]] = value[first_row : first_row + piece].astype(BF)

    for c in range(ffh // FW):
        keep_pieces(c, 0, turned[...], active[:, c * FW : (c + 1) * FW])
        red.start(c)
        for step in between.get(4 + c, ()):
            step()
    for i in range(blocks):
        rows = slice(i * B, (i + 1) * B)
        turned[:, rows] = stage[rows, :].astype(F32).T.astype(BF)
    for gather in gathers[7:]:
        gather.finish()
    later = {
        2: [functools.partial(red.second, 2)],
        9: [functools.partial(red.second, 3)],
    }

    def ffn_back(i, carry):
        rows = pl.ds(pl.multiple_of(i * B, B), B)
        cot = cot_all[rows, :]
        for j in range(ffh // FW):
            grad = dot_nn(cot, w[:, c_out + j * FW : c_out + (j + 1) * FW])
            cols = slice(j * FW, (j + 1) * FW)
            slope[rows, cols] = (grad * slope[rows, cols].astype(F32)).astype(BF)
        t_own[rows, :] = dot_nt(slope[rows, :], w[:, c_in:c_out]).astype(BF)
        t_copy(i).start()
        o = dot_nt(active[rows, :], w[:, c_out:c_end])
        n = i // 2

        @pl.when(i % 2 == p.core)
        def _():
            gmid[n] = o

        @pl.when(i % 2 != p.core)
        def _():
            o_send[n] = o.astype(BF)
            o_copy(n).start()

        during(i, 0, later)
        return carry

    lax.fori_loop(0, blocks, ffn_back, 0)
    for c in range(ffh // FW):
        keep_pieces(3 + c, 0, turned[...], slope[:, c * FW : (c + 1) * FW])
        for step in later.get(4 + c, ()):
            step()
        red.start(3 + c)

    gain_acc[...] = jnp.zeros_like(gain_acc)

    def back_middle(i, carry):
        rows = pl.ds(pl.multiple_of(i * B, B), B)
        t_copy(i).wait_recv()
        mid, scale = middle_of(rows)
        t = t_own[rows, :].astype(F32) + t_in[rows, :].astype(F32)
        tg = t * gain_two
        dot = jnp.mean(tg * mid, axis=1, keepdims=True)
        gm = cot_all[rows, :].astype(F32) + scale * tg - (scale * scale * scale * dot) * mid
        gy = gm.astype(BF)
        turned[:, rows] = gm.T.astype(BF)
        grad = dot_nn(gy, w[:, c_o : c_o + half])
        for pair in range(half // T):
            slope[rows, D + pair * T : D + (pair + 1) * T] = (grad[:, pair * T : (pair + 1) * T] * linv[pair, rows, :]).astype(BF)
        n = i // 2

        @pl.when(i % 2 == p.core)
        def _():
            gain_acc[1:2, :] += jnp.sum(t * mid * scale, axis=0, keepdims=True)
            o_copy(n).wait_recv()
            slope[pl.ds(pl.multiple_of(n * B, B), B), :D] = (mid + gmid[n] + o_in[n].astype(F32)).astype(BF)
            gmid[n] = gm

        during(i, 7, later)
        return carry

    lax.fori_loop(0, blocks, back_middle, 0)
    out_own = pltpu.make_async_copy(slope.at[pl.ds(pl.multiple_of(p.x * B, B), B), pl.ds(0, D)], out_ref.at[p.x], osem.at[0])
    out_over = remote(slope.at[pl.ds(pl.multiple_of((1 - p.x) * B, B), B), pl.ds(0, D)], out_ref.at[p.x], out_s.at[0], out_r.at[0], p.xn)
    out_there = remote(slope.at[pl.ds(pl.multiple_of((1 - p.x) * B, B), B), pl.ds(0, D)], out_ref.at[1 - p.x], out_s.at[0], out_r.at[0], p.xn)
    out_own.start()
    out_over.start()

    hist[...] = jnp.zeros_like(hist)
    far_sum[...] = jnp.zeros_like(far_sum)
    row_i = lax.broadcasted_iota(jnp.int32, (2 * T, 2 * T), 0)
    col_i = lax.broadcasted_iota(jnp.int32, (2 * T, 2 * T), 1)
    upto_incl = jnp.where(jnp.logical_and(row_i <= col_i, row_i // T == col_i // T), 1.0, 0.0).astype(BF)
    skip_left, skip_right = 96, 32

    def p_load(hp, qi):
        return pltpu.make_async_copy(probs_out.at[hp, :, pl.ds(qi * QT, QT)], p_slot.at[qi % 2], psem.at[qi % 2])

    p_load(0, 0).start()
    stages = {
        4: [functools.partial(red.second, 4)],
        5: [functools.partial(red.gathered_z, 0)],
        6: [functools.partial(red.third, 2)],
        7: [functools.partial(red.third, 3)],
        8: [functools.partial(red.second, 6), functools.partial(red.fourth, 2), functools.partial(red.third, 4), functools.partial(red.second, 5)],
        11: [functools.partial(red.fourth, 3), functools.partial(red.second, 7), functools.partial(red.second, 0)],
    }

    def lanes_of(m, hp):
        return pl.ds(pl.multiple_of(m * half + hp * T, T), T)

    def pair_back(hp, carry):
        lane_k = lax.broadcasted_iota(jnp.int32, (R, T), 1)
        tile_k = lax.broadcasted_iota(jnp.int32, (R, T), 0) // T
        for h in range(2):
            inside = (lane_k < 64) if h == 0 else (lane_k >= 64)
            other = lane_k - 64 if h == 0 else lane_k
            va[h] = jnp.where(inside, v[hp].astype(F32), jnp.where(other < 3, 1.0, 0.0)).astype(BF)
            ka[h] = jnp.where(inside, k[hp].astype(F32), jnp.where(other == tile_k, 1.0, 0.0)).astype(BF)
        dk_acc[...] = jnp.zeros_like(dk_acc)
        dv_acc[...] = jnp.zeros_like(dv_acc)
        lane_q = lax.broadcasted_iota(jnp.int32, (QT, T), 1)
        tile_q = lax.broadcasted_iota(jnp.int32, (QT, T), 0) // T
        for qi in range(units):
            for trip in range(heads // 2):
                if trip * units + qi in stages:
                    pl.when(hp == trip)(lambda todo=stages[trip * units + qi]: [step() for step in todo] and None)
            rows = slice(qi * QT, (qi + 1) * QT)
            p_load(hp, qi).wait()
            if qi + 1 < units:
                p_load(hp, qi + 1).start()
            else:
                pl.when(hp < heads // 2 - 1)(lambda: p_load(hp + 1, 0).start())
            do = slope[rows, pl.ds(pl.multiple_of(D + hp * T, T), T)].astype(F32)
            prod = do * mixed[hp, rows, :].astype(F32)
            qf = q[hp, rows, :].astype(F32)
            dps, dms, qms, dqs, grads = [], [], [], [], []
            for h in range(2):
                inside, other = halves(h, lane_q)
                rd = jnp.sum(jnp.where(inside, prod, 0.0), axis=1, keepdims=True)
                ra = rd.astype(BF).astype(F32)
                rb = (rd - ra).astype(BF).astype(F32)
                rc = rd - ra - rb
                dm = jnp.where(inside, do, 0.0)
                da = (dm - jnp.where(other == 0, ra, jnp.where(other == 1, rb, jnp.where(other == 2, rc, 0.0)))).astype(BF)
                dms.append(dm.astype(BF))
                qms.append(jnp.where(inside, qf, 0.0).astype(BF))
                dps.append(dot_nt(da, va[h]))
            for h in range(2):
                pb = p_slot[qi % 2, h]
                ds = (pb.astype(F32) * dps[h]).astype(BF)
                grads.append(ds)
                dqs.append(dot_nn(ds, ka[h]))
                dv_acc[...] += dot_tn(dms[h], pb)
                dk_acc[...] += dot_tn(qms[h], ds)
            cat[rows, lanes_of(0, hp)] = jnp.where(lane < 64, dqs[0], dqs[1]).astype(BF)
            in_tile = lax.broadcasted_iota(jnp.int32, (QT, T), 0) % T
            tile = tile_q + qi * sub
            for h in range(2):
                ds = grads[h]
                inside, other = halves(h, lane_q)
                spare = jnp.where(inside, 0.0, dqs[h])
                left = jnp.logical_or(other < tile - 1, jnp.logical_and(other == tile - 1, in_tile >= skip_left))
                right = jnp.logical_or(other > tile + 1, jnp.logical_and(other == tile + 1, in_tile < skip_right))
                for m, cond in enumerate((left, jnp.logical_and(right, other < nt), other < nt)):
                    far_sum[hp * 2 + h, m : m + 1, :] += jnp.sum(jnp.where(cond, spare, 0.0), axis=0, keepdims=True)
                found = jnp.zeros((8, T), F32)
                first_lane = min(max(qi * sub - 1, 0), nt - 4) * T
                sums_all = [dot_nn(ds[:, first_lane + m * 2 * T : first_lane + (m + 1) * 2 * T], upto_incl) for m in range(2)]
                for si in range(sub):
                    a = qi * sub + si
                    for d in range(3):
                        b = a + d - 1
                        if 0 <= b < nt:
                            r0, r1_ = (0, skip_left) if d == 0 else ((skip_right, T) if d == 2 else (0, T))
                            lane0 = b * T - first_lane
                            sums = sums_all[lane0 // (2 * T)][si * T + r0 : si * T + r1_, lane0 % (2 * T) : lane0 % (2 * T) + T]
                            idx = bound[a * T + r0 : a * T + r1_, d * T : (d + 1) * T]
                            got = jnp.where(idx >= 0, pick(sums, jnp.maximum(idx, 0)), 0.0)
                            found = found + jnp.sum(got.reshape((r1_ - r0) // 8, 8, T), axis=0)
                hist[hp * 2 + h] += found
        cat[:, lanes_of(1, hp)] = dk_acc[...].T.astype(BF)
        cat[:, lanes_of(2, hp)] = dv_acc[...].T.astype(BF)
        c = 6 + hp
        pair_qk = jnp.concatenate([cat[:, lanes_of(0, hp)], cat[:, lanes_of(1, hp)]], axis=1)
        keep_pieces(c, 0, n_t[...], pair_qk)
        keep_pieces(c, 2 * T, n_t[...], cat[:, lanes_of(2, hp)])
        keep_pieces(c, 3 * T, turned[...], mixed[hp])
        for trip in range(heads // 2):
            pl.when(hp == trip)(functools.partial(red.start, 6 + trip))
        return carry

    lax.fori_loop(0, heads // 2, pair_back, 0)

    def u_copy(n):
        return remote(slope.at[pl.ds((2 + n) * B, B), pl.ds(0, D)], o_in.at[2 + n], u_s.at[n], u_r.at[n], p.sib)

    for n in range(2):
        rows = pl.ds(pl.multiple_of((2 * n + 1 - p.core) * B, B), B)
        slope[(2 + n) * B : (3 + n) * B, :D] = dot_nt(cat[rows, :], w[:, :c_o]).astype(BF)
        u_copy(n).start()
    red.fifth(2)
    red.fifth(3)
    red.fourth(4)
    red.third(6)
    for n in range(2):
        rows = pl.ds(pl.multiple_of((2 * n + p.core) * B, B), B)
        t = dot_nt(cat[rows, :], w[:, :c_o])
        u_copy(n).wait_recv()
        t = t + o_in[2 + n].astype(F32)
        xf = x_all[rows, :].astype(F32)
        scale = lax.rsqrt(jnp.mean(xf * xf, axis=1, keepdims=True) + EPS)
        tg = t * gain_one
        dot = jnp.mean(tg * xf, axis=1, keepdims=True)
        gmid[n] = gmid[n] + scale * tg - (scale * scale * scale * dot) * xf
        gain_acc[0:1, :] += jnp.sum(t * xf * scale, axis=0, keepdims=True)
    ig_own = pltpu.make_async_copy(gmid.at[p.x], igrad_ref.at[p.x], osem.at[1])
    ig_own.start()
    slope[:B, D:] = gmid[1 - p.x].astype(BF)
    ig_over = remote(slope.at[pl.ds(0, B), pl.ds(D, D)], ig_in, out_s.at[1], out_r.at[1], p.xn)

    gains_rows = [gain_acc[m : m + 1, t * T : (t + 1) * T] for m in range(2) for t in range(D // T)]
    class_of = jnp.zeros((1, T), jnp.int32)
    for j, bkt in enumerate(classes):
        class_of = jnp.where(lane == bkt, j, class_of)
    used = jnp.logical_and(lane < 32, lane != 16)
    rows_h = []
    for h in range(heads):
        upto = jnp.sum(hist[h], axis=0, keepdims=True)
        sums = jnp.sum(far_sum[h], axis=1, keepdims=True)
        left, right, every = sums[0:1], sums[1:2], sums[2:3]
        near = every - left - right
        n_edges = len(starts)
        upto = jnp.where(lane < n_edges, upto, jnp.where(lane == n_edges, near, 0.0))
        below = jnp.where(lane == 0, 0.0, pltpu.roll(upto, 1, 1))
        per = upto - below + jnp.where(lane == 0, left, jnp.where(lane == n_edges, right, 0.0))
        rows_h.append(per)
    heads_rows = jnp.concatenate(rows_h + [jnp.zeros((8 - heads, T), F32)], axis=0)
    picked = jnp.take_along_axis(heads_rows, jnp.broadcast_to(class_of, (8, T)), axis=1)
    picked = jnp.where(used, picked, 0.0)[:heads]
    zero = jnp.zeros((heads, T), F32)
    first_half = jnp.where(p.core == 0, picked, zero)
    other_half = jnp.where(p.core == 0, zero, picked)
    e_src[0] = jnp.concatenate(gains_rows + [first_half, other_half], axis=0)

    def e_copy(n):
        device = (p.sib, p.xn, p.yn, p.zn(1), p.zn(2), p.zn(3))[n]
        return remote(e_src.at[min(n, 3)], e_in.at[n], ev_s.at[n], ev_r.at[n], device)

    ig_over.start()
    e_copy(0).start()
    e_copy(0).wait_recv()
    e_src[1] = e_src[0] + e_in[0]
    e_copy(1).start()
    red.third(5)
    red.third(0)
    red.fifth(4)
    red.gathered_z(1)
    red.sixth(2)
    red.second(8)
    red.fourth(6)
    red.third(7)
    e_copy(1).wait_recv()
    e_src[2] = e_src[1] + e_in[1]
    e_copy(2).start()
    red.sixth(3)
    red.fourth(7)
    e_copy(2).wait_recv()
    e_src[3] = e_src[2] + e_in[2]
    e_copy(3).start()
    e_copy(4).start()
    e_copy(5).start()
    red.fifth(0)
    red.fourth(5)
    red.second(1)
    red.third(8)
    red.fifth(6)
    red.fifth(7)
    red.fifth(5)
    red.third(1)
    red.sixth(6)
    red.fourth(8)
    red.fifth(1)
    red.sixth(7)
    red.fifth(8)
    red.sixth(5)
    red.sixth(0)
    red.sixth(1)
    red.sixth(4)
    red.sixth(8)
    for n in range(3, 6):
        e_copy(n).wait_recv()
    e_src[4] = e_src[3] + e_in[3] + e_in[4] + e_in[5]
    ev_out = pltpu.make_async_copy(e_src.at[4], evec_out, osem.at[2])
    ev_out.start()
    ig_over.wait_recv()
    ig_own.wait()
    gmid[0] = ig_in[...].astype(F32)
    ig_there = pltpu.make_async_copy(gmid.at[0], igrad_ref.at[1 - p.x], osem.at[1])
    ig_there.start()
    out_own.wait()
    out_there.wait_recv()
    for c in range(g.shape[0]):
        red.last(c)
    for i in range(blocks):
        y_copy(i).wait_send()
        t_copy(i).wait_send()
    for n in range(2):
        o_copy(n).wait_send()
        u_copy(n).wait_send()
    out_over.wait_send()
    ig_over.wait_send()
    for n in range(6):
        e_copy(n).wait_send()
    for gather in gathers:
        gather.drain()
    swap.drain()
    cot_swap.drain()
    for d in (1, 3, 2):
        extra_copy(d, False).wait_send()
    ev_out.wait()
    ig_there.wait()


def layer(inputs, positions, wq, wk, wv, wo_t, win, wout_t, extra_in, cotangent):
    D, INNER, FF = win.shape[0] * lax.axis_size("fsdp"), wo_t.shape[1], win.shape[1]
    half, ffh, shard = INNER // 2, FF // 2, wq.shape[0]
    B = inputs.shape[1]
    R = inputs.shape[0] * B * 2
    heads, pairs = half // 64, half // T
    width = 4 * half + 2 * ffh
    piece, FW = shard // 4, 512
    nc = width // FW
    zf = 2
    sds = jax.ShapeDtypeStruct
    any_ = pl.BlockSpec(memory_space=pl.ANY)
    vm = pl.BlockSpec(memory_space=pltpu.VMEM)
    sem = pltpu.SemaphoreType.DMA
    V = pltpu.VMEM
    return pl.pallas_call(
        layer_kernel,
        in_specs=[any_, vm] + [any_] * 8,
        out_specs=[any_] * 5,
        out_shape=[
            sds(inputs.shape, BF), sds(inputs.shape, F32), sds((2, nc, 4, piece, FW), BF), sds((24, T), F32), sds((pairs, 2, R, R), BF),
        ],
        scratch_shapes=[
            V((D, width), BF), V((R, D), BF), V((R, D), BF), V((D, T), BF), V((D, R), BF), V((D, R), BF),
            V((pairs, R, T), BF), V((pairs, R, T), BF), V((pairs, R, T), BF), V((pairs, R, T), BF), V((pairs, R, T), F32), V((T, T), F32),
            V((R, heads * 3 * T), BF), V((R, 3 * T), jnp.int32),
            V((2, R, T), BF), V((2, R, T), BF), V((2, 2, 256, R), BF),
            V((R, D), BF), V((R, D), BF), V((2, B, D), BF), V((4, B, D), BF),
            V((R, ffh), BF), V((2, B, D), F32), V((T, R), F32), V((T, R), F32),
            V((R, 3 * half), BF), V((R, D), BF), V((B, D), BF),
            V((heads, 8, T), F32), V((heads, 8, T), F32), V((8, D), F32), V((5, 24, T), F32), V((6, 24, T), F32),
            V((nc, 2, 2, 4, piece, FW), BF), V((nc - zf, 2, 2, 4, piece, FW // 2), BF), V((nc - zf, 2, 4, piece, FW // 2), BF),
            V((nc - zf, 3, piece, FW), BF), V((zf, 2, 2, 1, piece, FW // 2), BF), V((zf, 2, 1, piece, FW // 2), BF),
            V((zf, 3, 2, 2, piece, FW), BF), V((nc, piece, FW), BF),
            sem((10, 15)), sem((10, 15)), sem((3,)), sem((3,)), sem((3,)), sem((3,)), sem((3,)), sem((3,)), sem((12,)), sem((2,)),
            sem((4,)), sem((4,)), sem((4,)), sem((4,)), sem((2,)), sem((2,)), sem((2,)), sem((2,)), sem((2,)), sem((2,)), sem((6,)), sem((6,)),
            sem((nc, 10)), sem((nc, 10)), sem((nc,)), sem((3,)),
        ],
        compiler_params=pltpu.CompilerParams(collective_id=0, has_side_effects=True, vmem_limit_bytes=63 * 2**20),
        name="layer",
    )(inputs, positions, wq, wk, wv, wo_t, win, wout_t, extra_in, cotangent)


def finish_kernel(gfin, out_in, ig_in, wq, wk, wv, wo_t, win, wout_t, out, ig, gv, fa, fw, ob, ib, lsem, osem):
    cores, chunks, cols, piece, width = gv.shape
    half, third = fa.shape[2] // 2, fw.shape[2] // 2
    order = [(part, core) for part in range(3) for core in range(cores)]
    loads = [
        pltpu.make_async_copy(gfin.at[core, pl.ds(part * 3, 3)], gv.at[core, pl.ds(part * 3, 3)], lsem.at[n])
        for n, (part, core) in enumerate(order)
    ]
    through = [
        (pltpu.make_async_copy(a, b, lsem.at[len(order) + n]), pltpu.make_async_copy(b, c, osem.at[n]))
        for n, (a, b, c) in enumerate(((ig_in, ib, ig), (out_in, ob, out)))
    ]
    loads[0].start()
    for load, _ in through:
        load.start()
    for load in loads[1:]:
        load.start()
    stores = []
    for n, (part, core) in enumerate(order):
        loads[n].wait()

        def widen(col, carry):
            rows = pl.ds(pl.multiple_of(col * piece, 16), piece)
            for c in range(3):
                value = gv[core, part * 3 + c, col].astype(F32)
                if part < 2:
                    first = core * third + c * width
                    fw[part, rows, first : first + width] = value
                else:
                    first = core * half + c * T
                    for m in range(4):
                        fa[m, rows, first : first + T] = value[:, m * T : (m + 1) * T]
            return carry

        lax.fori_loop(0, cols, widen, 0)
        if part < 2:
            lanes = pl.ds(core * third, third)
            stores.append(pltpu.make_async_copy(fw.at[part, :, lanes], (wout_t, win)[part].at[:, lanes], osem.at[2 + n]))
            stores[-1].start()
        if n == 0:
            for load, store in through:
                load.wait()
                store.start()
                stores.append(store)
    for m, ref in enumerate((wq, wk, wv, wo_t)):
        stores.append(pltpu.make_async_copy(fa.at[m], ref, osem.at[6 + m]))
        stores[-1].start()
    for store in stores:
        store.wait()


def finish(gfin, out, igrad):
    cores, chunks, cols, piece, width = gfin.shape
    shard, d, ff = cols * piece, cols * piece * 4, cores * 3 * width
    sds = jax.ShapeDtypeStruct
    any_ = pl.BlockSpec(memory_space=pl.ANY)
    return pl.pallas_call(
        finish_kernel,
        in_specs=[any_] * 3,
        out_specs=[any_] * 8,
        out_shape=[sds((shard, d), F32)] * 4 + [sds((shard, ff), F32)] * 2 + [sds(out.shape, BF), sds(igrad.shape, F32)],
        scratch_shapes=[
            pltpu.VMEM(gfin.shape, BF), pltpu.VMEM((4, shard, d), F32), pltpu.VMEM((2, shard, ff), F32),
            pltpu.VMEM(out.shape, BF), pltpu.VMEM(igrad.shape, F32),
            pltpu.SemaphoreType.DMA((8,)), pltpu.SemaphoreType.DMA((10,)),
        ],
        compiler_params=pltpu.CompilerParams(vmem_limit_bytes=60 * 2**20),
        name="finish",
    )(gfin, out, igrad)


def fast_device(inputs, positions, w_query, w_key, w_value, w_output, gain_attn, rel_table, w_in, w_out, gain_ffn, cotangent):
    shard = gain_attn.shape[0]
    buckets, heads = rel_table.shape
    padded = jnp.pad(rel_table, ((0, shard - buckets), (0, T - 2 - heads)))
    extra = jnp.concatenate([gain_attn[:, None], gain_ffn[:, None], padded], axis=1)
    out, igrad, gfin, evec, _ = layer(inputs, positions, w_query, w_key, w_value, w_output.T, w_in, w_out.T, extra, cotangent)
    g_q, g_k, g_v, g_o, g_in, g_out, out, igrad = finish(gfin, out, igrad)
    z = lax.axis_index("fsdp")
    tiles = evec.shape[1]
    gains = evec[:12].reshape(2, -1)
    g_gain = lax.dynamic_slice_in_dim(gains, z * shard, shard, 1)
    g_table = lax.dynamic_slice_in_dim(evec[12:24], z * buckets, buckets, 1).T
    return out, igrad, g_q, g_k, g_v, g_o.T, g_gain[0], g_table, g_in, g_out.T, g_gain[1]


def rms_norm(values, gain):
    return values * lax.rsqrt(jnp.mean(values * values, axis=-1, keepdims=True) + EPS) * gain


def bias_onehot(query_positions, key_places, bucket_count):
    buckets = bucket_of(key_places[:, None, :] - query_positions[:, :, None])
    labels = lax.broadcasted_iota(jnp.int32, (1, bucket_count, 1, 1), 1)
    return (buckets[:, None, :, :] == labels).astype(jnp.bfloat16)


def split_heads(rows, head_count):
    return rows.reshape(rows.shape[0], rows.shape[1], head_count, -1)


def block_scores(query_rows, key_rows, onehot, table_b):
    head_count = table_b.shape[1]
    scores = jnp.einsum(
        "sqhd,skhd->shqk",
        split_heads(query_rows, head_count),
        split_heads(key_rows, head_count),
        preferred_element_type=jnp.float32,
    )
    bias_term = jnp.einsum("sbqk,bh->shqk", onehot, table_b, preferred_element_type=jnp.float32)
    return scores + bias_term


def pair_grads(
    query_rows,
    grad_rows,
    logsum,
    row_products,
    query_positions,
    key_rows,
    value_rows,
    key_places,
    table_b,
):
    head_count = table_b.shape[1]
    onehot = bias_onehot(query_positions, key_places, table_b.shape[0])
    scores = block_scores(query_rows, key_rows, onehot, table_b)
    probs = jnp.exp(scores - logsum[..., None])
    grad_heads = split_heads(grad_rows, head_count)
    dprobs = jnp.einsum(
        "sqhd,skhd->shqk",
        grad_heads,
        split_heads(value_rows, head_count),
        preferred_element_type=jnp.float32,
    )
    grad_scores = (probs * (dprobs - row_products[..., None])).astype(jnp.bfloat16)
    grad_query = jnp.einsum(
        "shqk,skhd->sqhd",
        grad_scores,
        split_heads(key_rows, head_count),
        preferred_element_type=jnp.float32,
    )
    grad_key = jnp.einsum(
        "shqk,sqhd->skhd",
        grad_scores,
        split_heads(query_rows, head_count),
        preferred_element_type=jnp.float32,
    )
    grad_value = jnp.einsum(
        "shqk,sqhd->skhd",
        probs.astype(jnp.bfloat16),
        grad_heads,
        preferred_element_type=jnp.float32,
    )
    grad_table = jnp.einsum(
        "sbqk,shqk->bh", onehot, grad_scores, preferred_element_type=jnp.float32
    )
    return (
        grad_query.reshape(query_rows.shape),
        grad_key.reshape(key_rows.shape),
        grad_value.reshape(value_rows.shape),
        grad_table,
    )


def add_rows(whole, first_row, added_term):
    current = lax.dynamic_slice_in_dim(whole, first_row, added_term.shape[1], 1)
    return lax.dynamic_update_slice_in_dim(whole, current + added_term, first_row, 1)


def project_rows(left_operand, right_operand):
    return jnp.dot(left_operand, right_operand, preferred_element_type=jnp.float32)


def outer_sum(left_operand, right_operand):
    return jnp.einsum("nf,nd->fd", left_operand, right_operand, preferred_element_type=jnp.float32)


def general_device(
    inputs,
    positions,
    w_query,
    w_key,
    w_value,
    w_output,
    gain_attn,
    rel_table,
    w_in,
    w_out,
    gain_ffn,
    cotangent,
):
    groups, block_rows, model_width = inputs.shape
    head_count = rel_table.shape[1]
    tokens = groups * block_rows
    query_w, key_w, value_w, output_w, gain_one, table_b = (
        lax.all_gather(w_query, "fsdp", axis=0, tiled=True),
        lax.all_gather(w_key, "fsdp", axis=0, tiled=True),
        lax.all_gather(w_value, "fsdp", axis=0, tiled=True),
        lax.all_gather(w_output, "fsdp", axis=1, tiled=True),
        lax.all_gather(gain_attn, "fsdp", axis=0, tiled=True),
        lax.all_gather(rel_table, "fsdp", axis=0, tiled=True),
    )
    in_w, out_w, gain_two = (
        lax.all_gather(w_in, "fsdp", axis=0, tiled=True),
        lax.all_gather(w_out, "fsdp", axis=1, tiled=True),
        lax.all_gather(gain_ffn, "fsdp", axis=0, tiled=True),
    )
    gain_one_f = gain_one.astype(jnp.float32)
    gain_two_f = gain_two.astype(jnp.float32)
    own_first = lax.axis_index("ctx") * block_rows
    query_positions = lax.dynamic_slice_in_dim(positions, own_first, block_rows, 1)
    flat_inputs = inputs.reshape(tokens, model_width).astype(jnp.float32)
    normed = rms_norm(flat_inputs, gain_one_f).astype(jnp.bfloat16)
    queries = project_rows(normed, query_w).astype(jnp.bfloat16).reshape(groups, block_rows, -1)
    key_block = project_rows(normed, key_w).astype(jnp.bfloat16).reshape(groups, block_rows, -1)
    value_block = project_rows(normed, value_w).astype(jnp.bfloat16).reshape(groups, block_rows, -1)
    inner_width = queries.shape[2]
    head_size = inner_width // head_count
    start_state = (
        jnp.full((groups, head_count, block_rows), -1e30, jnp.float32),
        jnp.zeros((groups, head_count, block_rows), jnp.float32),
        jnp.zeros((groups, block_rows, head_count, head_size), jnp.float32),
    )
    key_piece = lax.all_gather(key_block, "ctx", axis=1, tiled=True)
    value_portion = lax.all_gather(value_block, "ctx", axis=1, tiled=True)
    piece_rows = key_piece.shape[1]
    step_rows = math.gcd(piece_rows, block_rows)

    def forward_inner_step(block_index, state):
        running, total, weighted = state
        offset = block_index * step_rows
        key_part = lax.dynamic_slice_in_dim(key_piece, offset, step_rows, 1)
        value_part = lax.dynamic_slice_in_dim(value_portion, offset, step_rows, 1)
        key_places = lax.dynamic_slice_in_dim(positions, offset, step_rows, 1)
        onehot = bias_onehot(query_positions, key_places, table_b.shape[0])
        scores = block_scores(queries, key_part, onehot, table_b)
        newest = jnp.maximum(running, jnp.max(scores, axis=-1))
        factor = jnp.exp(running - newest)
        weights = jnp.exp(scores - newest[..., None])
        total = total * factor + jnp.sum(weights, axis=-1)
        update = jnp.einsum(
            "shqk,skhd->sqhd",
            weights.astype(jnp.bfloat16),
            split_heads(value_part, head_count),
            preferred_element_type=jnp.float32,
        )
        weighted = weighted * jnp.transpose(factor, (0, 2, 1))[..., None] + update
        return (newest, total, weighted)

    running, total, weighted = lax.fori_loop(
        0, piece_rows // step_rows, forward_inner_step, start_state
    )
    logsum = running + jnp.log(total)
    mixed = weighted / jnp.transpose(total, (0, 2, 1))[..., None]
    mixed_b = mixed.reshape(tokens, inner_width).astype(jnp.bfloat16)
    middle = flat_inputs + project_rows(mixed_b, output_w)
    normed_two = rms_norm(middle, gain_two_f).astype(jnp.bfloat16)
    hidden = project_rows(normed_two, in_w)
    active = jax.nn.gelu(hidden).astype(jnp.bfloat16)
    result = middle + project_rows(active, out_w)
    output = result.astype(jnp.bfloat16).reshape(inputs.shape)
    grad_top = cotangent.reshape(tokens, model_width).astype(jnp.float32)
    grad_branch = grad_top.astype(jnp.bfloat16)
    grad_out_w = outer_sum(active, grad_branch)
    grad_active = lax.dot_general(
        grad_branch, out_w, (((1,), (1,)), ((), ())), preferred_element_type=jnp.float32
    )
    gelu_pull = jax.vjp(jax.nn.gelu, hidden)[1]
    grad_hidden = gelu_pull(grad_active)[0].astype(jnp.bfloat16)
    grad_in_w = outer_sum(normed_two, grad_hidden)
    grad_normed_two = lax.dot_general(
        grad_hidden, in_w, (((1,), (1,)), ((), ())), preferred_element_type=jnp.float32
    )
    norm_pull = jax.vjp(rms_norm, middle, gain_two_f)[1]
    grad_from_norm, grad_gain_two = norm_pull(grad_normed_two)
    grad_middle = grad_top + grad_from_norm
    ffn_parts = (
        lax.psum_scatter(
            grad_in_w.astype(jnp.bfloat16), "fsdp", scatter_dimension=0, tiled=True
        ).astype(jnp.float32),
        lax.psum_scatter(
            grad_out_w.astype(jnp.bfloat16), "fsdp", scatter_dimension=1, tiled=True
        ).astype(jnp.float32),
        lax.psum_scatter(
            grad_gain_two.astype(jnp.bfloat16), "fsdp", scatter_dimension=0, tiled=True
        ).astype(jnp.float32),
    )
    ffn_parts = (
        lax.psum(ffn_parts[0].astype(jnp.bfloat16), ("seq", "ctx")).astype(jnp.float32),
        lax.psum(ffn_parts[1].astype(jnp.bfloat16), ("seq", "ctx")).astype(jnp.float32),
        lax.psum(ffn_parts[2].astype(jnp.bfloat16), ("seq", "ctx")).astype(jnp.float32),
    )
    grad_y = grad_middle.astype(jnp.bfloat16)
    grad_output_w = outer_sum(mixed_b, grad_y)
    grad_mixed = (
        lax.dot_general(
            grad_y, output_w, (((1,), (1,)), ((), ())), preferred_element_type=jnp.float32
        )
        .astype(jnp.bfloat16)
        .reshape(groups, block_rows, inner_width)
    )
    row_products = jnp.transpose(
        jnp.sum(split_heads(grad_mixed.astype(jnp.float32), head_count) * mixed, axis=-1), (0, 2, 1)
    )
    table_zero = jnp.zeros(table_b.shape, jnp.float32)
    seq_rows = block_rows * lax.axis_size("ctx")
    whole_zero = jnp.zeros((groups, seq_rows, inner_width), jnp.float32)
    start_back = (
        jnp.zeros((groups, block_rows, inner_width), jnp.float32),
        whole_zero,
        whole_zero,
        table_zero,
    )
    keys_key_piece = lax.all_gather(key_block, "ctx", axis=1, tiled=True)
    keys_value_portion = lax.all_gather(value_block, "ctx", axis=1, tiled=True)
    piece_rows = keys_key_piece.shape[1]
    keys_step_rows = math.gcd(piece_rows, block_rows)

    def keys_inner_step(block_index, state):
        query_total, key_total, value_total, table_total = state
        offset = block_index * keys_step_rows
        key_part = lax.dynamic_slice_in_dim(keys_key_piece, offset, keys_step_rows, 1)
        value_part = lax.dynamic_slice_in_dim(keys_value_portion, offset, keys_step_rows, 1)
        key_places = lax.dynamic_slice_in_dim(positions, offset, keys_step_rows, 1)
        grad_q, grad_k, grad_v, grad_t = pair_grads(
            queries,
            grad_mixed,
            logsum,
            row_products,
            query_positions,
            key_part,
            value_part,
            key_places,
            table_b,
        )
        return (
            query_total + grad_q,
            add_rows(key_total, offset, grad_k),
            add_rows(value_total, offset, grad_v),
            table_total + grad_t,
        )

    grad_query, key_whole, value_whole, grad_table = lax.fori_loop(
        0, piece_rows // keys_step_rows, keys_inner_step, start_back
    )
    grad_key, grad_value = (
        lax.psum_scatter(
            key_whole.astype(jnp.bfloat16), "ctx", scatter_dimension=1, tiled=True
        ).astype(jnp.float32),
        lax.psum_scatter(
            value_whole.astype(jnp.bfloat16), "ctx", scatter_dimension=1, tiled=True
        ).astype(jnp.float32),
    )
    query_b = grad_query.reshape(tokens, inner_width).astype(jnp.bfloat16)
    key_b = grad_key.reshape(tokens, inner_width).astype(jnp.bfloat16)
    value_b = grad_value.reshape(tokens, inner_width).astype(jnp.bfloat16)
    grad_query_w = outer_sum(normed, query_b)
    grad_key_w = outer_sum(normed, key_b)
    grad_value_w = outer_sum(normed, value_b)
    contract = (((1,), (1,)), ((), ()))
    grad_normed = lax.dot_general(query_b, query_w, contract, preferred_element_type=jnp.float32)
    grad_normed = grad_normed + lax.dot_general(
        key_b, key_w, contract, preferred_element_type=jnp.float32
    )
    grad_normed = grad_normed + lax.dot_general(
        value_b, value_w, contract, preferred_element_type=jnp.float32
    )
    first_pull = jax.vjp(rms_norm, flat_inputs, gain_one_f)[1]
    grad_from_first, grad_gain_one = first_pull(grad_normed)
    input_grad = (grad_middle + grad_from_first).reshape(inputs.shape)
    attn_parts = (
        lax.psum_scatter(
            grad_query_w.astype(jnp.bfloat16), "fsdp", scatter_dimension=0, tiled=True
        ).astype(jnp.float32),
        lax.psum_scatter(
            grad_key_w.astype(jnp.bfloat16), "fsdp", scatter_dimension=0, tiled=True
        ).astype(jnp.float32),
        lax.psum_scatter(
            grad_value_w.astype(jnp.bfloat16), "fsdp", scatter_dimension=0, tiled=True
        ).astype(jnp.float32),
        lax.psum_scatter(
            grad_output_w.astype(jnp.bfloat16), "fsdp", scatter_dimension=1, tiled=True
        ).astype(jnp.float32),
        lax.psum_scatter(
            grad_gain_one.astype(jnp.bfloat16), "fsdp", scatter_dimension=0, tiled=True
        ).astype(jnp.float32),
        lax.psum_scatter(
            grad_table.astype(jnp.bfloat16), "fsdp", scatter_dimension=0, tiled=True
        ).astype(jnp.float32),
    )
    attn_parts = (
        lax.psum(attn_parts[0].astype(jnp.bfloat16), ("seq", "ctx")).astype(jnp.float32),
        lax.psum(attn_parts[1].astype(jnp.bfloat16), ("seq", "ctx")).astype(jnp.float32),
        lax.psum(attn_parts[2].astype(jnp.bfloat16), ("seq", "ctx")).astype(jnp.float32),
        lax.psum(attn_parts[3].astype(jnp.bfloat16), ("seq", "ctx")).astype(jnp.float32),
        lax.psum(attn_parts[4].astype(jnp.bfloat16), ("seq", "ctx")).astype(jnp.float32),
        lax.psum(attn_parts[5].astype(jnp.bfloat16), ("seq", "ctx")).astype(jnp.float32),
    )
    return (
        output,
        input_grad,
        attn_parts[0],
        attn_parts[1],
        attn_parts[2],
        attn_parts[3],
        attn_parts[4],
        attn_parts[5],
        ffn_parts[0],
        ffn_parts[1],
        ffn_parts[2],
    )


def solution(mesh):
    in_specs = (
        P(("seq", "fsdp"), "ctx", None),
        P(("seq", "fsdp"), None),
        P("fsdp", None),
        P("fsdp", None),
        P("fsdp", None),
        P(None, "fsdp"),
        P("fsdp"),
        P("fsdp", None),
        P("fsdp", None),
        P(None, "fsdp"),
        P("fsdp"),
        P(("seq", "fsdp"), "ctx", None),
    )
    out_specs = (
        P(("seq", "fsdp"), "ctx", None),
        P(("seq", "fsdp"), "ctx", None),
        P("fsdp", None),
        P("fsdp", None),
        P("fsdp", None),
        P(None, "fsdp"),
        P("fsdp"),
        P("fsdp", None),
        P("fsdp", None),
        P(None, "fsdp"),
        P("fsdp"),
    )
    fits = mesh.shape["seq"] == 2 and mesh.shape["ctx"] == 4 and mesh.shape["fsdp"] == 4
    per_device = fast_device if fits else general_device
    return jax.shard_map(
        per_device, mesh=mesh, in_specs=in_specs, out_specs=out_specs, check_vma=False
    )
```
